32 devices in a mesh: dp: 16 (over z, y, x), shard: 2 (over core).
Axes of the slice: x: 2, y: 2, z: 4, core: 2. Of those that a mesh axis runs over, the one named last changes fastest.
Arguments:
- canvases: bfloat16 [2, 128, 6, 6, 2048], P(None, ('dp', 'shard')), may hold values from -6 to 6
- crop_map: int32 [2, 128, 36], P(None, ('dp', 'shard')), may hold values from 0 to 3, as said below
- partner: int32 [2, 128, 4], P(None, ('dp', 'shard')), may hold values from 0 to 3, as said below
- queue: bfloat16 [512, 128], P(('dp', 'shard')), may hold values from -0.5 to 0.5
- w_reduce: bfloat16 [2048, 512], P(('dp', 'shard')), may hold values from -0.125 to 0.125
- w_spatial: bfloat16 [4608, 512], P(('dp', 'shard')), may hold values from -0.09375 to 0.09375
- w_expand: bfloat16 [512, 2048], P(('dp', 'shard')), may hold values from -0.25 to 0.25
- w_hidden: bfloat16 [2048, 2048], P(('dp', 'shard')), may hold values from -0.125 to 0.125
- w_project: bfloat16 [2048, 128], P(('dp', 'shard')), may hold values from -0.125 to 0.125
- norm_mid: float32 [4, 512], replicated, may hold values from -0.8 to 1.5, as said below
- norm_wide: float32 [4, 2048], replicated, may hold values from -0.8 to 1.5, as said below
- bias_out: float32 [128], replicated, may hold values from -1.5 to 1.5
- prototypes: bfloat16 [3000, 128], replicated, may hold values from -0.75 to 0.75
Outputs:
- loss: float32 [], replicated
- grad_canvases: float32 [2, 128, 6, 6, 2048], P(None, ('dp', 'shard'))
- grad_reduce: float32 [2048, 512], P(('dp', 'shard'))
- grad_spatial: float32 [4608, 512], P(('dp', 'shard'))
- grad_expand: float32 [512, 2048], P(('dp', 'shard'))
- grad_hidden: float32 [2048, 2048], P(('dp', 'shard'))
- grad_project: float32 [2048, 128], P(('dp', 'shard'))
- grad_norm_mid: float32 [4, 512], replicated
- grad_norm_wide: float32 [4, 2048], replicated
- grad_bias_out: float32 [128], replicated
- grad_prototypes: float32 [3000, 128], replicated
The draws below stay inside these ranges and needn't reach their ends.
Inputs may be any that keep to these rules, and one draw needn't show every extreme that they name: `crop_map`: every one of a canvas's 4 crops covers at least one of its pixels. A crop's partner is another crop of the same canvas, never itself. `norm_mid`: rows 0 and 2 are gains, rows 1 and 3 shifts. `norm_wide`: rows 0 and 2 are gains, rows 1 and 3 shifts.
All inputs are finite; a program needn't handle non-finite values.
Results may differ from the reference program's by a relative error of at most 0.024.
Values may be sent and summed in bfloat16 or wider, within the bound.
No kernel may reach another device: no remote copies, remote signals or barrier semaphores. Data moves between devices by JAX's collectives and lax.ppermute only.
A program may use at most 128 MiB of HBM per device.

```python
import jax
import jax.numpy as jnp
from jax import lax

D = 2048
MID = 512
PROJ = 128
PROTOS = 3000
SIDE = 6
CROPS = 4
SINK_ITERS = 3
MICRO = 2
CANVASES = 128
QUEUE = 512


def draw_crop_map(key, part):
    key = jax.random.fold_in(key, 11)
    key_base, key_rank = jax.random.split(key)
    full_shape = (MICRO, CANVASES, SIDE * SIDE)
    base_ids = jax.random.randint(key_base, full_shape, 0, CROPS)
    rank_scores = jax.random.randint(key_rank, full_shape, 0, 2 ** 20) * (SIDE * SIDE) + jnp.arange(SIDE * SIDE, dtype=jnp.int32)
    ordering = jnp.argsort(rank_scores, axis=2)
    pixel_rank = jnp.argsort(ordering, axis=2).astype(jnp.int32)
    return jnp.where(pixel_rank < CROPS, pixel_rank, base_ids).astype(jnp.int32)


def draw_partner(key, part):
    key = jax.random.fold_in(key, 12)
    offsets = jax.random.randint(key, (MICRO, CANVASES, CROPS), 1, CROPS)
    return ((jnp.arange(CROPS, dtype=jnp.int32) + offsets) % CROPS).astype(jnp.int32)


def norm_lookup_rows(key, width):
    key_gain, key_shift = jax.random.split(key)
    gains = jax.random.uniform(key_gain, (4, width), jnp.float32, 0.5, 1.5)
    shifts = jax.random.uniform(key_shift, (4, width), jnp.float32, -0.8, 0.8)
    even_rows = jnp.arange(4)[:, None] % 2 == 0
    return jnp.where(even_rows, gains, shifts).astype(jnp.float32)


def draw_norm_mid(key, part):
    key = jax.random.fold_in(key, 13)
    return norm_lookup_rows(key, MID)


def draw_norm_wide(key, part):
    key = jax.random.fold_in(key, 14)
    return norm_lookup_rows(key, D)


def levels(key, shape, cuts, smallest, high):
    factor_of = 1.0
    for position, shards_of in cuts:
        steps = jax.random.uniform(jax.random.fold_in(jax.random.fold_in(key, 6), position), (shards_of,), jnp.float32, smallest / len(cuts), high / len(cuts))
        factor_of = factor_of * jnp.repeat(jnp.exp(steps), shape[position] // shards_of).reshape((-1,) + (1,) * (len(shape) - 1 - position))
    return factor_of


def scatter_about(rng, extent, deviation, most, cuts=(), kind=jnp.bfloat16):
    values = deviation * jax.random.normal(rng, extent, jnp.float32)
    if cuts:
        values = values * levels(rng, extent, cuts, -0.22, 0.18)
    return jnp.clip(values, -most, most).astype(kind)


def setup_inputs(seed: int = 0) -> dict:
    keys = jax.random.split(jax.random.key(seed), 14)
    return {
        "canvases": scatter_about(keys[0], (MICRO, CANVASES, SIDE, SIDE, D), 1.0, 6.0, ((1, 32),)),
        "crop_map": draw_crop_map(jax.random.fold_in(keys[13], 71), 0),
        "partner": draw_partner(jax.random.fold_in(keys[13], 71), 0),
        "queue": scatter_about(keys[3], (QUEUE, PROJ), PROJ ** -0.5, 0.5, ((0, 32),)),
        "w_reduce": scatter_about(keys[4], (D, MID), D ** -0.5, 0.125, ((0, 32),)),
        "w_spatial": scatter_about(keys[5], (9 * MID, MID), (9 * MID) ** -0.5, 0.09375, ((0, 32),)),
        "w_expand": scatter_about(keys[6], (MID, D), MID ** -0.5, 0.25, ((0, 32),)),
        "w_hidden": scatter_about(keys[7], (D, D), D ** -0.5, 0.125, ((0, 32),)),
        "w_project": scatter_about(keys[8], (D, PROJ), D ** -0.5, 0.125, ((0, 32),)),
        "norm_mid": draw_norm_mid(jax.random.fold_in(keys[13], 71), 0),
        "norm_wide": draw_norm_wide(jax.random.fold_in(keys[13], 71), 0),
        "bias_out": scatter_about(keys[11], (PROJ,), 0.3, 1.5, (), jnp.float32),
        "prototypes": scatter_about(keys[12], (PROTOS, PROJ), (PROJ // 2) ** -0.5, 0.75),
    }


EPS_NORM = 1e-05
EPS_UNIT = 1e-06
SOFTMAX_HEAT = 0.1
SINK_EPS = 0.05
HIGH = lax.Precision.HIGHEST

@jax.custom_vjp
def low(v):
    return lax.optimization_barrier(v.astype(jnp.bfloat16)).astype(jnp.float32)

@jax.custom_vjp
def low_back(v):
    return v

def low_keep(v):
    return (low(v), None)

def low_pass(kept, grad):
    return (grad,)

def back_keep(v):
    return (v, None)

def back_low(kept, grad):
    return (low(grad),)
low.defvjp(low_keep, low_pass)
low_back.defvjp(back_keep, back_low)

def matmul(left, right):
    return jnp.dot(left, right, precision=HIGH, preferred_element_type=jnp.float32)

def batch_norm(hidden, gain_row, shift_row):
    average = lax.optimization_barrier(jnp.mean(hidden, 0))
    spread = lax.optimization_barrier(jnp.mean(hidden * hidden, 0)) - average * average
    return gain_row * (hidden - average) * lax.rsqrt(spread + EPS_NORM) + shift_row

def trunk(w_reduce, w_spatial, w_expand, w_hidden, w_project, norm_mid, norm_wide, bias_out, prototypes, inputs, onehot, crop_sizes):
    canvas_count = inputs.shape[0]
    input_rows = inputs.reshape(canvas_count * SIDE * SIDE, D)
    pre_one = low_back(matmul(input_rows, w_reduce))
    first_activation = low(jax.nn.silu(batch_norm(pre_one, norm_mid[0], norm_mid[1])))
    kernel = w_spatial.reshape(3, 3, MID, MID)
    pre_two = lax.conv_general_dilated(first_activation.reshape(canvas_count, SIDE, SIDE, MID), kernel, (1, 1), ((1, 1), (1, 1)), dimension_numbers=('NHWC', 'HWIO', 'NHWC'), precision=HIGH, preferred_element_type=jnp.float32)
    pre_two = low_back(pre_two.reshape(canvas_count * SIDE * SIDE, MID))
    act_two = low(jax.nn.silu(batch_norm(pre_two, norm_mid[2], norm_mid[3])))
    pre_three = low_back(matmul(act_two, w_expand))
    block_out = jax.nn.silu(batch_norm(pre_three, norm_wide[0], norm_wide[1]) + input_rows)
    pooled = jnp.einsum('cps,csd->cpd', onehot, block_out.reshape(canvas_count, SIDE * SIDE, D), precision=HIGH) / crop_sizes[:, :, None]
    pooled = low(pooled.reshape(canvas_count * CROPS, D))
    pre_head = low_back(matmul(pooled, w_hidden))
    act_head = low(jax.nn.silu(batch_norm(pre_head, norm_wide[2], norm_wide[3])))
    embed = low_back(matmul(act_head, w_project)) + bias_out
    unit_embed = low(embed * lax.rsqrt(lax.optimization_barrier(jnp.sum(embed * embed, 1, keepdims=True)) + EPS_UNIT))
    return low_back(matmul(unit_embed, prototypes.T))

def codes(prototype_scores, queue_scores):
    batch_codes = jnp.exp(prototype_scores / SINK_EPS)
    stored_codes = jnp.exp(queue_scores / SINK_EPS)
    for turn in range(SINK_ITERS):
        row_totals = lax.optimization_barrier(jnp.sum(batch_codes, 0)) + lax.optimization_barrier(jnp.sum(stored_codes, 0))
        batch_codes = batch_codes / row_totals
        stored_codes = stored_codes / row_totals
        batch_codes = batch_codes / lax.optimization_barrier(jnp.sum(batch_codes, 1, keepdims=True))
        stored_codes = stored_codes / lax.optimization_barrier(jnp.sum(stored_codes, 1, keepdims=True))
    return batch_codes

def swapped(prototype_scores, target_codes, pick):
    target = jnp.einsum('cab,cbk->cak', pick, target_codes.reshape(-1, CROPS, PROTOS), precision=HIGH).reshape(-1, PROTOS)
    log_likelihoods = jax.nn.log_softmax(prototype_scores / SOFTMAX_HEAT, axis=1)
    return -jnp.sum(target * log_likelihoods)

def reference(canvases, crop_map, partner, queue, w_reduce, w_spatial, w_expand, w_hidden, w_project, norm_mid, norm_wide, bias_out, prototypes):
    params = (w_reduce.astype(jnp.float32), w_spatial.astype(jnp.float32), w_expand.astype(jnp.float32), w_hidden.astype(jnp.float32), w_project.astype(jnp.float32), norm_mid.astype(jnp.float32), norm_wide.astype(jnp.float32), bias_out.astype(jnp.float32), prototypes.astype(jnp.float32))
    queue_scores = matmul(queue.astype(jnp.float32), params[8].T)
    crop_ids = jnp.arange(CROPS, dtype=jnp.int32)
    loss_factor_weight = 1.0 / (MICRO * CROPS * CANVASES)
    totals = tuple((jnp.zeros_like(param) for param in params))
    loss_sum = jnp.zeros((), jnp.float32)
    input_grads = []
    for micro_index in range(MICRO):
        inputs = canvases[micro_index].astype(jnp.float32)
        onehot = (crop_map[micro_index][:, None, :] == crop_ids[None, :, None]).astype(jnp.float32)
        crop_sizes = lax.optimization_barrier(jnp.sum(onehot, 2))
        pick = (partner[micro_index][:, :, None] == crop_ids[None, None, :]).astype(jnp.float32)

        def forward(*values):
            return trunk(*values, onehot, crop_sizes)
        prototype_scores, pull_trunk = jax.vjp(forward, *params, inputs)
        target_codes = codes(prototype_scores, queue_scores)

        def objective(values):
            return swapped(values, target_codes, pick)
        loss_part, pull_loss = jax.vjp(objective, prototype_scores)
        score_grad, = pull_loss(jnp.ones((), jnp.float32) * loss_factor_weight)
        grads = pull_trunk(score_grad)
        totals = tuple((former + latest for former, latest in zip(totals, grads[:-1])))
        input_grads.append(grads[-1])
        loss_sum = loss_sum + loss_part
    grad_input = jnp.stack(input_grads)
    return (loss_sum * loss_factor_weight, grad_input, totals[0], totals[1], totals[2], totals[3], totals[4], totals[5], totals[6], totals[7], totals[8])
```

```python
import jax
import jax.numpy as jnp
from jax import lax
from jax.experimental import pallas as pl
from jax.experimental.pallas import tpu as pltpu
from jax.sharding import PartitionSpec as P

D = 2048
MID = 512
PROTOS = 3000
SIDE = 6
CROPS = 4
SINK_ITERS = 3
MICRO = 2


EPS_NORM = 1e-05
EPS_UNIT = 1e-06
SOFTMAX_HEAT = 0.1
SINK_EPS = 0.05
HIGH = lax.Precision.HIGHEST
BOTH = ("dp", "shard")
GATHERED_CODES_BYTES = 32 * 2**20


def product(left, right):
    return jnp.dot(left, right, preferred_element_type=jnp.float32)


def product_t(left, right):
    return lax.dot_general(
        left, right, (((0,), (0,)), ((), ())), preferred_element_type=jnp.float32
    )


def product_bt(left, right):
    return lax.dot_general(
        left, right, (((1,), (1,)), ((), ())), preferred_element_type=jnp.float32
    )


def silu_slope(values):
    sigmoid_value = jax.nn.sigmoid(values)
    return sigmoid_value * (1.0 + values * (1.0 - sigmoid_value))


def swap_cores(values):
    return lax.ppermute(values, "shard", [(0, 1), (1, 0)])


def flip_dp(values, bits, size):
    return lax.ppermute(values, "dp", [(i, i ^ bits) for i in range(size)])


def flip_both(values, dp_bits, size):
    pairs = [(2 * i + c, 2 * (i ^ dp_bits[c]) + c) for i in range(size) for c in range(2)]
    return lax.ppermute(values, BOTH, pairs)


def sum_over_dp(values, size):
    bit = 1
    while bit < size:
        if bit * 2 < size:
            one, two, three = (flip_dp(values, bit * k, size) for k in (1, 2, 3))
            values = (values + one) + (two + three)
            bit *= 4
        else:
            values = values + flip_dp(values, bit, size)
            bit *= 2
    return values


def exchange_orders(size):
    bits = [1 << k for k in range(size.bit_length() - 1)][::-1]
    first = bits[:-2] + [bits[-1], bits[-2]] if len(bits) > 1 else bits
    return list(zip(first, bits))


def relative_slots(size):
    orders = exchange_orders(size)
    me_dp, me_core = lax.axis_index("dp"), lax.axis_index("shard")
    device = jnp.arange(2 * size, dtype=jnp.int32)
    apart_dp, apart_core = (device // 2) ^ me_dp, (device % 2) ^ me_core
    holder = device % 2
    slot = apart_core * size
    for place, (bit_zero, bit_one) in enumerate(orders):
        on = jnp.where(holder == 0, apart_dp & bit_zero, apart_dp & bit_one) != 0
        slot = slot + jnp.where(on, 1 << place, 0)
    return slot.astype(jnp.int32)


def gather_relative(shard, size):
    held = shard[None]
    for dp_bits in exchange_orders(size):
        held = jnp.concatenate([held, flip_both(held, dp_bits, size)], 0)
    return jnp.concatenate([held, swap_cores(held)], 0)


def scatter_relative(blocks, size):
    half = blocks.shape[0] // 2
    held = blocks[:half].astype(jnp.float32) + swap_cores(blocks[half:]).astype(jnp.float32)
    for dp_bits in exchange_orders(size)[::-1]:
        half = held.shape[0] // 2
        sent = held[half:].astype(jnp.bfloat16)
        held = held[:half] + flip_both(sent, dp_bits, size).astype(jnp.float32)
    return held[0]


def reorder_kernel(to_slots, table, source, target):
    def move(i, carry):
        slot = table[i]
        if to_slots:
            target[slot] = source[i].astype(target.dtype)
        else:
            target[i] = source[slot]
        return carry

    lax.fori_loop(0, source.shape[0], move, 0)


def reorder(blocks, slots, to_slots):
    return pl.pallas_call(
        lambda *refs: reorder_kernel(to_slots, *refs),
        out_shape=jax.ShapeDtypeStruct(blocks.shape, jnp.bfloat16),
        in_specs=[
            pl.BlockSpec(memory_space=pltpu.SMEM),
            pl.BlockSpec(memory_space=pltpu.VMEM),
        ],
        out_specs=pl.BlockSpec(memory_space=pltpu.VMEM),
        compiler_params=pltpu.CompilerParams(vmem_limit_bytes=32 * 2**20),
        cost_estimate=pl.CostEstimate(
            flops=0, bytes_accessed=4 * blocks.size, transcendentals=0
        ),
    )(slots, blocks)


def gather_rows(shard, slots, size):
    blocks = reorder(gather_relative(shard, size), slots, False)
    return blocks.reshape(-1, shard.shape[1])


def scatter_rows(grads, slots, size):
    blocks = grads.reshape(2 * size, -1, grads.shape[1])
    return scatter_relative(reorder(blocks, slots, True), size)


def norm_forward(hidden, gain_row, shift_row, row_total, size):
    totals = sum_over_dp(jnp.stack([jnp.sum(hidden, 0), jnp.sum(hidden * hidden, 0)]), size)
    average = totals[0] / row_total
    inverse = lax.rsqrt(totals[1] / row_total - average * average + EPS_NORM)
    normed = (hidden - average) * inverse
    return (gain_row * normed + shift_row, normed, inverse)


def norm_backward(grad_out, normed, inverse, gain_row, row_total, size, extra=None):
    totals = jnp.stack([jnp.sum(grad_out, 0), jnp.sum(grad_out * normed, 0)])
    if extra is None:
        totals = sum_over_dp(totals, size)
    else:
        width = extra.shape[0]
        extra_rows = jnp.pad(extra, (0, totals.shape[1] - width))[None]
        totals = sum_over_dp(jnp.concatenate([totals, extra_rows], 0), size)
        extra = totals[2, :width]
    grad_in = (
        gain_row * inverse * (grad_out - totals[0] / row_total - normed * (totals[1] / row_total))
    )
    return (grad_in, totals[1], totals[0], extra)


def make_patches(values):
    canvas_count, side_len = (values.shape[0], values.shape[1])
    padded = jnp.pad(values, ((0, 0), (1, 1), (1, 1), (0, 0)))
    pieces = [
        padded[:, row_shift : row_shift + side_len, col_shift : col_shift + side_len, :]
        for row_shift in range(3)
        for col_shift in range(3)
    ]
    return jnp.concatenate(pieces, 3).reshape(canvas_count * side_len * side_len, -1)


def fold_patches(grads, canvas_count, side_len, channels):
    grads = grads.reshape(canvas_count, side_len, side_len, 9, channels)
    summed = jnp.zeros((canvas_count, side_len + 2, side_len + 2, channels), jnp.float32)
    for row_shift in range(3):
        for col_shift in range(3):
            summed = summed + jnp.pad(
                grads[:, :, :, row_shift * 3 + col_shift, :],
                ((0, 0), (row_shift, 2 - row_shift), (col_shift, 2 - col_shift), (0, 0)),
            )
    return summed[:, 1 : side_len + 1, 1 : side_len + 1, :].reshape(
        canvas_count * side_len * side_len, channels
    )


def sinkhorn(batch_codes, stored_codes, total):
    for turn in range(SINK_ITERS):
        column_totals = total(jnp.sum(batch_codes, 0) + jnp.sum(stored_codes, 0))
        batch_codes = batch_codes / column_totals
        stored_codes = stored_codes / column_totals
        batch_codes = batch_codes / jnp.sum(batch_codes, 1, keepdims=True)
        stored_codes = stored_codes / jnp.sum(stored_codes, 1, keepdims=True)
    return batch_codes


def swapped_loss(scores, codes, pick, loss_factor_weight):
    rows = scores.shape[0]
    target = jnp.einsum(
        "cab,cbk->cak", pick, codes.reshape(rows // CROPS, CROPS, PROTOS), precision=HIGH
    ).reshape(rows, PROTOS)
    log_likelihoods = jax.nn.log_softmax(scores / SOFTMAX_HEAT, axis=1)
    score_grad = (jnp.exp(log_likelihoods) * jnp.sum(target, 1, keepdims=True) - target) * (
        loss_factor_weight / SOFTMAX_HEAT
    )
    return -jnp.sum(target * log_likelihoods), score_grad.astype(jnp.bfloat16)


def per_device(
    canvases,
    crop_map,
    partner,
    queue,
    w_reduce,
    w_spatial,
    w_expand,
    w_hidden,
    w_project,
    norm_mid,
    norm_wide,
    bias_out,
    prototypes,
):
    size = lax.axis_size("dp")
    me_dp, me_core = lax.axis_index("dp"), lax.axis_index("shard")
    own_canvases = canvases.shape[1]
    canvas_count = 2 * own_canvases
    pixels = SIDE * SIDE
    local_rows = canvas_count * pixels
    local_crops = canvas_count * CROPS
    pixel_total = float(local_rows * size)
    crop_count = local_crops * size
    crop_total = float(crop_count)
    loss_factor_weight = 1.0 / (MICRO * crop_total)
    crop_ids = jnp.arange(CROPS, dtype=jnp.int32)
    slots = relative_slots(size)

    def both_cores(values):
        mine = lax.dynamic_index_in_dim(values, me_core, 0, keepdims=False)
        other = lax.dynamic_index_in_dim(values, 1 - me_core, 0, keepdims=False)
        return jnp.concatenate([mine, swap_cores(other)], 0)

    full_reduce = gather_rows(w_reduce, slots, size)
    full_spatial = gather_rows(w_spatial, slots, size)
    full_expand = gather_rows(w_expand, slots, size)
    full_head = lax.all_gather(
        jnp.concatenate([w_hidden, w_project], 1), BOTH, axis=0, tiled=True
    )
    full_hidden, full_project = full_head[:, :D], full_head[:, D:]

    input_rows = both_cores(canvases).reshape(local_rows, D)
    labels = both_cores(jnp.concatenate([crop_map, partner], 2))
    crop_map, partner = labels[:, :pixels], labels[:, pixels:]
    onehot = (crop_map[:, None, :] == crop_ids[None, :, None]).astype(jnp.float32)
    crop_sizes = jnp.sum(onehot, 2)

    gathered_codes = crop_count * PROTOS * 4 <= GATHERED_CODES_BYTES
    if gathered_codes:
        all_queue = lax.all_gather(queue, BOTH, axis=0, tiled=True)
        all_partner = lax.all_gather(partner, "dp", axis=0, tiled=True)
    else:
        all_queue = jnp.concatenate([queue, swap_cores(queue)], 0)
        all_partner = partner
    queue_codes = jnp.exp(product_bt(all_queue, prototypes) / SINK_EPS)
    pick = (all_partner[:, :, None] == crop_ids[None, None, :]).astype(jnp.float32)

    pre_one = product(input_rows, full_reduce)
    norm_one, unit_one, inv_one = norm_forward(
        pre_one, norm_mid[0], norm_mid[1], pixel_total, size
    )
    first_activation = jax.nn.silu(norm_one).astype(jnp.bfloat16)
    image_patches = make_patches(first_activation.reshape(canvas_count, SIDE, SIDE, MID))
    pre_two = product(image_patches, full_spatial)
    norm_two, unit_two, inv_two = norm_forward(
        pre_two, norm_mid[2], norm_mid[3], pixel_total, size
    )
    act_two = jax.nn.silu(norm_two).astype(jnp.bfloat16)
    pre_three = product(act_two, full_expand)
    norm_three, unit_three, inv_three = norm_forward(
        pre_three, norm_wide[0], norm_wide[1], pixel_total, size
    )
    joined = norm_three + input_rows.astype(jnp.float32)
    block_out = jax.nn.silu(joined)
    pooled = (
        jnp.einsum(
            "cps,csd->cpd", onehot, block_out.reshape(canvas_count, pixels, D), precision=HIGH
        )
        / crop_sizes[:, :, None]
    )
    pooled_low = pooled.reshape(local_crops, D).astype(jnp.bfloat16)
    pre_head = product(pooled_low, full_hidden)
    norm_head, unit_head, inv_head = norm_forward(
        pre_head, norm_wide[2], norm_wide[3], crop_total, size
    )
    act_head = jax.nn.silu(norm_head).astype(jnp.bfloat16)
    embed = product(act_head, full_project) + bias_out
    inv_length = lax.rsqrt(jnp.sum(embed * embed, 1, keepdims=True) + EPS_UNIT)
    unit_embed = embed * inv_length
    unit_low = unit_embed.astype(jnp.bfloat16)

    if gathered_codes:
        spread = jnp.broadcast_to(unit_low[None], (size,) + unit_low.shape)
        all_units = lax.all_to_all(spread, "dp", 0, 0).reshape(crop_count, -1)
        scores = product_bt(all_units, prototypes)
        codes = sinkhorn(jnp.exp(scores / SINK_EPS), queue_codes, lambda sums: sums)
        loss_part, score_low = swapped_loss(scores, codes, pick, loss_factor_weight)
        proto_part = product_t(score_low, all_units)
        score_low = lax.dynamic_slice_in_dim(score_low, me_dp * local_crops, local_crops, 0)
    else:
        scores = product_bt(unit_low, prototypes)
        codes = sinkhorn(
            jnp.exp(scores / SINK_EPS), queue_codes, lambda sums: sum_over_dp(sums, size)
        )
        loss_part, score_low = swapped_loss(scores, codes, pick, loss_factor_weight)
        proto_part, loss_part = lax.psum((product_t(score_low, unit_low), loss_part), "dp")
    proto_grad = proto_part + swap_cores(proto_part)
    unit_grad = product(score_low, prototypes)
    embed_grad = inv_length * (
        unit_grad - unit_embed * jnp.sum(unit_grad * unit_embed, 1, keepdims=True)
    )
    embed_low = embed_grad.astype(jnp.bfloat16)

    head_act_grad = product_bt(embed_low, full_project) * silu_slope(norm_head)
    head_grad, gain_head, shift_head, bias_part = norm_backward(
        head_act_grad,
        unit_head,
        inv_head,
        norm_wide[2],
        crop_total,
        size,
        jnp.sum(embed_grad, 0),
    )
    head_low = head_grad.astype(jnp.bfloat16)
    left = lax.all_gather(
        jnp.concatenate([pooled_low, act_head], 1), "dp", axis=0, tiled=True
    )
    right = lax.all_gather(jnp.concatenate([head_low, embed_low], 1), "dp", axis=0, tiled=True)
    chip_rows = 2 * w_hidden.shape[0]
    first_row = me_dp * chip_rows
    hidden_part = product_t(
        lax.dynamic_slice_in_dim(left[:, :D], first_row, chip_rows, 1), right[:, :D]
    )
    project_part = product_t(
        lax.dynamic_slice_in_dim(left[:, D:], first_row, chip_rows, 1), right[:, D:]
    )

    def own_rows(part):
        half = chip_rows // 2
        mine = lax.dynamic_slice_in_dim(part, me_core * half, half, 0)
        other = lax.dynamic_slice_in_dim(part, (1 - me_core) * half, half, 0)
        return mine + swap_cores(other)

    grad_hidden, grad_project = own_rows(hidden_part), own_rows(project_part)

    pooled_grad = (
        product_bt(head_low, full_hidden).reshape(canvas_count, CROPS, D)
        / crop_sizes[:, :, None]
    )
    out_grad = jnp.einsum("cps,cpd->csd", onehot, pooled_grad, precision=HIGH).reshape(
        local_rows, D
    )
    joined_grad = out_grad * silu_slope(joined)
    three_grad, gain_three, shift_three, _ = norm_backward(
        joined_grad, unit_three, inv_three, norm_wide[0], pixel_total, size
    )
    three_low = three_grad.astype(jnp.bfloat16)
    grad_expand = scatter_rows(product_t(act_two, three_low), slots, size)
    two_act_grad = product_bt(three_low, full_expand) * silu_slope(norm_two)
    two_grad, gain_two, shift_two, _ = norm_backward(
        two_act_grad, unit_two, inv_two, norm_mid[2], pixel_total, size
    )
    two_low = two_grad.astype(jnp.bfloat16)
    grad_spatial = scatter_rows(product_t(image_patches, two_low), slots, size)
    patch_grad = product_bt(two_low, full_spatial)
    one_act_grad = fold_patches(patch_grad, canvas_count, SIDE, MID) * silu_slope(norm_one)
    one_grad, gain_one, shift_one, _ = norm_backward(
        one_act_grad, unit_one, inv_one, norm_mid[0], pixel_total, size
    )
    one_low = one_grad.astype(jnp.bfloat16)
    grad_reduce = scatter_rows(product_t(input_rows, one_low), slots, size)
    input_grad = (joined_grad + product_bt(one_low, full_reduce)).reshape(
        2, own_canvases, SIDE, SIDE, D
    )
    other_micro = swap_cores(input_grad[1])
    on_first = me_core == 0
    grad_canvases = jnp.stack(
        [
            jnp.where(on_first, input_grad[0], other_micro),
            jnp.where(on_first, other_micro, input_grad[0]),
        ]
    )
    narrow = jnp.concatenate(
        [
            jnp.stack([gain_one, shift_one, gain_two, shift_two]).reshape(-1),
            jnp.stack([gain_three, shift_three, gain_head, shift_head]).reshape(-1),
            bias_part,
            jnp.broadcast_to(loss_part, (128,)),
        ]
    )
    narrow = narrow + swap_cores(narrow)
    mid_end, wide_end = norm_mid.size, norm_mid.size + norm_wide.size
    bias_end = wide_end + bias_out.shape[0]
    return (
        narrow[bias_end] * loss_factor_weight,
        grad_canvases,
        grad_reduce,
        grad_spatial,
        grad_expand,
        grad_hidden,
        grad_project,
        narrow[:mid_end].reshape(norm_mid.shape),
        narrow[mid_end:wide_end].reshape(norm_wide.shape),
        narrow[wide_end:bias_end],
        proto_grad,
    )


def solution(mesh):
    return jax.shard_map(
        per_device,
        mesh=mesh,
        in_specs=(
            P(None, ("dp", "shard"), None, None, None),
            P(None, ("dp", "shard"), None),
            P(None, ("dp", "shard"), None),
            P(("dp", "shard"), None),
            P(("dp", "shard"), None),
            P(("dp", "shard"), None),
            P(("dp", "shard"), None),
            P(("dp", "shard"), None),
            P(("dp", "shard"), None),
            P(),
            P(),
            P(),
            P(),
        ),
        out_specs=(
            P(),
            P(None, ("dp", "shard"), None, None, None),
            P(("dp", "shard"), None),
            P(("dp", "shard"), None),
            P(("dp", "shard"), None),
            P(("dp", "shard"), None),
            P(("dp", "shard"), None),
            P(),
            P(),
            P(),
            P(),
        ),
        check_vma=False,
    )
```

```python
import jax
import jax.numpy as jnp
from jax import lax
from jax.experimental import pallas as pl
from jax.experimental.pallas import tpu as pltpu
from jax.sharding import PartitionSpec as P

D = 2048
MID = 512
PROTOS = 3000
SIDE = 6
CROPS = 4
SINK_ITERS = 3
MICRO = 2


EPS_NORM = 1e-05
EPS_UNIT = 1e-06
SOFTMAX_HEAT = 0.1
SINK_EPS = 0.05
HIGH = lax.Precision.HIGHEST
BOTH = ("dp", "shard")
GATHERED_CODES_BYTES = 32 * 2**20
MIB = 2**20
LANES = 512


def product(left, right):
    return jnp.dot(left, right, preferred_element_type=jnp.float32)


def product_t(left, right):
    return lax.dot_general(
        left, right, (((0,), (0,)), ((), ())), preferred_element_type=jnp.float32
    )


def product_bt(left, right):
    return lax.dot_general(
        left, right, (((1,), (1,)), ((), ())), preferred_element_type=jnp.float32
    )


def silu_slope(values):
    sigmoid_value = jax.nn.sigmoid(values)
    return sigmoid_value * (1.0 + values * (1.0 - sigmoid_value))


def swap_cores(values):
    return lax.ppermute(values, "shard", [(0, 1), (1, 0)])


def flip_dp(values, bits, size):
    return lax.ppermute(values, "dp", [(i, i ^ bits) for i in range(size)])


def flip_both(values, dp_bits, size):
    pairs = [(2 * i + c, 2 * (i ^ dp_bits[c]) + c) for i in range(size) for c in range(2)]
    return lax.ppermute(values, BOTH, pairs)


def sum_over_dp(values, size):
    bit = 1
    while bit < size:
        if bit * 2 < size:
            one, two, three = (flip_dp(values, bit * k, size) for k in (1, 2, 3))
            values = (values + one) + (two + three)
            bit *= 4
        else:
            values = values + flip_dp(values, bit, size)
            bit *= 2
    return values


def exchange_orders(size):
    bits = [1 << k for k in range(size.bit_length() - 1)][::-1]
    first = bits[:-2] + [bits[-1], bits[-2]] if len(bits) > 1 else bits
    return list(zip(first, bits))


def relative_slots(size):
    orders = exchange_orders(size)
    me_dp, me_core = lax.axis_index("dp"), lax.axis_index("shard")
    device = jnp.arange(2 * size, dtype=jnp.int32)
    apart_dp, apart_core = (device // 2) ^ me_dp, (device % 2) ^ me_core
    holder = device % 2
    slot = apart_core * size
    for place, (bit_zero, bit_one) in enumerate(orders):
        on = jnp.where(holder == 0, apart_dp & bit_zero, apart_dp & bit_one) != 0
        slot = slot + jnp.where(on, 1 << place, 0)
    return slot.astype(jnp.int32)


def gather_relative(shard, size):
    held = shard[None]
    for dp_bits in exchange_orders(size):
        held = jnp.concatenate([held, flip_both(held, dp_bits, size)], 0)
    return jnp.concatenate([held, swap_cores(held)], 0)


def scatter_relative(blocks, size):
    half = blocks.shape[0] // 2
    held = blocks[:half].astype(jnp.float32) + swap_cores(blocks[half:]).astype(jnp.float32)
    for dp_bits in exchange_orders(size)[::-1]:
        half = held.shape[0] // 2
        sent = held[half:].astype(jnp.bfloat16)
        held = held[:half] + flip_both(sent, dp_bits, size).astype(jnp.float32)
    return held[0]


def reorder_kernel(to_slots, table, source, target):
    def move(i, carry):
        slot = table[i]
        if to_slots:
            target[slot] = source[i].astype(target.dtype)
        else:
            target[i] = source[slot]
        return carry

    lax.fori_loop(0, source.shape[0], move, 0)


def reorder(blocks, slots, to_slots):
    return pl.pallas_call(
        lambda *refs: reorder_kernel(to_slots, *refs),
        out_shape=jax.ShapeDtypeStruct(blocks.shape, jnp.bfloat16),
        in_specs=[
            pl.BlockSpec(memory_space=pltpu.SMEM),
            pl.BlockSpec(memory_space=pltpu.VMEM),
        ],
        out_specs=pl.BlockSpec(memory_space=pltpu.VMEM),
        compiler_params=pltpu.CompilerParams(vmem_limit_bytes=32 * 2**20),
        cost_estimate=pl.CostEstimate(
            flops=0, bytes_accessed=4 * blocks.size, transcendentals=0
        ),
    )(slots, blocks)


def gather_rows(shard, slots, size):
    blocks = reorder(gather_relative(shard, size), slots, False)
    return blocks.reshape(-1, shard.shape[1])


def scatter_rows(grads, slots, size):
    blocks = grads.reshape(2 * size, -1, grads.shape[1])
    return scatter_relative(reorder(blocks, slots, True), size)


def spread_dp(values, size):
    return lax.all_to_all(jnp.broadcast_to(values[None], (size,) + values.shape), "dp", 0, 0)


def norm_forward(hidden, gain_row, shift_row, row_total, size):
    totals = sum_over_dp(jnp.stack([jnp.sum(hidden, 0), jnp.sum(hidden * hidden, 0)]), size)
    average = totals[0] / row_total
    inverse = lax.rsqrt(totals[1] / row_total - average * average + EPS_NORM)
    normed = (hidden - average) * inverse
    return (gain_row * normed + shift_row, normed, inverse)


def norm_backward(grad_out, normed, inverse, gain_row, row_total, size, extra=None):
    totals = jnp.stack([jnp.sum(grad_out, 0), jnp.sum(grad_out * normed, 0)])
    if extra is None:
        totals = sum_over_dp(totals, size)
    else:
        width = extra.shape[0]
        extra_rows = jnp.pad(extra, (0, totals.shape[1] - width))[None]
        totals = sum_over_dp(jnp.concatenate([totals, extra_rows], 0), size)
        extra = totals[2, :width]
    grad_in = (
        gain_row * inverse * (grad_out - totals[0] / row_total - normed * (totals[1] / row_total))
    )
    return (grad_in, totals[1], totals[0], extra)


def make_patches(values):
    canvas_count, side_len = (values.shape[0], values.shape[1])
    padded = jnp.pad(values, ((0, 0), (1, 1), (1, 1), (0, 0)))
    pieces = [
        padded[:, row_shift : row_shift + side_len, col_shift : col_shift + side_len, :]
        for row_shift in range(3)
        for col_shift in range(3)
    ]
    return jnp.concatenate(pieces, 3).reshape(canvas_count * side_len * side_len, -1)


def fold_patches(grads, canvas_count, side_len, channels):
    grads = grads.reshape(canvas_count, side_len, side_len, 9, channels)
    summed = jnp.zeros((canvas_count, side_len + 2, side_len + 2, channels), jnp.float32)
    for row_shift in range(3):
        for col_shift in range(3):
            summed = summed + jnp.pad(
                grads[:, :, :, row_shift * 3 + col_shift, :],
                ((0, 0), (row_shift, 2 - row_shift), (col_shift, 2 - col_shift), (0, 0)),
            )
    return summed[:, 1 : side_len + 1, 1 : side_len + 1, :].reshape(
        canvas_count * side_len * side_len, channels
    )


def kernel_call(body, outs, args, smem=0, scratch=(), flops=0, transcendentals=0, limit=32):
    size_of = lambda a: a.size * a.dtype.itemsize
    result = pl.pallas_call(
        body,
        out_shape=[jax.ShapeDtypeStruct(shape, dtype) for shape, dtype in outs],
        in_specs=[
            pl.BlockSpec(memory_space=pltpu.SMEM if i < smem else pltpu.VMEM)
            for i in range(len(args))
        ],
        out_specs=[pl.BlockSpec(memory_space=pltpu.VMEM) for _ in outs],
        scratch_shapes=list(scratch),
        compiler_params=pltpu.CompilerParams(vmem_limit_bytes=limit * MIB),
        cost_estimate=pl.CostEstimate(
            flops=int(flops),
            bytes_accessed=int(sum(size_of(a) for a in args)),
            transcendentals=int(transcendentals),
        ),
    )(*args)
    return result


def add_columns(total_ref, columns, values):
    rows, width = values.shape
    total_ref[:, columns] += jnp.sum(values.reshape(rows // 8, 8, width), 0)


def codes_kernel(
    crops,
    first_row,
    units_ref,
    partner_ref,
    proto_ref,
    loss_ref,
    proto_grad_ref,
    unit_grad_ref,
    codes_ref,
    heat_ref,
    score_ref,
    total_ref,
    scale_ref,
    inverse_ref,
    *,
    factor,
):
    rows_all, width = codes_ref.shape
    own = unit_grad_ref.shape[0]
    chunks = [slice(k, k + LANES) for k in range(0, width, LANES)]
    lane = lax.broadcasted_iota(jnp.int32, (1, width), 1)
    real = lane < PROTOS

    def scores(rows, columns):
        return lax.dot_general(
            units_ref[rows, :],
            proto_ref[columns, :],
            (((1,), (1,)), ((), ())),
            preferred_element_type=jnp.float32,
        )

    def keep(values, columns):
        if columns.stop <= PROTOS:
            return values
        lanes = columns.start + lax.broadcasted_iota(jnp.int32, values.shape, 1)
        return jnp.where(lanes < PROTOS, values, 0.0)

    def fold(values):
        return sum(values[:, k : k + 128] for k in range(0, values.shape[1], 128))

    total_ref[...] = jnp.zeros_like(total_ref)

    def first(i, carry):
        rows = pl.ds(pl.multiple_of(i * 128, 128), 128)
        for columns in chunks:
            powers = keep(jnp.exp(scores(rows, columns) * (1.0 / SINK_EPS)), columns)
            codes_ref[rows, columns] = powers
            add_columns(total_ref, columns, powers)
        return carry

    lax.fori_loop(0, rows_all // 128, first, 0)

    def column_factors(turn):
        total = jnp.sum(total_ref[...], 0, keepdims=True)
        total = jnp.where(real, total, 1.0)
        if turn == 0:
            scale = jnp.where(total > 1e30, 2.0**-64, 1.0)
            scale_ref[...] = jnp.broadcast_to(scale, scale_ref.shape)
            total = total * scale
        inverse_ref[...] = jnp.broadcast_to(1.0 / total, inverse_ref.shape)

    def divided(turn, rows, columns):
        values = codes_ref[rows, columns]
        if turn == 0:
            values = values * scale_ref[0:1, columns]
        return values * inverse_ref[0:1, columns]

    def row_inverse(turn, rows):
        part = sum(fold(divided(turn, rows, columns)) for columns in chunks)
        return 1.0 / jnp.sum(part, 1, keepdims=True)

    for turn in range(SINK_ITERS - 1):
        column_factors(turn)
        total_ref[...] = jnp.zeros_like(total_ref)

        def both(i, carry):
            rows = pl.ds(pl.multiple_of(i * 64, 64), 64)
            inverse = row_inverse(turn, rows)
            for columns in chunks:
                values = divided(turn, rows, columns) * inverse
                codes_ref[rows, columns] = values
                add_columns(total_ref, columns, values)
            return carry

        lax.fori_loop(0, rows_all // 64, both, 0)

    column_factors(SINK_ITERS - 1)
    proto_grad_ref[...] = jnp.zeros_like(proto_grad_ref)
    loss_ref[...] = jnp.zeros_like(loss_ref)
    block = 128

    def last(i, carry):
        rows = pl.ds(pl.multiple_of(i * block, block), block)
        inverse = row_inverse(SINK_ITERS - 1, rows)
        row = lax.broadcasted_iota(jnp.int32, (block, block), 0)
        column = lax.broadcasted_iota(jnp.int32, (block, block), 1)
        pick = (column == (row // CROPS) * CROPS + partner_ref[rows, :]).astype(jnp.bfloat16)
        heat_part = jnp.zeros((block, 128), jnp.float32)
        target_part = jnp.zeros((block, 128), jnp.float32)
        loss_part = jnp.zeros((block, 128), jnp.float32)
        for columns in chunks:
            score = scores(rows, columns)
            heat = keep(jnp.exp(score * (1.0 / SOFTMAX_HEAT)), columns)
            heat_ref[:, columns] = heat
            heat_part += fold(heat)
            codes = divided(SINK_ITERS - 1, rows, columns) * inverse
            high = codes.astype(jnp.bfloat16)
            rest = (codes - high.astype(jnp.float32)).astype(jnp.bfloat16)
            target = product(pick, high) + product(pick, rest)
            codes_ref[rows, columns] = target
            target_part += fold(target)
            loss_part += fold(target * score)
        heat_sum = jnp.sum(heat_part, 1, keepdims=True)
        target_sum = jnp.sum(target_part, 1, keepdims=True)
        row_loss = (
            target_sum * jnp.log(heat_sum)
            - jnp.sum(loss_part, 1, keepdims=True) * (1.0 / SOFTMAX_HEAT)
        )
        loss_ref[...] += jnp.broadcast_to(jnp.sum(row_loss, 0, keepdims=True), loss_ref.shape)
        ratio = target_sum / heat_sum * factor
        for columns in chunks:
            grad = heat_ref[:, columns] * ratio - codes_ref[rows, columns] * factor
            low = grad.astype(jnp.bfloat16)
            score_ref[rows, columns] = low
            proto_grad_ref[:, columns] += product_t(units_ref[rows, :], low)
        return carry

    lax.fori_loop(0, crops // block, last, 0)
    mine = pl.ds(pl.multiple_of(first_row[0], own), own)
    unit_grad_ref[...] = product(score_ref[mine, :], proto_ref[...])


def gathered_loss(units, queue, partner, prototypes, first_row, own, loss_factor_weight):
    crops, dim = units.shape
    width = -(-PROTOS // LANES) * LANES
    rows_all = crops + queue.shape[0]
    padded = jnp.pad(prototypes, ((0, width - PROTOS), (0, 0)))
    f32, bf16 = jnp.float32, jnp.bfloat16
    loss, proto_grad, unit_grad = kernel_call(
        lambda *refs: codes_kernel(crops, *refs, factor=loss_factor_weight / SOFTMAX_HEAT),
        [((8, 128), f32), ((dim, width), f32), ((own, dim), f32)],
        [first_row, jnp.concatenate([units, queue], 0), partner, padded],
        smem=1,
        scratch=[
            pltpu.VMEM((rows_all, width), f32),
            pltpu.VMEM((128, width), f32),
            pltpu.VMEM((crops, width), bf16),
            pltpu.VMEM((8, width), f32),
            pltpu.VMEM((8, width), f32),
            pltpu.VMEM((8, width), f32),
        ],
        flops=2 * width * (rows_all * dim + 6 * crops * dim),
        transcendentals=width * (rows_all + crops),
        limit=40,
    )
    return loss[0, 0], proto_grad.T[:PROTOS], unit_grad


def sinkhorn(batch_codes, stored_codes, total):
    for turn in range(SINK_ITERS):
        column_totals = total(jnp.sum(batch_codes, 0) + jnp.sum(stored_codes, 0))
        batch_codes = batch_codes / column_totals
        stored_codes = stored_codes / column_totals
        batch_codes = batch_codes / jnp.sum(batch_codes, 1, keepdims=True)
        stored_codes = stored_codes / jnp.sum(stored_codes, 1, keepdims=True)
    return batch_codes


def swapped_loss(scores, codes, pick, loss_factor_weight):
    rows = scores.shape[0]
    target = jnp.einsum(
        "cab,cbk->cak", pick, codes.reshape(rows // CROPS, CROPS, PROTOS), precision=HIGH
    ).reshape(rows, PROTOS)
    log_likelihoods = jax.nn.log_softmax(scores / SOFTMAX_HEAT, axis=1)
    score_grad = (jnp.exp(log_likelihoods) * jnp.sum(target, 1, keepdims=True) - target) * (
        loss_factor_weight / SOFTMAX_HEAT
    )
    return -jnp.sum(target * log_likelihoods), score_grad.astype(jnp.bfloat16)


def per_device(
    canvases,
    crop_map,
    partner,
    queue,
    w_reduce,
    w_spatial,
    w_expand,
    w_hidden,
    w_project,
    norm_mid,
    norm_wide,
    bias_out,
    prototypes,
):
    size = lax.axis_size("dp")
    me_dp, me_core = lax.axis_index("dp"), lax.axis_index("shard")
    own_canvases = canvases.shape[1]
    canvas_count = 2 * own_canvases
    pixels = SIDE * SIDE
    local_rows = canvas_count * pixels
    local_crops = canvas_count * CROPS
    pixel_total = float(local_rows * size)
    crop_count = local_crops * size
    crop_total = float(crop_count)
    loss_factor_weight = 1.0 / (MICRO * crop_total)
    crop_ids = jnp.arange(CROPS, dtype=jnp.int32)
    slots = relative_slots(size)

    def both_cores(values):
        mine = lax.dynamic_index_in_dim(values, me_core, 0, keepdims=False)
        other = lax.dynamic_index_in_dim(values, 1 - me_core, 0, keepdims=False)
        return jnp.concatenate([mine, swap_cores(other)], 0)

    full_reduce = gather_rows(w_reduce, slots, size)
    full_spatial = gather_rows(w_spatial, slots, size)
    full_expand = gather_rows(w_expand, slots, size)
    full_head = lax.all_gather(
        jnp.concatenate([w_hidden, w_project], 1), BOTH, axis=0, tiled=True
    )
    full_hidden, full_project = full_head[:, :D], full_head[:, D:]

    input_rows = both_cores(canvases).reshape(local_rows, D)
    labels = both_cores(jnp.concatenate([crop_map, partner], 2))
    crop_map, partner = labels[:, :pixels], labels[:, pixels:]
    onehot = (crop_map[:, None, :] == crop_ids[None, :, None]).astype(jnp.float32)
    crop_sizes = jnp.sum(onehot, 2)

    gathered_codes = crop_count * PROTOS * 4 <= GATHERED_CODES_BYTES
    chip_queue = jnp.concatenate([queue, swap_cores(queue)], 0)
    if gathered_codes:
        width = queue.shape[1]
        partner_rows = -(-local_crops // width)
        packed = jnp.pad(
            partner.astype(jnp.bfloat16).reshape(-1), (0, partner_rows * width - local_crops)
        ).reshape(partner_rows, width)
        packed = spread_dp(jnp.concatenate([chip_queue, packed], 0), size)
        all_queue = packed[:, : chip_queue.shape[0]].reshape(-1, width)
        all_partner = packed[:, chip_queue.shape[0] :].reshape(size, -1)[:, :local_crops]
        all_partner = all_partner.astype(jnp.int32).reshape(crop_count, 1)

    pre_one = product(input_rows, full_reduce)
    norm_one, unit_one, inv_one = norm_forward(
        pre_one, norm_mid[0], norm_mid[1], pixel_total, size
    )
    first_activation = jax.nn.silu(norm_one).astype(jnp.bfloat16)
    image_patches = make_patches(first_activation.reshape(canvas_count, SIDE, SIDE, MID))
    pre_two = product(image_patches, full_spatial)
    norm_two, unit_two, inv_two = norm_forward(
        pre_two, norm_mid[2], norm_mid[3], pixel_total, size
    )
    act_two = jax.nn.silu(norm_two).astype(jnp.bfloat16)
    pre_three = product(act_two, full_expand)
    norm_three, unit_three, inv_three = norm_forward(
        pre_three, norm_wide[0], norm_wide[1], pixel_total, size
    )
    joined = norm_three + input_rows.astype(jnp.float32)
    block_out = jax.nn.silu(joined)
    pooled = (
        jnp.einsum(
            "cps,csd->cpd", onehot, block_out.reshape(canvas_count, pixels, D), precision=HIGH
        )
        / crop_sizes[:, :, None]
    )
    pooled_low = pooled.reshape(local_crops, D).astype(jnp.bfloat16)
    pre_head = product(pooled_low, full_hidden)
    norm_head, unit_head, inv_head = norm_forward(
        pre_head, norm_wide[2], norm_wide[3], crop_total, size
    )
    act_head = jax.nn.silu(norm_head).astype(jnp.bfloat16)
    embed = product(act_head, full_project) + bias_out
    inv_length = lax.rsqrt(jnp.sum(embed * embed, 1, keepdims=True) + EPS_UNIT)
    unit_embed = embed * inv_length
    unit_low = unit_embed.astype(jnp.bfloat16)

    if gathered_codes:
        all_units = spread_dp(unit_low, size).reshape(crop_count, -1)
        loss_part, proto_part, unit_grad = gathered_loss(
            all_units,
            all_queue,
            all_partner,
            prototypes,
            (me_dp * local_crops).astype(jnp.int32).reshape(1),
            local_crops,
            loss_factor_weight,
        )
    else:
        queue_codes = jnp.exp(product_bt(chip_queue, prototypes) / SINK_EPS)
        pick = (partner[:, :, None] == crop_ids[None, None, :]).astype(jnp.float32)
        scores = product_bt(unit_low, prototypes)
        codes = sinkhorn(
            jnp.exp(scores / SINK_EPS), queue_codes, lambda sums: sum_over_dp(sums, size)
        )
        loss_part, score_low = swapped_loss(scores, codes, pick, loss_factor_weight)
        proto_part, loss_part = lax.psum((product_t(score_low, unit_low), loss_part), "dp")
        unit_grad = product(score_low, prototypes)
    proto_grad = proto_part + swap_cores(proto_part)
    embed_grad = inv_length * (
        unit_grad - unit_embed * jnp.sum(unit_grad * unit_embed, 1, keepdims=True)
    )
    embed_low = embed_grad.astype(jnp.bfloat16)

    head_act_grad = product_bt(embed_low, full_project) * silu_slope(norm_head)
    head_grad, gain_head, shift_head, bias_part = norm_backward(
        head_act_grad,
        unit_head,
        inv_head,
        norm_wide[2],
        crop_total,
        size,
        jnp.sum(embed_grad, 0),
    )
    head_low = head_grad.astype(jnp.bfloat16)
    left = lax.all_gather(
        jnp.concatenate([pooled_low, act_head], 1), "dp", axis=0, tiled=True
    )
    right = lax.all_gather(jnp.concatenate([head_low, embed_low], 1), "dp", axis=0, tiled=True)
    chip_rows = 2 * w_hidden.shape[0]
    first_row = me_dp * chip_rows
    hidden_part = product_t(
        lax.dynamic_slice_in_dim(left[:, :D], first_row, chip_rows, 1), right[:, :D]
    )
    project_part = product_t(
        lax.dynamic_slice_in_dim(left[:, D:], first_row, chip_rows, 1), right[:, D:]
    )

    def own_rows(part):
        half = chip_rows // 2
        mine = lax.dynamic_slice_in_dim(part, me_core * half, half, 0)
        other = lax.dynamic_slice_in_dim(part, (1 - me_core) * half, half, 0)
        return mine + swap_cores(other)

    grad_hidden, grad_project = own_rows(hidden_part), own_rows(project_part)

    pooled_grad = (
        product_bt(head_low, full_hidden).reshape(canvas_count, CROPS, D)
        / crop_sizes[:, :, None]
    )
    out_grad = jnp.einsum("cps,cpd->csd", onehot, pooled_grad, precision=HIGH).reshape(
        local_rows, D
    )
    joined_grad = out_grad * silu_slope(joined)
    three_grad, gain_three, shift_three, _ = norm_backward(
        joined_grad, unit_three, inv_three, norm_wide[0], pixel_total, size
    )
    three_low = three_grad.astype(jnp.bfloat16)
    grad_expand = scatter_rows(product_t(act_two, three_low), slots, size)
    two_act_grad = product_bt(three_low, full_expand) * silu_slope(norm_two)
    two_grad, gain_two, shift_two, _ = norm_backward(
        two_act_grad, unit_two, inv_two, norm_mid[2], pixel_total, size
    )
    two_low = two_grad.astype(jnp.bfloat16)
    grad_spatial = scatter_rows(product_t(image_patches, two_low), slots, size)
    patch_grad = product_bt(two_low, full_spatial)
    one_act_grad = fold_patches(patch_grad, canvas_count, SIDE, MID) * silu_slope(norm_one)
    one_grad, gain_one, shift_one, _ = norm_backward(
        one_act_grad, unit_one, inv_one, norm_mid[0], pixel_total, size
    )
    one_low = one_grad.astype(jnp.bfloat16)
    grad_reduce = scatter_rows(product_t(input_rows, one_low), slots, size)
    input_grad = (joined_grad + product_bt(one_low, full_reduce)).reshape(
        2, own_canvases, SIDE, SIDE, D
    )
    other_micro = swap_cores(input_grad[1])
    on_first = me_core == 0
    grad_canvases = jnp.stack(
        [
            jnp.where(on_first, input_grad[0], other_micro),
            jnp.where(on_first, other_micro, input_grad[0]),
        ]
    )
    narrow = jnp.concatenate(
        [
            jnp.stack([gain_one, shift_one, gain_two, shift_two]).reshape(-1),
            jnp.stack([gain_three, shift_three, gain_head, shift_head]).reshape(-1),
            bias_part,
            jnp.broadcast_to(loss_part, (128,)),
        ]
    )
    narrow = narrow + swap_cores(narrow)
    mid_end, wide_end = norm_mid.size, norm_mid.size + norm_wide.size
    bias_end = wide_end + bias_out.shape[0]
    return (
        narrow[bias_end] * loss_factor_weight,
        grad_canvases,
        grad_reduce,
        grad_spatial,
        grad_expand,
        grad_hidden,
        grad_project,
        narrow[:mid_end].reshape(norm_mid.shape),
        narrow[mid_end:wide_end].reshape(norm_wide.shape),
        narrow[wide_end:bias_end],
        proto_grad,
    )


def solution(mesh):
    return jax.shard_map(
        per_device,
        mesh=mesh,
        in_specs=(
            P(None, ("dp", "shard"), None, None, None),
            P(None, ("dp", "shard"), None),
            P(None, ("dp", "shard"), None),
            P(("dp", "shard"), None),
            P(("dp", "shard"), None),
            P(("dp", "shard"), None),
            P(("dp", "shard"), None),
            P(("dp", "shard"), None),
            P(("dp", "shard"), None),
            P(),
            P(),
            P(),
            P(),
        ),
        out_specs=(
            P(),
            P(None, ("dp", "shard"), None, None, None),
            P(("dp", "shard"), None),
            P(("dp", "shard"), None),
            P(("dp", "shard"), None),
            P(("dp", "shard"), None),
            P(("dp", "shard"), None),
            P(),
            P(),
            P(),
            P(),
        ),
        check_vma=False,
    )
```

```python
import dataclasses

import jax
import jax.numpy as jnp
import numpy as np
from jax import lax
from jax.experimental import pallas as pl
from jax.experimental.pallas import tpu as pltpu
from jax.sharding import PartitionSpec as P

D = 2048
MID = 512
PROTOS = 3000
SIDE = 6
CROPS = 4
SINK_ITERS = 3
MICRO = 2


EPS_NORM = 1e-05
EPS_UNIT = 1e-06
SOFTMAX_HEAT = 0.1
SINK_EPS = 0.05
HIGH = lax.Precision.HIGHEST
BOTH = ("dp", "shard")
GATHERED_CODES_BYTES = 32 * 2**20
MIB = 2**20
LANES = 512
CHUNKS = 4


def product(left, right):
    return jnp.dot(left, right, preferred_element_type=jnp.float32)


def product_t(left, right):
    return lax.dot_general(
        left, right, (((0,), (0,)), ((), ())), preferred_element_type=jnp.float32
    )


def product_bt(left, right):
    return lax.dot_general(
        left, right, (((1,), (1,)), ((), ())), preferred_element_type=jnp.float32
    )


def silu_slope(values):
    sigmoid_value = jax.nn.sigmoid(values)
    return sigmoid_value * (1.0 + values * (1.0 - sigmoid_value))


@dataclasses.dataclass
class Scalars:
    array: jax.Array


@dataclasses.dataclass
class Left:
    array: jax.Array


@dataclasses.dataclass
class Loaded:
    array: jax.Array


@dataclasses.dataclass
class Streamed:
    array: jax.Array


class Arriving:
    def __init__(self, ref, copy):
        self.ref, self.copy = ref, copy
        self.shape = ref.shape

    def __getitem__(self, index):
        if self.copy is not None:
            self.copy.wait()
            self.copy = None
        return self.ref[index]


FAR, PUT_FAR = "far", "put far"


def kernel_call(body, outs, args, scratch=(), flops=0, transcendentals=0, limit=17, after=()):
    spaces = {Scalars: pltpu.SMEM, Left: pltpu.HBM, Streamed: pltpu.HBM}
    in_spaces = [spaces.get(type(a), pltpu.VMEM) for a in args] + [pl.ANY] * len(after)
    arrays = []
    for a in args:
        if isinstance(a, (Left, Loaded, Streamed)):
            a = pltpu.with_memory_space_constraint(a.array, pltpu.HBM)
        arrays.append(a.array if isinstance(a, Scalars) else a)
    used = len(arrays)
    out_spaces = [pltpu.HBM if FAR in out else pltpu.VMEM for out in outs]

    streamed = [i for i, a in enumerate(args) if isinstance(a, Streamed)]
    scratch = list(scratch)
    own_scratch = len(scratch)
    for i in streamed:
        scratch += [pltpu.VMEM(arrays[i].shape, arrays[i].dtype), pltpu.SemaphoreType.DMA]

    def kernel(*refs):
        inputs, refs = list(refs[:used]), refs[used + len(after) :]
        mine = len(outs) + own_scratch
        for k, i in enumerate(streamed):
            buffer, sem = refs[mine + 2 * k : mine + 2 * k + 2]
            copy = pltpu.make_async_copy(inputs[i], buffer, sem)
            copy.start()
            inputs[i] = Arriving(buffer, copy)
        body(*inputs, *refs[:mine])

    moved = sum(a.size * a.dtype.itemsize for a in arrays)
    return pl.pallas_call(
        kernel,
        out_shape=[
            jax.ShapeDtypeStruct(*out) if len(out) == 2 else pltpu.HBM(*out[:2]) for out in outs
        ],
        in_specs=[pl.BlockSpec(memory_space=space) for space in in_spaces],
        out_specs=[pl.BlockSpec(memory_space=space) for space in out_spaces],
        scratch_shapes=list(scratch),
        compiler_params=pltpu.CompilerParams(vmem_limit_bytes=limit * MIB),
        cost_estimate=pl.CostEstimate(
            flops=int(flops), bytes_accessed=int(moved), transcendentals=int(transcendentals)
        ),
    )(*arrays, *after)


def join_kernel(counts, *refs):
    outs = refs[sum(counts) :]
    start = 0
    for count, joined in zip(counts, outs):
        parts = refs[start : start + count]
        start += count
        length = parts[0].shape[0]

        def move(i, carry):
            for k, part in enumerate(parts):
                joined[i + k * length] = part[i]
            return carry

        lax.fori_loop(0, length, move, 0)


def join(groups, after=()):
    counts = [len(group) for group in groups]
    outs = [
        ((len(group) * group[0].shape[0],) + group[0].shape[1:], group[0].dtype)
        for group in groups
    ]
    return kernel_call(
        lambda *refs: join_kernel(counts, *refs),
        outs,
        [part for group in groups for part in group],
        after=after,
    )


def hold_kernel(source, target):
    target[...] = source[...]


def hold(values, after=()):
    return kernel_call(hold_kernel, [(values.shape, values.dtype)], [values], after=after)[0]


def add_parts_kernel(parts, *refs):
    ins, outs = refs[: 2 * len(parts)], refs[2 * len(parts) :]
    for k, count in enumerate(parts):
        kept, received = ins[2 * k : 2 * k + 2]
        kept_out, *sent = outs[: count]
        outs = outs[count:]
        length = kept_out.shape[0]

        def move(i, carry):
            kept_out[i] = kept[i].astype(jnp.float32) + received[i].astype(jnp.float32)
            for j, sent_out in enumerate(sent):
                place = i + (j + 1) * length
                total = kept[place].astype(jnp.float32) + received[place].astype(jnp.float32)
                sent_out[i] = total.astype(jnp.bfloat16)
            return carry

        lax.fori_loop(0, length, move, 0)


def add_parts(pairs, parts, after=()):
    outs = []
    for (kept, _), count in zip(pairs, parts):
        shape = (kept.shape[0] // count,) + kept.shape[1:]
        outs += [(shape, jnp.float32, PUT_FAR)] + [(shape, jnp.bfloat16, PUT_FAR)] * (count - 1)
    found = kernel_call(
        lambda *refs: add_parts_kernel(parts, *refs),
        outs,
        [Loaded(array) for pair in pairs for array in pair],
        after=after,
    )
    result = []
    for count in parts:
        result.append((found[0], list(found[1:count])))
        found = found[count:]
    return result


def swap_cores(values):
    return lax.ppermute(values, "shard", [(0, 1), (1, 0)])


def flip_dp(values, bits, size):
    return lax.ppermute(values, "dp", [(i, i ^ bits) for i in range(size)])


def flip_both(values, dp_bits, size):
    pairs = [(2 * i + c, 2 * (i ^ dp_bits[c]) + c) for i in range(size) for c in range(2)]
    return lax.ppermute(values, BOTH, pairs)


def copies_of(size):
    return size if size <= STEPS_DP else 1


def terms_over_dp(copies):
    if copies.shape[0] > 1:
        return lax.all_to_all(copies, "dp", 0, 0)
    return lax.psum(copies, "dp")


Z_BITS = (8, 4, 12)
XY_BITS = ((1, 2), (2, 1))
STEPS_DP = 16


def relative_slots(size):
    me_dp, me_core = lax.axis_index("dp"), lax.axis_index("shard")
    device = jnp.arange(2 * size, dtype=jnp.int32)
    apart_dp, apart_core = (device // 2) ^ me_dp, (device % 2) ^ me_core
    holder = device % 2
    on = lambda bit: jnp.where((apart_dp & bit) != 0, 1, 0)
    low, high = (jnp.where(holder == 0, on(zero), on(one)) for zero, one in XY_BITS)
    slot = on(Z_BITS[0]) + 2 * on(Z_BITS[1]) + 4 * low + 8 * high + size * apart_core
    return slot.astype(jnp.int32)


class Gathering:
    def __init__(self, shard, size):
        self.size = size
        self.held = shard[None]
        self.step = 0

    def send(self):
        step, held = self.step, self.held
        self.step += 1
        if step == 0:
            return [held] + [flip_dp(held, bits, self.size) for bits in Z_BITS]
        return [held, flip_both(held, XY_BITS[step - 1], self.size)]

    def finish(self, slots):
        return Gathered(self.held, swap_cores(self.held), slots)


def gather_step(parts, after=()):
    joined = join([part.send() for part in parts], after)
    for part, held in zip(parts, joined):
        part.held = held


def other_core_dp(held, size):
    device = jnp.arange(2 * size, dtype=jnp.int32)
    other = (device % 2) != lax.axis_index("shard")
    slots = jnp.where(other, size, 0) + device // 2
    return Gathered(held, swap_cores(held), slots.astype(jnp.int32))


class Scattering:
    def __init__(self, kept, sent, size, before):
        self.size = size
        self.kept = kept
        sent, _ = lax.optimization_barrier((sent, before))
        self.received = flip_both(sent, XY_BITS[1], size)
        self.step = 0

    @property
    def parts(self):
        return (2, 4)[self.step]

    def send(self, kept, sent):
        self.kept = kept
        if self.step == 0:
            self.received = flip_both(sent[0], XY_BITS[0], self.size)
        else:
            self.received = [flip_dp(part, bits, self.size) for part, bits in zip(sent, Z_BITS)]
        self.step += 1

    def finish(self):
        one, two, three = (part[0].astype(jnp.float32) for part in self.received)
        return (self.kept[0] + one) + (two + three)


def scatter_step(sums, after=()):
    found = add_parts(
        [(one.kept, one.received) for one in sums], [one.parts for one in sums], after
    )
    for one, (kept, sent) in zip(sums, found):
        one.send(kept, sent)


@dataclasses.dataclass
class Gathered:
    held: jax.Array
    other: jax.Array | None = None
    slots: jax.Array | None = None

    @property
    def count(self):
        return 1 if self.other is None else 3

    @property
    def shape(self):
        if self.other is None:
            return self.held.shape
        half, rows, width = self.held.shape
        return (2 * half * rows, width)

    def inputs(self):
        if self.other is None:
            return [Left(self.held)]
        return [Scalars(self.slots), Left(self.held), Left(self.other)]

    def scratch(self, chunks=1):
        copies = chunks if self.other is None else 2 * self.held.shape[0]
        return [pltpu.VMEM(self.shape, jnp.bfloat16), pltpu.SemaphoreType.DMA((copies,))]


def fetch_weight(inputs, weight, sems, chunks=1):
    count = sems.shape[0]
    rows = weight.shape[0] // count
    each = count // chunks

    def copy(source, i):
        target = weight.at[pl.ds(pl.multiple_of(i * rows, rows), rows)]
        return pltpu.make_async_copy(source, target, sems.at[i])

    if len(inputs) == 1:
        copies = [copy(inputs[0].at[pl.ds(i * rows, rows)], i) for i in range(count)]
        for one in copies:
            one.start()

        def wait_ordered(chunk):
            for one in copies[chunk * each : (chunk + 1) * each]:
                one.wait()

        return wait_ordered

    table, held, other = inputs
    half = held.shape[0]

    def begin(i, carry):
        slot = table[i]

        @pl.when(slot < half)
        def _():
            copy(held.at[slot], i).start()

        @pl.when(slot >= half)
        def _():
            copy(other.at[slot - half], i).start()

        return carry

    lax.fori_loop(0, count, begin, 0)

    def wait(chunk):
        def finish(i, carry):
            copy(held.at[0], i).wait()
            return carry

        lax.fori_loop(chunk * each, (chunk + 1) * each, finish, 0)

    return wait


def weight_grad_kernel(beside, table, *refs):
    left, left_peer, right, right_peer = refs[:4]
    if beside:
        second, second_peer, second_right, second_right_peer, core = refs[4:9]
        kept_ref, sent_ref, total_ref, second_ref = refs[9:]
    else:
        kept_ref, sent_ref, total_ref = refs[4:]
    half, rows, _ = kept_ref.shape
    width = right.shape[1]
    for k in range(0, total_ref.shape[0], 512):
        total_ref[k : k + 512, :] = product_t(left[:, k : k + 512], right[...]) + product_t(
            left_peer[:, k : k + 512], right_peer[...]
        )
    if beside:
        second_ref[...] = product_t(second[...], second_right[...]) + product_t(
            second_peer[...], second_right_peer[...]
        )

    def place(out_ref, slot, i):
        found = total_ref[pl.ds(pl.multiple_of(i * rows, rows), rows), :]
        out_ref[slot, :, :width] = found.astype(out_ref.dtype)
        for part in range(beside):
            start = ((2 * i + core[0]) * beside + part) * rows
            across = second_ref.shape[1]
            columns = slice(width + part * across, width + (part + 1) * across)
            found = second_ref[pl.ds(pl.multiple_of(start, rows), rows), :]
            out_ref[slot, :, columns] = found.astype(out_ref.dtype)

    def move(i, carry):
        slot = table[i]

        @pl.when(slot < half)
        def _():
            place(kept_ref, slot, i)

        @pl.when(slot >= half)
        def _():
            place(sent_ref, slot - half, i)

        return carry

    lax.fori_loop(0, 2 * half, move, 0)


def weight_grad(left, right, slots, size, before, second=None, after=()):
    depth, width = left[0].shape[1], right[0].shape[1]
    rows = depth // size
    args = [Scalars(slots), *left, *right]
    scratch, beside, extra = [pltpu.VMEM((depth, width), jnp.float32)], 0, 0
    if second is not None:
        (second_left, second_right, core) = second
        args += [*second_left, *second_right, core]
        second_shape = (second_left[0].shape[1], second_right[0].shape[1])
        beside = second_shape[0] // (2 * depth)
        extra = beside * second_shape[1]
        scratch.append(pltpu.VMEM(second_shape, jnp.float32))
    shape = (size // 2, rows, width + extra)
    kept, sent = kernel_call(
        lambda *refs: weight_grad_kernel(beside, *refs),
        [(shape, jnp.float32, PUT_FAR), (shape, jnp.bfloat16, PUT_FAR)],
        args,
        scratch=scratch,
        flops=4 * left[0].shape[0] * depth * width,
        after=after,
    )
    return Scattering(kept, sent, size, before)


def swap_columns(total):
    me = lax.axis_index("shard")
    half = total.shape[0] // 2
    mine = lax.dynamic_slice_in_dim(total, me * half, half, 0)
    other = swap_cores(lax.dynamic_slice_in_dim(total, (1 - me) * half, half, 0))
    first, second = jnp.where(me == 0, mine, other), jnp.where(me == 0, other, mine)
    return jnp.concatenate([first, second], 1)


def tiles(rows, width, high, wide):
    for r in range(0, rows, high):
        for k in range(0, width, wide):
            yield slice(r, r + high), slice(k, k + wide)


def norm_factors(terms, norm_ref, row, count):
    totals = jnp.sum(terms[...], 0)
    average = totals[0:1] / count
    inverse = lax.rsqrt(totals[1:2] / count - average * average + EPS_NORM)
    return average, inverse, norm_ref[row : row + 1, :], norm_ref[row + 1 : row + 2, :]


def normalize(values, factors, columns):
    average, inverse, gain, shift = (part[:, columns] for part in factors)
    unit = (values - average) * inverse
    return unit, gain * unit + shift


def silu(values):
    return values * jax.nn.sigmoid(values)


def norm_backward(grad, unit, factors, totals, count, columns):
    _, inverse, gain, _ = (part[:, columns] for part in factors)
    mean_grad = totals[0:1, columns] / count
    mean_product = totals[1:2, columns] / count
    return gain * inverse * (grad - mean_grad - unit * mean_product)


class Sums:
    def __init__(self, out_ref):
        self.out_ref = out_ref
        self.parts = {}

    def add(self, columns, first, second):
        key = (columns.start, columns.stop)
        fold = lambda v: jnp.sum(v.reshape(v.shape[0] // 8, 8, v.shape[1]), 0)
        first, second = fold(first), fold(second)
        if key in self.parts:
            first, second = self.parts[key][0] + first, self.parts[key][1] + second
        self.parts[key] = (first, second)

    def store(self):
        for (start, stop), (first, second) in self.parts.items():
            first = jnp.sum(first, 0, keepdims=True)
            second = jnp.sum(second, 0, keepdims=True)
            for copy in range(self.out_ref.shape[0]):
                self.out_ref[copy, 0:1, start:stop] = first
                self.out_ref[copy, 1:2, start:stop] = second


def reduce_kernel(weights, x_ref, *refs):
    inputs, refs = refs[:weights], refs[weights:]
    pre_ref, sums_ref, weight_out, weight, sems, out_sem = refs
    fetch_weight(inputs, weight, sems)(0)
    copy_out = pltpu.make_async_copy(weight, weight_out, out_sem)
    copy_out.start()
    sums = Sums(sums_ref)
    for columns in (slice(k, k + 256) for k in range(0, MID, 256)):
        pre = product(x_ref[...], weight[:, columns])
        pre_ref[:, columns] = pre
        sums.add(columns, pre, pre * pre)
    sums.store()
    copy_out.wait()


def spatial_kernel(weights, count, pre_ref, norm_ref, valid_ref, *refs):
    term_refs, *refs = refs
    inputs, refs = refs[:weights], refs[weights:]
    out_ref, sums_ref, patches_out, weight_out, padded, patches, sem, weight, sems, out_sem = refs
    wait = fetch_weight(inputs, weight, sems)
    rows = pre_ref.shape[0]
    factors = norm_factors(term_refs, norm_ref, 0, count)
    edge = jnp.zeros((EDGE, MID), jnp.float32)
    padded[0:EDGE, :] = edge
    padded[EDGE + rows :, :] = edge
    for high, columns in tiles(rows, MID, 48, 512):
        _, shifted = normalize(pre_ref[high, columns], factors, columns)
        low = silu(shifted).astype(jnp.bfloat16)
        padded[EDGE + high.start : EDGE + high.stop, columns] = low.astype(jnp.float32)
    for place in range(9):
        offset = EDGE + neighbour(place, rows // (2 * SIDE * SIDE))
        for high, columns in tiles(rows, MID, 48, 512):
            values = padded[offset + high.start : offset + high.stop, columns]
            values = values * valid_ref[high, place : place + 1]
            patches[high, place * MID : (place + 1) * MID] = values.astype(jnp.bfloat16)
    copy = pltpu.make_async_copy(patches, patches_out, sem)
    copy.start()
    wait(0)
    copy_out = pltpu.make_async_copy(weight, weight_out, out_sem)
    copy_out.start()
    sums = Sums(sums_ref)
    for columns in (slice(k, k + 256) for k in range(0, MID, 256)):
        pre = product(patches[...], weight[:, columns])
        out_ref[:, columns] = pre
        sums.add(columns, pre, pre * pre)
    sums.store()
    copy.wait()
    copy_out.wait()


def expand_kernel(weights, count, pre_ref, norm_ref, *refs):
    term_refs, *refs = refs
    inputs, refs = refs[:weights], refs[weights:]
    act_ref, out_ref, sums_ref, weight_out, side_ref, weight, sems, out_sem = refs
    wait = fetch_weight(inputs, weight, sems)
    factors = norm_factors(term_refs, norm_ref, 2, count)
    for high, columns in tiles(pre_ref.shape[0], MID, 48, 512):
        _, shifted = normalize(pre_ref[high, columns], factors, columns)
        act_ref[high, columns] = silu(shifted).astype(jnp.bfloat16)
    wait(0)
    copy_out = pltpu.make_async_copy(weight, weight_out, out_sem)
    copy_out.start()
    if weight.shape[1] > D:
        side_ref[...] = weight[:, D:]
    else:
        side_ref[...] = jnp.zeros_like(side_ref)
    sums = Sums(sums_ref)
    for columns in (slice(k, k + 256) for k in range(0, D, 256)):
        pre = product(act_ref[...], weight[:, columns])
        out_ref[:, columns] = pre
        sums.add(columns, pre, pre * pre)
    sums.store()
    copy_out.wait()


def split(values):
    high = values.astype(jnp.bfloat16)
    return high, (values - high.astype(jnp.float32)).astype(jnp.bfloat16)


def pool_kernel(weights, count, pre_ref, x_ref, norm_ref, pool_ref, size_ref, *refs):
    term_refs, *refs = refs
    inputs, refs = refs[:weights], refs[weights:]
    pooled_ref, out_ref, sums_ref, project_ref, high_ref, rest_ref, weight, sems = refs
    wait = fetch_weight(inputs, weight, sems, CHUNKS)
    factors = norm_factors(term_refs, norm_ref, 0, count)
    rows = pre_ref.shape[0]
    for k in range(0, D, 256):
        for high, columns in tiles(rows, 256, 96, 256):
            across = slice(k + columns.start, k + columns.stop)
            _, shifted = normalize(pre_ref[high, across], factors, across)
            block = silu(shifted + x_ref[high, across].astype(jnp.float32))
            high_ref[high, columns], rest_ref[high, columns] = split(block)
        pooled = product(pool_ref[...], high_ref[...]) + product(pool_ref[...], rest_ref[...])
        pooled_ref[:, k : k + 256] = (pooled / size_ref[...]).astype(jnp.bfloat16)
    step = D // CHUNKS
    total = 0.0
    for chunk in range(CHUNKS):
        wait(chunk)
        part = slice(chunk * step, (chunk + 1) * step)
        total = total + product(pooled_ref[:, part], weight[part, :D])
    out_ref[...] = total
    project_ref[...] = weight[:, D:]
    sums = Sums(sums_ref)
    for columns in (slice(k, k + 512) for k in range(0, D, 512)):
        pre = out_ref[:, columns]
        sums.add(columns, pre, pre * pre)
    sums.store()


def embed_kernel(count, pre_ref, norm_ref, project_ref, bias_ref, *refs):
    term_refs, *refs = refs
    act_ref, unit_ref, inverse_ref, low_ref = refs
    factors = norm_factors(term_refs, norm_ref, 2, count)
    for high, columns in tiles(pre_ref.shape[0], D, pre_ref.shape[0], 512):
        _, shifted = normalize(pre_ref[high, columns], factors, columns)
        act_ref[high, columns] = silu(shifted).astype(jnp.bfloat16)
    embed = product(act_ref[...], project_ref[...]) + bias_ref[...]
    inverse = lax.rsqrt(jnp.sum(embed * embed, 1, keepdims=True) + EPS_UNIT)
    unit = embed * inverse
    unit_ref[...] = unit
    inverse_ref[...] = jnp.broadcast_to(inverse, inverse_ref.shape)
    low_ref[...] = jnp.broadcast_to(unit.astype(jnp.bfloat16)[None], low_ref.shape)


def embed_back_kernel(
    count, grad_ref, unit_ref, inverse_ref, project_ref, pre_ref, norm_ref, *refs
):
    term_refs, *refs = refs
    low_ref, out_ref, sums_ref, bias_ref = refs
    grad, unit = grad_ref[...], unit_ref[...]
    embed_grad = inverse_ref[...] * (grad - unit * jnp.sum(grad * unit, 1, keepdims=True))
    low_ref[...] = embed_grad.astype(jnp.bfloat16)
    bias_ref[...] = jnp.sum(embed_grad, 0, keepdims=True)
    factors = norm_factors(term_refs, norm_ref, 2, count)
    sums = Sums(sums_ref)
    for columns in (slice(k, k + 512) for k in range(0, D, 512)):
        back = product_bt(low_ref[...], project_ref[columns, :])
        head_unit, shifted = normalize(pre_ref[:, columns], factors, columns)
        back = back * silu_slope(shifted)
        out_ref[:, columns] = back
        sums.add(columns, back, back * head_unit)
    sums.store()


def pool_back_kernel(
    weights,
    crop_count,
    count,
    grad_ref,
    head_pre_ref,
    pre_ref,
    x_ref,
    norm_ref,
    spread_ref,
    size_ref,
    *refs,
):
    head_terms, head_back, pre_terms, *refs = refs
    inputs, refs = refs[:weights], refs[weights:]
    low_ref, own_ref, other_ref, sums_ref, weight, sems = refs
    wait = fetch_weight(inputs, weight, sems, CHUNKS)
    step = D // CHUNKS
    head_factors = norm_factors(head_terms, norm_ref, 2, crop_count)
    totals = jnp.sum(head_back[...], 0)
    for columns in (slice(k, k + 512) for k in range(0, D, 512)):
        unit, _ = normalize(head_pre_ref[:, columns], head_factors, columns)
        grad = norm_backward(
            grad_ref[:, columns], unit, head_factors, totals, crop_count, columns
        )
        low_ref[:, columns] = grad.astype(jnp.bfloat16)
    factors = norm_factors(pre_terms, norm_ref, 0, count)
    sums = Sums(sums_ref)
    own_rows = own_ref.shape[0]
    for chunk in range(CHUNKS):
        wait(chunk)
        part = slice(chunk * step, (chunk + 1) * step)
        pooled = product_bt(low_ref[...], weight[part, :D]) / size_ref[...]
        high_part, rest_part = split(pooled)
        for rows, columns in tiles(2 * own_rows, part.stop - part.start, 48, 256):
            across = slice(part.start + columns.start, part.start + columns.stop)
            spread = spread_ref[rows, :]
            out_grad = product(spread, high_part[:, columns]) + product(
                spread, rest_part[:, columns]
            )
            unit, shifted = normalize(pre_ref[rows, across], factors, across)
            joined = shifted + x_ref[rows, across].astype(jnp.float32)
            joined_grad = out_grad * silu_slope(joined)
            if rows.start < own_rows:
                own_ref[rows, across] = joined_grad
            else:
                other_ref[rows.start - own_rows : rows.stop - own_rows, across] = joined_grad
            sums.add(across, joined_grad, joined_grad * unit)
    sums.store()


def column_halves(low_ref, core, kept_ref, sent_ref):
    half = kept_ref.shape[1]
    for out_ref, which in ((kept_ref, core[0]), (sent_ref, 1 - core[0])):
        out_ref[...] = low_ref[:, pl.ds(pl.multiple_of(which * half, half), half)]


def expand_back_kernel(
    count, core, own_ref, other_ref, pre_ref, wide_ref, weight_ref, before_ref, mid_ref, bias_ref, *refs
):
    pre_terms, back_terms, before_terms, kept_ref, sent_ref, out_ref, sums_ref, low_ref = refs
    factors = norm_factors(pre_terms, wide_ref, 0, count)
    totals = jnp.sum(back_terms[...], 0)
    own_rows = own_ref.shape[0]
    for rows, columns in tiles(2 * own_rows, D, 48, 512):
        unit, _ = normalize(pre_ref[rows, columns], factors, columns)
        if rows.start < own_rows:
            grad = own_ref[rows, columns]
        else:
            grad = other_ref[rows.start - own_rows : rows.stop - own_rows, columns]
        grad = norm_backward(grad, unit, factors, totals, count, columns)
        low_ref[rows, columns] = grad.astype(jnp.bfloat16)
    column_halves(low_ref, core, kept_ref, sent_ref)
    factors = norm_factors(before_terms, mid_ref, 2, count)
    sums = Sums(sums_ref)
    for columns in (slice(k, k + 256) for k in range(0, MID, 256)):
        back = product_bt(low_ref[...], weight_ref[columns, :D])
        unit, shifted = normalize(before_ref[:, columns], factors, columns)
        back = back * silu_slope(shifted)
        out_ref[:, columns] = back
        sums.add(columns, back, back * unit)
    sums.store()
    bias = jnp.concatenate([bias_ref[...], jnp.zeros_like(bias_ref)], 0)
    for copy in range(sums_ref.shape[0]):
        sums_ref[copy, :, MID:] = bias


def spatial_back_kernel(
    count, core, grad_ref, pre_ref, norm_ref, weight_ref, before_ref, valid_ref, *refs
):
    pre_terms, back_terms, before_terms, kept_ref, sent_ref, out_ref, sums_ref, slots, low_ref = refs
    rows = grad_ref.shape[0]
    factors = norm_factors(pre_terms, norm_ref, 2, count)
    totals = jnp.sum(back_terms[...], 0)
    for high, columns in tiles(rows, MID, 48, 512):
        unit, _ = normalize(pre_ref[high, columns], factors, columns)
        grad = norm_backward(grad_ref[high, columns], unit, factors, totals, count, columns)
        low_ref[high, columns] = grad.astype(jnp.bfloat16)
    column_halves(low_ref, core, kept_ref, sent_ref)
    edge = jnp.zeros((EDGE, MID), jnp.float32)
    for place in range(9):
        slots[place, 0:EDGE, :] = edge
        slots[place, EDGE + rows :, :] = edge
        for columns in (slice(k, k + 256) for k in range(0, MID, 256)):
            patch = product_bt(
                low_ref[...],
                weight_ref[place * MID + columns.start : place * MID + columns.stop, :],
            )
            slots[place, EDGE : EDGE + rows, columns] = patch * valid_ref[:, place : place + 1]
    factors = norm_factors(before_terms, norm_ref, 0, count)
    sums = Sums(sums_ref)
    for high, columns in tiles(rows, MID, 48, 256):
        back = 0.0
        for place in range(9):
            start = EDGE - neighbour(place, rows // (2 * SIDE * SIDE)) + high.start
            back = back + slots[place, start : start + high.stop - high.start, columns]
        unit, shifted = normalize(before_ref[high, columns], factors, columns)
        back = back * silu_slope(shifted)
        out_ref[high, columns] = back
        sums.add(columns, back, back * unit)
    sums.store()


def reduce_back_kernel(
    count,
    core,
    grad_ref,
    pre_ref,
    norm_ref,
    pre_terms,
    back_terms,
    low_ref,
    other_ref,
    kept_ref,
    sent_ref,
):
    rows = grad_ref.shape[0]
    factors = norm_factors(pre_terms, norm_ref, 0, count)
    totals = jnp.sum(back_terms[...], 0)
    for high, columns in tiles(rows, MID, 48, 512):
        unit, _ = normalize(pre_ref[high, columns], factors, columns)
        grad = norm_backward(grad_ref[high, columns], unit, factors, totals, count, columns)
        low_ref[high, columns] = grad.astype(jnp.bfloat16)
    other_ref[...] = low_ref[rows // 2 :, :]
    column_halves(low_ref, core, kept_ref, sent_ref)


def arrange_kernel(core, canvases_ref, own_ref, other_ref, rows_ref):
    _, _, _, canvas_count, _ = canvases_ref.shape
    for which, out_ref in enumerate((own_ref, other_ref)):
        micro = core[0] if which == 0 else 1 - core[0]
        for pixel in range(SIDE * SIDE):
            rows = slice(pixel * canvas_count, (pixel + 1) * canvas_count)
            values = canvases_ref[micro, pixel // SIDE, pixel % SIDE]
            rows_ref[rows, :] = values.astype(jnp.float32)
        out_ref[...] = rows_ref[...].astype(jnp.bfloat16)


def input_grad_kernel(
    core, own_ref, other_ref, low_ref, other_low_ref, weight_ref, out_ref, rows_ref
):
    own_rows = own_ref.shape[0]
    canvas_count = out_ref.shape[3]
    for which in range(2):
        micro = core[0] if which == 0 else 1 - core[0]
        grad_ref = own_ref if which == 0 else other_ref
        low = low_ref[:own_rows, :] if which == 0 else other_low_ref[...]
        for columns in (slice(k, k + 512) for k in range(0, D, 512)):
            rows_ref[:, columns] = grad_ref[:, columns] + product_bt(low, weight_ref[columns, :])
        for pixel in range(SIDE * SIDE):
            rows = slice(pixel * canvas_count, (pixel + 1) * canvas_count)
            out_ref[micro, pixel // SIDE, pixel % SIDE] = rows_ref[rows, :]


def inside_canvas(own_canvases):
    valid = np.zeros((2, SIDE, SIDE, own_canvases, 16), np.float32)
    for place in range(9):
        down, right = place // 3 - 1, place % 3 - 1
        for y in range(SIDE):
            for x in range(SIDE):
                valid[:, y, x, :, place] = 0 <= y + down < SIDE and 0 <= x + right < SIDE
    return jnp.asarray(valid.reshape(-1, 16))


def neighbour(place, own_canvases):
    return ((place // 3 - 1) * SIDE + place % 3 - 1) * own_canvases


EDGE = 32


def add_columns(total_ref, columns, values):
    rows, width = values.shape
    total_ref[:, columns] += jnp.sum(values.reshape(rows // 8, 8, width), 0)


def codes_kernel(
    crops,
    device_crops,
    place,
    units_ref,
    side_ref,
    prototypes_ref,
    loss_ref,
    proto_grad_ref,
    unit_grad_ref,
    proto_ref,
    partner_ref,
    codes_ref,
    heat_ref,
    score_ref,
    total_ref,
    scale_ref,
    inverse_ref,
    *,
    factor,
):
    rows_all, width = codes_ref.shape
    own = unit_grad_ref.shape[0]
    chunks = [slice(k, k + LANES) for k in range(0, width, LANES)]
    real = lax.broadcasted_iota(jnp.int32, (1, width), 1) < PROTOS

    dim = units_ref.shape[1]
    proto_ref[PROTOS // 16 * 16 :, :] = jnp.zeros((width - PROTOS // 16 * 16, dim), jnp.bfloat16)
    proto_ref[:PROTOS, :] = prototypes_ref[...]

    queue_rows = side_ref.shape[0]
    device_rows = queue_rows // (crops // device_crops)
    crop = lax.broadcasted_iota(jnp.int32, (crops, queue_rows), 0)
    holder = crop // device_crops ^ place[1]
    row = lax.broadcasted_iota(jnp.int32, (crops, queue_rows), 1)
    holds = (row == holder * device_rows).astype(jnp.bfloat16)
    found = product(holds, side_ref[:, dim:])
    crop = lax.broadcasted_iota(jnp.int32, found.shape, 0)
    lane = lax.broadcasted_iota(jnp.int32, found.shape, 1)
    here = lane == place[1] * device_crops + crop % device_crops
    partner = jnp.sum(jnp.where(here, found, 0.0), 1, keepdims=True)
    partner_ref[...] = partner.astype(jnp.int32)

    def scores(rows, columns, queue=False):
        left = side_ref[rows, :dim] if queue else units_ref[rows, :]
        return product_bt(left, proto_ref[columns, :])

    def keep(values, columns):
        if columns.stop <= PROTOS:
            return values
        lanes = columns.start + lax.broadcasted_iota(jnp.int32, values.shape, 1)
        return jnp.where(lanes < PROTOS, values, 0.0)

    def fold(values):
        return sum(values[:, k : k + 128] for k in range(0, values.shape[1], 128))

    total_ref[...] = jnp.zeros_like(total_ref)

    for queue, start, count in ((False, 0, crops), (True, crops, queue_rows)):

        def first(i, carry):
            rows = pl.ds(pl.multiple_of(i * 128, 128), 128)
            target = pl.ds(pl.multiple_of(start + i * 128, 128), 128)
            for columns in chunks:
                score = scores(rows, columns, queue)
                powers = keep(jnp.exp(score * (1.0 / SINK_EPS)), columns)
                codes_ref[target, columns] = powers
                add_columns(total_ref, columns, powers)
            return carry

        lax.fori_loop(0, count // 128, first, 0)

    def column_factors(turn):
        total = jnp.sum(total_ref[...], 0, keepdims=True)
        total = jnp.where(real, total, 1.0)
        if turn == 0:
            scale = jnp.where(total > 1e30, 2.0**-64, 1.0)
            scale_ref[...] = jnp.broadcast_to(scale, scale_ref.shape)
            total = total * scale
        inverse_ref[...] = jnp.broadcast_to(1.0 / total, inverse_ref.shape)

    def divided(turn, rows, columns):
        values = codes_ref[rows, columns]
        if turn == 0:
            values = values * scale_ref[0:1, columns]
        return values * inverse_ref[0:1, columns]

    def row_inverse(turn, rows):
        part = sum(fold(divided(turn, rows, columns)) for columns in chunks)
        return 1.0 / jnp.sum(part, 1, keepdims=True)

    for turn in range(SINK_ITERS - 1):
        column_factors(turn)
        total_ref[...] = jnp.zeros_like(total_ref)

        def both(i, carry):
            rows = pl.ds(pl.multiple_of(i * 64, 64), 64)
            inverse = row_inverse(turn, rows)
            for columns in chunks:
                values = divided(turn, rows, columns) * inverse
                codes_ref[rows, columns] = values
                add_columns(total_ref, columns, values)
            return carry

        lax.fori_loop(0, rows_all // 64, both, 0)

    column_factors(SINK_ITERS - 1)
    proto_grad_ref[...] = jnp.zeros_like(proto_grad_ref)
    loss_ref[...] = jnp.zeros_like(loss_ref)
    block = 128

    def last(i, carry):
        rows = pl.ds(pl.multiple_of(i * block, block), block)
        inverse = row_inverse(SINK_ITERS - 1, rows)
        row = lax.broadcasted_iota(jnp.int32, (block, block), 0)
        column = lax.broadcasted_iota(jnp.int32, (block, block), 1)
        pick = (column == (row // CROPS) * CROPS + partner_ref[rows, :]).astype(jnp.bfloat16)
        heat_part = jnp.zeros((block, 128), jnp.float32)
        target_part = jnp.zeros((block, 128), jnp.float32)
        loss_part = jnp.zeros((block, 128), jnp.float32)
        for columns in chunks:
            score = scores(rows, columns)
            heat = keep(jnp.exp(score * (1.0 / SOFTMAX_HEAT)), columns)
            heat_ref[:, columns] = heat
            heat_part += fold(heat)
            codes = divided(SINK_ITERS - 1, rows, columns) * inverse
            high = codes.astype(jnp.bfloat16)
            rest = (codes - high.astype(jnp.float32)).astype(jnp.bfloat16)
            target = product(pick, high) + product(pick, rest)
            codes_ref[rows, columns] = target
            target_part += fold(target)
            loss_part += fold(target * score)
        heat_sum = jnp.sum(heat_part, 1, keepdims=True)
        target_sum = jnp.sum(target_part, 1, keepdims=True)
        row_loss = (
            target_sum * jnp.log(heat_sum)
            - jnp.sum(loss_part, 1, keepdims=True) * (1.0 / SOFTMAX_HEAT)
        )
        loss_ref[...] += jnp.broadcast_to(jnp.sum(row_loss, 0, keepdims=True), loss_ref.shape)
        ratio = target_sum / heat_sum * factor
        for columns in chunks:
            grad = heat_ref[:, columns] * ratio - codes_ref[rows, columns] * factor
            low = grad.astype(jnp.bfloat16)
            score_ref[rows, columns] = low
            proto_grad_ref[:, columns] += product_t(units_ref[rows, :], low)
        return carry

    lax.fori_loop(0, crops // block, last, 0)
    mine = pl.ds(pl.multiple_of(place[0], own), own)
    unit_grad_ref[...] = product(score_ref[mine, :], proto_ref[...])


def gathered_loss(units, side, prototypes, place, own, device_crops, loss_factor_weight):
    crops, dim = units.shape
    width = -(-PROTOS // LANES) * LANES
    rows_all = crops + side.shape[0]
    f32, bf16 = jnp.float32, jnp.bfloat16
    loss, proto_grad, unit_grad = kernel_call(
        lambda *refs: codes_kernel(
            crops, device_crops, *refs, factor=loss_factor_weight / SOFTMAX_HEAT
        ),
        [((8, 128), f32), ((dim, width), f32), ((own, dim), f32)],
        [Scalars(place), units, side, prototypes],
        scratch=[
            pltpu.VMEM((width, dim), bf16),
            pltpu.VMEM((crops, 1), jnp.int32),
            pltpu.VMEM((rows_all, width), f32),
            pltpu.VMEM((128, width), f32),
            pltpu.VMEM((crops, width), bf16),
            pltpu.VMEM((8, width), f32),
            pltpu.VMEM((8, width), f32),
            pltpu.VMEM((8, width), f32),
        ],
        flops=2 * width * (rows_all * dim + 6 * crops * dim),
        transcendentals=width * (rows_all + crops),
        limit=24,
    )
    return loss[0, 0], proto_grad, unit_grad


def sinkhorn(batch_codes, stored_codes, total):
    for turn in range(SINK_ITERS):
        column_totals = total(jnp.sum(batch_codes, 0) + jnp.sum(stored_codes, 0))
        batch_codes = batch_codes / column_totals
        stored_codes = stored_codes / column_totals
        batch_codes = batch_codes / jnp.sum(batch_codes, 1, keepdims=True)
        stored_codes = stored_codes / jnp.sum(stored_codes, 1, keepdims=True)
    return batch_codes


def swapped_loss(scores, codes, pick, loss_factor_weight):
    rows = scores.shape[0]
    target = jnp.einsum(
        "cab,cbk->cak", pick, codes.reshape(rows // CROPS, CROPS, PROTOS), precision=HIGH
    ).reshape(rows, PROTOS)
    log_likelihoods = jax.nn.log_softmax(scores / SOFTMAX_HEAT, axis=1)
    score_grad = (jnp.exp(log_likelihoods) * jnp.sum(target, 1, keepdims=True) - target) * (
        loss_factor_weight / SOFTMAX_HEAT
    )
    return -jnp.sum(target * log_likelihoods), score_grad.astype(jnp.bfloat16)


def per_device(
    canvases,
    crop_map,
    partner,
    queue,
    w_reduce,
    w_spatial,
    w_expand,
    w_hidden,
    w_project,
    norm_mid,
    norm_wide,
    bias_out,
    prototypes,
):
    f32, bf16 = jnp.float32, jnp.bfloat16
    size = lax.axis_size("dp")
    me_dp, me_core = lax.axis_index("dp"), lax.axis_index("shard")
    core = Scalars(me_core.astype(jnp.int32).reshape(1))
    own_canvases = canvases.shape[1]
    canvas_count = 2 * own_canvases
    pixels = SIDE * SIDE
    own_rows = own_canvases * pixels
    local_rows = canvas_count * pixels
    local_crops = canvas_count * CROPS
    pixel_total = float(local_rows * size)
    crop_count = local_crops * size
    crop_total = float(crop_count)
    loss_factor_weight = 1.0 / (MICRO * crop_total)
    crop_ids = jnp.arange(CROPS, dtype=jnp.int32)
    valid = inside_canvas(own_canvases)
    proj = bias_out.shape[0]
    partner_size = partner.size
    copies = copies_of(size)
    by_steps = size == STEPS_DP
    if by_steps:
        slots = relative_slots(size)
        chip_slots = lax.dynamic_slice_in_dim(slots.reshape(size, 2), me_core, 1, 1)[:, 0]

    def both_cores(values):
        mine = lax.dynamic_index_in_dim(values, me_core, 0, keepdims=False)
        other = lax.dynamic_index_in_dim(values, 1 - me_core, 0, keepdims=False)
        return jnp.concatenate([mine, swap_cores(other)], 0)

    def gather_whole(shard):
        return Gathered(lax.all_gather(shard, BOTH, axis=0, tiled=True))

    head_shard = jnp.concatenate([w_hidden, w_project], 1)
    beside = queue.shape[1]
    gathered_codes = (
        crop_count * PROTOS * 4 <= GATHERED_CODES_BYTES
        and queue.shape[0] == w_expand.shape[0]
        and partner_size <= beside
    )
    if gathered_codes:
        partners = jnp.pad(
            partner.astype(bf16).reshape(1, -1),
            ((0, 0), (0, beside - partner_size)),
        )
        partners = jnp.broadcast_to(partners, (queue.shape[0], beside))
        w_expand = jnp.concatenate([w_expand, queue, partners], 1)

    labels = both_cores(jnp.concatenate([crop_map, partner], 2))
    crop_map, partner = labels[:, :pixels], labels[:, pixels:]
    crop_of = jnp.arange(local_crops, dtype=jnp.int32)
    pixel_crop = crop_map + CROPS * jnp.arange(canvas_count, dtype=jnp.int32)[:, None]
    pixel_crop = pixel_crop.reshape(2, own_canvases, pixels).swapaxes(1, 2).reshape(local_rows)
    pool = (crop_of[:, None] == pixel_crop[None, :]).astype(bf16)
    spread = (pixel_crop[:, None] == crop_of[None, :]).astype(bf16)
    crop_sizes = jnp.sum(pool.astype(f32), 1, keepdims=True)

    half_rows = ((own_rows, D), bf16)
    own_x, other_x = kernel_call(
        arrange_kernel,
        [half_rows, half_rows],
        [core, canvases.transpose(0, 2, 3, 1, 4)],
        scratch=[pltpu.VMEM((own_rows, D), f32)],
    )
    input_rows = join([(own_x[None], swap_cores(other_x)[None])])[0].reshape(local_rows, D)

    if by_steps:
        reduce_part = Gathering(w_reduce, size)
        gather_step([reduce_part])
        spatial_part = Gathering(hold(w_spatial, [reduce_part.held]), size)
        gather_step([reduce_part], [pool, spread, crop_sizes, input_rows])
        head_held = lax.all_gather(hold(head_shard, [reduce_part.held]), "dp", axis=0)
        gather_step([reduce_part, spatial_part])
        expand_part = Gathering(hold(w_expand, [spatial_part.held]), size)
        reduce_all = reduce_part.finish(slots)
    else:
        reduce_all = gather_whole(w_reduce)

    mid_rows, wide_rows = ((local_rows, MID), f32), ((local_rows, D), f32)
    mid_sums, wide_sums = ((copies, 2, MID), f32), ((copies, 2, D), f32)

    def weight_out(weight):
        return (weight.shape, bf16, FAR)

    pre_one, sums, full_reduce = kernel_call(
        lambda *refs: reduce_kernel(reduce_all.count, *refs),
        [mid_rows, mid_sums, weight_out(reduce_all)],
        [input_rows] + reduce_all.inputs(),
        scratch=reduce_all.scratch() + [pltpu.SemaphoreType.DMA],
        flops=2 * local_rows * D * MID,
    )
    terms_one = terms_over_dp(sums)
    if by_steps:
        gather_step([spatial_part, expand_part], [sums])
        gather_step([spatial_part], [terms_one])
        spatial_all = spatial_part.finish(slots)
    else:
        spatial_all, expand_all = gather_whole(w_spatial), gather_whole(w_expand)

    pre_two, sums, image_patches, full_spatial = kernel_call(
        lambda *refs: spatial_kernel(spatial_all.count, pixel_total, *refs),
        [
            mid_rows,
            mid_sums,
            ((local_rows, 9 * MID), bf16, FAR),
            weight_out(spatial_all),
        ],
        [pre_one, norm_mid, valid, terms_one] + spatial_all.inputs(),
        scratch=[
            pltpu.VMEM((local_rows + 2 * EDGE, MID), f32),
            pltpu.VMEM((local_rows, 9 * MID), bf16),
            pltpu.SemaphoreType.DMA,
        ]
        + spatial_all.scratch()
        + [pltpu.SemaphoreType.DMA],
        flops=2 * local_rows * 9 * MID * MID,
    )
    terms_two = terms_over_dp(sums)
    if by_steps:
        gather_step([expand_part], [sums])
        gather_step([expand_part], [terms_two])
        expand_all = expand_part.finish(slots)

    side = ((expand_all.shape[0], max(expand_all.shape[1] - D, 128)), bf16)
    act_two, pre_three, sums, full_expand, side = kernel_call(
        lambda *refs: expand_kernel(expand_all.count, pixel_total, *refs),
        [((local_rows, MID), bf16), wide_rows, wide_sums, weight_out(expand_all), side],
        [pre_two, norm_mid, terms_two] + expand_all.inputs(),
        scratch=expand_all.scratch() + [pltpu.SemaphoreType.DMA],
        flops=2 * local_rows * D * MID,
    )
    terms_three = terms_over_dp(sums)
    if by_steps:
        head_held, _ = lax.optimization_barrier((head_held, sums))
        head = other_core_dp(head_held, size)
    else:
        head = gather_whole(head_shard)

    crop_rows = ((local_crops, D), f32)
    pooled_low, pre_head, sums, full_project = kernel_call(
        lambda *refs: pool_kernel(head.count, pixel_total, *refs),
        [((local_crops, D), bf16), crop_rows, wide_sums, ((D, proj), bf16)],
        [pre_three, input_rows, norm_wide, pool, crop_sizes, terms_three] + head.inputs(),
        scratch=[pltpu.VMEM((local_rows, 256), bf16), pltpu.VMEM((local_rows, 256), bf16)]
        + head.scratch(CHUNKS),
        flops=2 * local_crops * D * D,
        transcendentals=local_rows * D,
    )
    terms_head = terms_over_dp(sums)

    embed_rows = ((local_crops, proj), f32)
    act_head, unit_embed, inv_length, unit_low = kernel_call(
        lambda *refs: embed_kernel(crop_total, *refs),
        [
            ((local_crops, D), bf16),
            embed_rows,
            embed_rows,
            ((copies, local_crops, proj), bf16),
        ],
        [pre_head, norm_wide, Streamed(full_project), bias_out.reshape(1, proj), terms_head],
        flops=2 * local_crops * D * proj,
    )

    if gathered_codes:
        all_units = lax.all_to_all(unit_low, "dp", 0, 0).reshape(crop_count, proj)
        loss_part, proto_part, unit_grad = gathered_loss(
            all_units,
            side,
            prototypes,
            jnp.stack([me_dp * local_crops, me_core]).astype(jnp.int32),
            local_crops,
            own_canvases * CROPS,
            loss_factor_weight,
        )
    else:
        chip_queue = jnp.concatenate([queue, swap_cores(queue)], 0)
        queue_codes = jnp.exp(product_bt(chip_queue, prototypes) / SINK_EPS)
        pick = (partner[:, :, None] == crop_ids[None, None, :]).astype(f32)
        all_units = unit_low
        scores = product_bt(unit_low[0], prototypes)
        codes = sinkhorn(
            jnp.exp(scores / SINK_EPS), queue_codes, lambda sums: lax.psum(sums, "dp")
        )
        loss_part, score_low = swapped_loss(scores, codes, pick, loss_factor_weight)
        proto_part, loss_part = lax.psum((product_t(unit_low[0], score_low), loss_part), "dp")
        unit_grad = product(score_low, prototypes)

    embed_low, head_act_grad, sums, bias_part = kernel_call(
        lambda *refs: embed_back_kernel(crop_total, *refs),
        [((local_crops, proj), bf16), crop_rows, wide_sums, ((1, proj), f32)],
        [
            unit_grad,
            unit_embed,
            inv_length,
            Streamed(full_project),
            Streamed(pre_head),
            norm_wide,
            terms_head,
        ],
        flops=2 * local_crops * D * proj,
    )
    back_head = terms_over_dp(sums)

    left = lax.all_gather(pooled_low, "dp", axis=0, tiled=True)

    own_part = ((own_rows, D), f32)
    head_low, own_grad, other_grad, sums = kernel_call(
        lambda *refs: pool_back_kernel(head.count, crop_total, pixel_total, *refs),
        [((local_crops, D), bf16), own_part, own_part, wide_sums],
        [
            head_act_grad,
            pre_head,
            Streamed(pre_three),
            Streamed(input_rows),
            norm_wide,
            spread,
            crop_sizes,
            terms_head,
            back_head,
            terms_three,
        ]
        + head.inputs(),
        scratch=head.scratch(CHUNKS),
        flops=2 * local_crops * D * D,
        transcendentals=local_rows * D,
        after=[left],
    )
    back_three = terms_over_dp(sums)
    other_grad, _ = lax.optimization_barrier((other_grad, back_three))
    peer_grad = swap_cores(other_grad)

    right = lax.all_gather(head_low, "dp", axis=0, tiled=True)

    def low_halves(width):
        return [((local_rows, width // 2), bf16)] * 2

    three_kept, three_sent, two_act_grad, sums = kernel_call(
        lambda *refs: expand_back_kernel(pixel_total, *refs),
        [*low_halves(D), mid_rows, ((copies, 2, MID + proj), f32)],
        [
            core,
            own_grad,
            other_grad,
            Streamed(pre_three),
            norm_wide,
            Streamed(full_expand),
            Streamed(pre_two),
            norm_mid,
            bias_part,
            terms_three,
            back_three,
            terms_two,
        ],
        scratch=[pltpu.VMEM((local_rows, D), bf16)],
        flops=2 * local_rows * D * MID,
    )
    back_two = terms_over_dp(sums)
    before_two = []
    if by_steps:
        expand_sum = weight_grad(
            (act_two, swap_cores(act_two)),
            (three_kept, swap_cores(three_sent)),
            chip_slots,
            size,
            back_two,
            (
                (act_head, swap_cores(act_head)),
                (embed_low, swap_cores(embed_low)),
                core,
            ),
            after=[sums],
        )
        before_two = [expand_sum.kept]

    two_kept, two_sent, one_act_grad, sums = kernel_call(
        lambda *refs: spatial_back_kernel(pixel_total, *refs),
        [*low_halves(MID), mid_rows, mid_sums],
        [
            core,
            two_act_grad,
            Streamed(pre_two),
            norm_mid,
            Streamed(full_spatial),
            Streamed(pre_one),
            valid,
            terms_two,
            back_two,
            terms_one,
        ],
        scratch=[
            pltpu.VMEM((9, local_rows + 2 * EDGE, MID), f32),
            pltpu.VMEM((local_rows, MID), bf16),
        ],
        flops=2 * local_rows * 9 * MID * MID,
        after=before_two,
    )
    back_one = terms_over_dp(sums)
    before_one = []
    if by_steps:
        spatial_sum = weight_grad(
            (image_patches, swap_cores(image_patches)),
            (two_kept, swap_cores(two_sent)),
            chip_slots,
            size,
            two_kept,
            after=[sums],
        )
        before_one = [spatial_sum.kept]

    one_low, other_low, one_kept, one_sent = kernel_call(
        lambda *refs: reduce_back_kernel(pixel_total, *refs),
        [((local_rows, MID), bf16), ((own_rows, MID), bf16), *low_halves(MID)],
        [core, one_act_grad, Streamed(pre_one), norm_mid, terms_one, back_one],
        after=before_one,
    )
    if by_steps:
        scatter_step([expand_sum])
        reduce_sum = weight_grad(
            (input_rows, swap_cores(input_rows)),
            (one_kept, swap_cores(one_sent)),
            chip_slots,
            size,
            one_low,
        )
        scatter_step([spatial_sum, expand_sum])
        scatter_step([reduce_sum])
        last = reduce_sum.kept
        other_low, _ = lax.optimization_barrier((other_low, last))
    else:
        last = one_low

    proto_part, left, right, _ = lax.optimization_barrier((proto_part, left, right, last))
    if gathered_codes:
        proto_part = proto_part[:, :PROTOS]
    proto_grad = (proto_part + swap_cores(proto_part)).T
    chip_rows = 2 * w_hidden.shape[0]
    hidden_part = product_t(
        lax.dynamic_slice_in_dim(left, me_dp * chip_rows, chip_rows, 1), right
    )

    def own_half(part):
        half = chip_rows // 2
        mine = lax.dynamic_slice_in_dim(part, me_core * half, half, 0)
        other = lax.dynamic_slice_in_dim(part, (1 - me_core) * half, half, 0)
        return mine + swap_cores(other)

    grad_hidden = own_half(hidden_part)
    by_pixel = kernel_call(
        input_grad_kernel,
        [((MICRO, SIDE, SIDE, own_canvases, D), f32)],
        [core, own_grad, peer_grad, one_low, swap_cores(other_low), full_reduce],
        scratch=[pltpu.VMEM((own_rows, D), f32)],
        flops=2 * local_rows * D * MID,
    )[0]

    if by_steps:
        scatter_step([spatial_sum, reduce_sum], [by_pixel, proto_grad])
        grad_reduce = swap_columns(reduce_sum.finish())
        grad_spatial = swap_columns(spatial_sum.finish())
        total = expand_sum.finish()
        grad_expand = swap_columns(total[:, : D // 2])
        grad_project = jnp.concatenate(
            [total[:, k : k + proj] for k in range(D // 2, total.shape[1], proj)], 0
        )
    else:

        def scatter(first, kept, sent):
            lows = jnp.concatenate(
                [jnp.where(me_core == 0, kept, sent), jnp.where(me_core == 0, sent, kept)], 1
            )
            return lax.psum_scatter(
                product_t(first, lows), BOTH, scatter_dimension=0, tiled=True
            )

        grad_reduce = scatter(input_rows, one_kept, one_sent)
        grad_spatial = scatter(image_patches, two_kept, two_sent)
        grad_expand = scatter(act_two, three_kept, three_sent)
        grad_project = lax.psum_scatter(
            product_t(act_head, embed_low), BOTH, scatter_dimension=0, tiled=True
        )

    backs, _ = lax.optimization_barrier(((back_one, back_two, back_three, back_head), last))
    total_one, total_two, total_three, total_head = (jnp.sum(back, 0) for back in backs)
    narrow = jnp.concatenate(
        [
            jnp.stack([total_one[1], total_one[0], total_two[1, :MID], total_two[0, :MID]])
            .reshape(-1),
            jnp.stack([total_three[1], total_three[0], total_head[1], total_head[0]]).reshape(-1),
            total_two[0, MID:],
            jnp.broadcast_to(loss_part, (128,)),
        ]
    )
    narrow = narrow + swap_cores(narrow)
    mid_end, wide_end = norm_mid.size, norm_mid.size + norm_wide.size
    bias_end = wide_end + proj
    return (
        narrow[bias_end] * loss_factor_weight,
        by_pixel.transpose(0, 3, 1, 2, 4),
        grad_reduce,
        grad_spatial,
        grad_expand,
        grad_hidden,
        grad_project,
        narrow[:mid_end].reshape(norm_mid.shape),
        narrow[mid_end:wide_end].reshape(norm_wide.shape),
        narrow[wide_end:bias_end],
        proto_grad,
    )


def solution(mesh):
    return jax.shard_map(
        per_device,
        mesh=mesh,
        in_specs=(
            P(None, ("dp", "shard"), None, None, None),
            P(None, ("dp", "shard"), None),
            P(None, ("dp", "shard"), None),
            P(("dp", "shard"), None),
            P(("dp", "shard"), None),
            P(("dp", "shard"), None),
            P(("dp", "shard"), None),
            P(("dp", "shard"), None),
            P(("dp", "shard"), None),
            P(),
            P(),
            P(),
            P(),
        ),
        out_specs=(
            P(),
            P(None, ("dp", "shard"), None, None, None),
            P(("dp", "shard"), None),
            P(("dp", "shard"), None),
            P(("dp", "shard"), None),
            P(("dp", "shard"), None),
            P(("dp", "shard"), None),
            P(),
            P(),
            P(),
            P(),
        ),
        check_vma=False,
    )
```

```python
import dataclasses

import jax
import jax.numpy as jnp
import numpy as np
from jax import lax
from jax.experimental import pallas as pl
from jax.experimental.pallas import tpu as pltpu
from jax.sharding import PartitionSpec as P

D = 2048
MID = 512
PROTOS = 3000
SIDE = 6
CROPS = 4
SINK_ITERS = 3
MICRO = 2


EPS_NORM = 1e-05
EPS_UNIT = 1e-06
SOFTMAX_HEAT = 0.1
SINK_EPS = 0.05
HIGH = lax.Precision.HIGHEST
BOTH = ("dp", "shard")
GATHERED_CODES_BYTES = 32 * 2**20
MIB = 2**20
LANES = 512
CHUNKS = 4


def product(left, right):
    return jnp.dot(left, right, preferred_element_type=jnp.float32)


def product_t(left, right):
    return lax.dot_general(
        left, right, (((0,), (0,)), ((), ())), preferred_element_type=jnp.float32
    )


def product_bt(left, right):
    return lax.dot_general(
        left, right, (((1,), (1,)), ((), ())), preferred_element_type=jnp.float32
    )


def silu_slope(values):
    sigmoid_value = jax.nn.sigmoid(values)
    return sigmoid_value * (1.0 + values * (1.0 - sigmoid_value))


@dataclasses.dataclass
class Scalars:
    array: jax.Array


@dataclasses.dataclass
class Left:
    array: jax.Array


@dataclasses.dataclass
class Loaded:
    array: jax.Array


@dataclasses.dataclass
class Streamed:
    array: jax.Array


class Arriving:
    def __init__(self, ref, copy):
        self.ref, self.copy = ref, copy
        self.shape = ref.shape

    def __getitem__(self, index):
        if self.copy is not None:
            self.copy.wait()
            self.copy = None
        return self.ref[index]


FAR, PUT_FAR = "far", "put far"


def kernel_call(body, outs, args, scratch=(), flops=0, transcendentals=0, limit=17, after=()):
    spaces = {Scalars: pltpu.SMEM, Left: pltpu.HBM, Streamed: pltpu.HBM}
    in_spaces = [spaces.get(type(a), pltpu.VMEM) for a in args] + [pl.ANY] * len(after)
    arrays = []
    for a in args:
        if isinstance(a, (Left, Loaded, Streamed)):
            a = pltpu.with_memory_space_constraint(a.array, pltpu.HBM)
        arrays.append(a.array if isinstance(a, Scalars) else a)
    used = len(arrays)
    out_spaces = [pltpu.HBM if FAR in out else pltpu.VMEM for out in outs]

    streamed = [i for i, a in enumerate(args) if isinstance(a, Streamed)]
    scratch = list(scratch)
    own_scratch = len(scratch)
    for i in streamed:
        scratch += [pltpu.VMEM(arrays[i].shape, arrays[i].dtype), pltpu.SemaphoreType.DMA]

    def kernel(*refs):
        inputs, refs = list(refs[:used]), refs[used + len(after) :]
        mine = len(outs) + own_scratch
        for k, i in enumerate(streamed):
            buffer, sem = refs[mine + 2 * k : mine + 2 * k + 2]
            copy = pltpu.make_async_copy(inputs[i], buffer, sem)
            copy.start()
            inputs[i] = Arriving(buffer, copy)
        body(*inputs, *refs[:mine])

    moved = sum(a.size * a.dtype.itemsize for a in arrays)
    return pl.pallas_call(
        kernel,
        out_shape=[
            jax.ShapeDtypeStruct(*out) if len(out) == 2 else pltpu.HBM(*out[:2]) for out in outs
        ],
        in_specs=[pl.BlockSpec(memory_space=space) for space in in_spaces],
        out_specs=[pl.BlockSpec(memory_space=space) for space in out_spaces],
        scratch_shapes=list(scratch),
        compiler_params=pltpu.CompilerParams(vmem_limit_bytes=limit * MIB),
        cost_estimate=pl.CostEstimate(
            flops=int(flops), bytes_accessed=int(moved), transcendentals=int(transcendentals)
        ),
    )(*arrays, *after)


def join_kernel(counts, *refs):
    outs = refs[sum(counts) :]
    start = 0
    for count, joined in zip(counts, outs):
        parts = refs[start : start + count]
        start += count
        length = parts[0].shape[0]

        def move(i, carry):
            for k, part in enumerate(parts):
                joined[i + k * length] = part[i]
            return carry

        lax.fori_loop(0, length, move, 0)


def join(groups, after=()):
    counts = [len(group) for group in groups]
    outs = [
        ((len(group) * group[0].shape[0],) + group[0].shape[1:], group[0].dtype)
        for group in groups
    ]
    return kernel_call(
        lambda *refs: join_kernel(counts, *refs),
        outs,
        [part for group in groups for part in group],
        after=after,
    )


def hold_kernel(source, target):
    target[...] = source[...]


def hold(values, after=()):
    return kernel_call(hold_kernel, [(values.shape, values.dtype)], [values], after=after)[0]


def add_parts_kernel(kept, received, *totals):
    length = totals[0].shape[0]

    def move(i, carry):
        for k, out_ref in enumerate(totals):
            place = i + k * length
            total = kept[place].astype(jnp.float32) + received[place].astype(jnp.float32)
            out_ref[i] = total.astype(out_ref.dtype)
        return carry

    lax.fori_loop(0, length, move, 0)


def add_parts(kept, received, count, after=()):
    shape = (kept.shape[0] // count,) + kept.shape[1:]
    kept, *sent = kernel_call(
        add_parts_kernel,
        [(shape, jnp.float32, PUT_FAR)] + [(shape, jnp.bfloat16, PUT_FAR)] * (count - 1),
        [Loaded(kept), Loaded(received)],
        after=after,
    )
    return kept, sent


def swap_cores(values):
    return lax.ppermute(values, "shard", [(0, 1), (1, 0)])


def flip_dp(values, bits, size):
    return lax.ppermute(values, "dp", [(i, i ^ bits) for i in range(size)])


def flip_both(values, dp_bits, size):
    pairs = [(2 * i + c, 2 * (i ^ dp_bits[c]) + c) for i in range(size) for c in range(2)]
    return lax.ppermute(values, BOTH, pairs)


def copies_of(size):
    return size if size <= STEPS_DP else 1


def terms_over_dp(copies):
    if copies.shape[0] > 1:
        return lax.all_to_all(copies, "dp", 0, 0)
    return lax.psum(copies, "dp")


Z_BITS = (8, 4, 12)
XY_BITS = ((1, 2), (2, 1))
STEPS_DP = 16


def relative_slots(size):
    me_dp, me_core = lax.axis_index("dp"), lax.axis_index("shard")
    device = jnp.arange(2 * size, dtype=jnp.int32)
    apart_dp, apart_core = (device // 2) ^ me_dp, (device % 2) ^ me_core
    holder = device % 2
    on = lambda bit: jnp.where((apart_dp & bit) != 0, 1, 0)
    low, high = (jnp.where(holder == 0, on(zero), on(one)) for zero, one in XY_BITS)
    slot = on(Z_BITS[0]) + 2 * on(Z_BITS[1]) + 4 * low + 8 * high + size * apart_core
    return slot.astype(jnp.int32)


class Gathering:
    def __init__(self, shard, size):
        self.size = size
        self.held = shard[None]
        self.step = 0

    def send(self):
        step, held = self.step, self.held
        self.step += 1
        if step == 0:
            return [held] + [flip_dp(held, bits, self.size) for bits in Z_BITS]
        return [held, flip_both(held, XY_BITS[step - 1], self.size)]

    def finish(self, slots):
        return Gathered(self.held, swap_cores(self.held), slots)


def gather_step(parts, after=()):
    joined = join([part.send() for part in parts], after)
    for part, held in zip(parts, joined):
        part.held = held


def other_core_dp(held, size):
    device = jnp.arange(2 * size, dtype=jnp.int32)
    other = (device % 2) != lax.axis_index("shard")
    slots = jnp.where(other, size, 0) + device // 2
    return Gathered(held, swap_cores(held), slots.astype(jnp.int32))


class Scattering:
    def __init__(self, kept, sent, size, before):
        self.size = size
        self.kept = kept
        sent, _ = lax.optimization_barrier((sent, before))
        self.received = flip_both(sent, XY_BITS[1], size)

    def second(self, after=()):
        self.kept, sent = add_parts(self.kept, self.received, 2, after)
        self.received = flip_both(sent[0], XY_BITS[0], self.size)

    def third(self, after=()):
        self.kept, sent = add_parts(self.kept, self.received, 4, after)
        self.received = [flip_dp(part, bits, self.size) for part, bits in zip(sent, Z_BITS)]

    def finish(self):
        one, two, three = (part[0].astype(jnp.float32) for part in self.received)
        return (self.kept[0] + one) + (two + three)


@dataclasses.dataclass
class Gathered:
    held: jax.Array
    other: jax.Array | None = None
    slots: jax.Array | None = None

    @property
    def count(self):
        return 1 if self.other is None else 3

    @property
    def shape(self):
        if self.other is None:
            return self.held.shape
        half, rows, width = self.held.shape
        return (2 * half * rows, width)

    def inputs(self):
        if self.other is None:
            return [Left(self.held)]
        return [Scalars(self.slots), Left(self.held), Left(self.other)]

    def scratch(self, chunks=1):
        copies = chunks if self.other is None else 2 * self.held.shape[0]
        return [pltpu.VMEM(self.shape, jnp.bfloat16), pltpu.SemaphoreType.DMA((copies,))]


def fetch_weight(inputs, weight, sems, chunks=1):
    count = sems.shape[0]
    rows = weight.shape[0] // count
    each = count // chunks

    def copy(source, i):
        target = weight.at[pl.ds(pl.multiple_of(i * rows, rows), rows)]
        return pltpu.make_async_copy(source, target, sems.at[i])

    if len(inputs) == 1:
        copies = [copy(inputs[0].at[pl.ds(i * rows, rows)], i) for i in range(count)]
        for one in copies:
            one.start()

        def wait_ordered(chunk):
            for one in copies[chunk * each : (chunk + 1) * each]:
                one.wait()

        return wait_ordered

    table, held, other = inputs
    half = held.shape[0]

    def begin(i, carry):
        slot = table[i]

        @pl.when(slot < half)
        def _():
            copy(held.at[slot], i).start()

        @pl.when(slot >= half)
        def _():
            copy(other.at[slot - half], i).start()

        return carry

    lax.fori_loop(0, count, begin, 0)

    def wait(chunk):
        def finish(i, carry):
            copy(held.at[0], i).wait()
            return carry

        lax.fori_loop(chunk * each, (chunk + 1) * each, finish, 0)

    return wait


def weight_grad_kernel(beside, table, *refs):
    left, left_peer, right, right_peer = refs[:4]
    if beside:
        second, second_peer, second_right, second_right_peer, core = refs[4:9]
        kept_ref, sent_ref, total_ref, second_ref = refs[9:]
    else:
        kept_ref, sent_ref, total_ref = refs[4:]
    half, rows, _ = kept_ref.shape
    width = right.shape[1]
    for k in range(0, total_ref.shape[0], 512):
        total_ref[k : k + 512, :] = product_t(left[:, k : k + 512], right[...]) + product_t(
            left_peer[:, k : k + 512], right_peer[...]
        )
    if beside:
        second_ref[...] = product_t(second[...], second_right[...]) + product_t(
            second_peer[...], second_right_peer[...]
        )

    def place(out_ref, slot, i):
        found = total_ref[pl.ds(pl.multiple_of(i * rows, rows), rows), :]
        out_ref[slot, :, :width] = found.astype(out_ref.dtype)
        for part in range(beside):
            start = ((2 * i + core[0]) * beside + part) * rows
            across = second_ref.shape[1]
            columns = slice(width + part * across, width + (part + 1) * across)
            found = second_ref[pl.ds(pl.multiple_of(start, rows), rows), :]
            out_ref[slot, :, columns] = found.astype(out_ref.dtype)

    def move(i, carry):
        slot = table[i]

        @pl.when(slot < half)
        def _():
            place(kept_ref, slot, i)

        @pl.when(slot >= half)
        def _():
            place(sent_ref, slot - half, i)

        return carry

    lax.fori_loop(0, 2 * half, move, 0)


def weight_grad(left, right, slots, size, before, second=None, after=()):
    depth, width = left[0].shape[1], right[0].shape[1]
    rows = depth // size
    args = [Scalars(slots), *left, *right]
    scratch, beside, extra = [pltpu.VMEM((depth, width), jnp.float32)], 0, 0
    if second is not None:
        (second_left, second_right, core) = second
        args += [*second_left, *second_right, core]
        second_shape = (second_left[0].shape[1], second_right[0].shape[1])
        beside = second_shape[0] // (2 * depth)
        extra = beside * second_shape[1]
        scratch.append(pltpu.VMEM(second_shape, jnp.float32))
    shape = (size // 2, rows, width + extra)
    kept, sent = kernel_call(
        lambda *refs: weight_grad_kernel(beside, *refs),
        [(shape, jnp.float32, PUT_FAR), (shape, jnp.bfloat16, PUT_FAR)],
        args,
        scratch=scratch,
        flops=4 * left[0].shape[0] * depth * width,
        after=after,
    )
    return Scattering(kept, sent, size, before)


def swap_columns(*totals):
    me = lax.axis_index("shard")

    def half_of(core):
        halves = [total.shape[0] // 2 for total in totals]
        return jnp.concatenate(
            [
                lax.dynamic_slice_in_dim(total, core * half, half, 0)
                for total, half in zip(totals, halves)
            ]
        )

    mine, other = half_of(me), swap_cores(half_of(1 - me))
    first, second = jnp.where(me == 0, mine, other), jnp.where(me == 0, other, mine)
    both, found, start = jnp.concatenate([first, second], 1), [], 0
    for total in totals:
        found.append(both[start : start + total.shape[0] // 2])
        start += total.shape[0] // 2
    return found


def tiles(rows, width, high, wide):
    for r in range(0, rows, high):
        for k in range(0, width, wide):
            yield slice(r, r + high), slice(k, k + wide)


def norm_factors(terms, norm_ref, row, count):
    totals = jnp.sum(terms[...], 0)
    average = totals[0:1] / count
    inverse = lax.rsqrt(totals[1:2] / count - average * average + EPS_NORM)
    return average, inverse, norm_ref[row : row + 1, :], norm_ref[row + 1 : row + 2, :]


def normalize(values, factors, columns):
    average, inverse, gain, shift = (part[:, columns] for part in factors)
    unit = (values - average) * inverse
    return unit, gain * unit + shift


def silu(values):
    return values * jax.nn.sigmoid(values)


def norm_backward(grad, unit, factors, totals, count, columns):
    _, inverse, gain, _ = (part[:, columns] for part in factors)
    mean_grad = totals[0:1, columns] / count
    mean_product = totals[1:2, columns] / count
    return gain * inverse * (grad - mean_grad - unit * mean_product)


class Sums:
    def __init__(self, out_ref):
        self.out_ref = out_ref
        self.parts = {}

    def add(self, columns, first, second):
        key = (columns.start, columns.stop)
        fold = lambda v: jnp.sum(v.reshape(v.shape[0] // 8, 8, v.shape[1]), 0)
        first, second = fold(first), fold(second)
        if key in self.parts:
            first, second = self.parts[key][0] + first, self.parts[key][1] + second
        self.parts[key] = (first, second)

    def store(self):
        for (start, stop), (first, second) in self.parts.items():
            first = jnp.sum(first, 0, keepdims=True)
            second = jnp.sum(second, 0, keepdims=True)
            for copy in range(self.out_ref.shape[0]):
                self.out_ref[copy, 0:1, start:stop] = first
                self.out_ref[copy, 1:2, start:stop] = second


def reduce_kernel(weights, x_ref, *refs):
    inputs, refs = refs[:weights], refs[weights:]
    pre_ref, sums_ref, weight_out, weight, sems, out_sem = refs
    fetch_weight(inputs, weight, sems)(0)
    copy_out = pltpu.make_async_copy(weight, weight_out, out_sem)
    copy_out.start()
    sums = Sums(sums_ref)
    for columns in (slice(k, k + 256) for k in range(0, MID, 256)):
        pre = product(x_ref[...], weight[:, columns])
        pre_ref[:, columns] = pre
        sums.add(columns, pre, pre * pre)
    sums.store()
    copy_out.wait()


def spatial_kernel(weights, count, pre_ref, norm_ref, valid_ref, *refs):
    term_refs, *refs = refs
    inputs, refs = refs[:weights], refs[weights:]
    out_ref, sums_ref, patches_out, weight_out, padded, patches, sem, weight, sems, out_sem = refs
    wait = fetch_weight(inputs, weight, sems)
    rows = pre_ref.shape[0]
    factors = norm_factors(term_refs, norm_ref, 0, count)
    edge = jnp.zeros((EDGE, MID), jnp.float32)
    padded[0:EDGE, :] = edge
    padded[EDGE + rows :, :] = edge
    for high, columns in tiles(rows, MID, 48, 512):
        _, shifted = normalize(pre_ref[high, columns], factors, columns)
        low = silu(shifted).astype(jnp.bfloat16)
        padded[EDGE + high.start : EDGE + high.stop, columns] = low.astype(jnp.float32)
    for place in range(9):
        offset = EDGE + neighbour(place, rows // (2 * SIDE * SIDE))
        for high, columns in tiles(rows, MID, 48, 512):
            values = padded[offset + high.start : offset + high.stop, columns]
            values = values * valid_ref[high, place : place + 1]
            patches[high, place * MID : (place + 1) * MID] = values.astype(jnp.bfloat16)
    copy = pltpu.make_async_copy(patches, patches_out, sem)
    copy.start()
    wait(0)
    copy_out = pltpu.make_async_copy(weight, weight_out, out_sem)
    copy_out.start()
    sums = Sums(sums_ref)
    for columns in (slice(k, k + 256) for k in range(0, MID, 256)):
        pre = product(patches[...], weight[:, columns])
        out_ref[:, columns] = pre
        sums.add(columns, pre, pre * pre)
    sums.store()
    copy.wait()
    copy_out.wait()


def expand_kernel(weights, count, pre_ref, norm_ref, *refs):
    term_refs, *refs = refs
    inputs, refs = refs[:weights], refs[weights:]
    act_ref, out_ref, sums_ref, weight_out, side_ref, weight, sems, out_sem = refs
    wait = fetch_weight(inputs, weight, sems)
    factors = norm_factors(term_refs, norm_ref, 2, count)
    for high, columns in tiles(pre_ref.shape[0], MID, 48, 512):
        _, shifted = normalize(pre_ref[high, columns], factors, columns)
        act_ref[high, columns] = silu(shifted).astype(jnp.bfloat16)
    wait(0)
    copy_out = pltpu.make_async_copy(weight, weight_out, out_sem)
    copy_out.start()
    if weight.shape[1] > D:
        side_ref[...] = weight[:, D:]
    else:
        side_ref[...] = jnp.zeros_like(side_ref)
    sums = Sums(sums_ref)
    for columns in (slice(k, k + 256) for k in range(0, D, 256)):
        pre = product(act_ref[...], weight[:, columns])
        out_ref[:, columns] = pre
        sums.add(columns, pre, pre * pre)
    sums.store()
    copy_out.wait()


def split(values):
    high = values.astype(jnp.bfloat16)
    return high, (values - high.astype(jnp.float32)).astype(jnp.bfloat16)


def pool_kernel(weights, count, pre_ref, x_ref, norm_ref, pool_ref, size_ref, *refs):
    term_refs, *refs = refs
    inputs, refs = refs[:weights], refs[weights:]
    pooled_ref, out_ref, sums_ref, project_ref, high_ref, rest_ref, weight, sems = refs
    wait = fetch_weight(inputs, weight, sems, CHUNKS)
    factors = norm_factors(term_refs, norm_ref, 0, count)
    rows = pre_ref.shape[0]
    for k in range(0, D, 256):
        for high, columns in tiles(rows, 256, 96, 256):
            across = slice(k + columns.start, k + columns.stop)
            _, shifted = normalize(pre_ref[high, across], factors, across)
            block = silu(shifted + x_ref[high, across].astype(jnp.float32))
            high_ref[high, columns], rest_ref[high, columns] = split(block)
        pooled = product(pool_ref[...], high_ref[...]) + product(pool_ref[...], rest_ref[...])
        pooled_ref[:, k : k + 256] = (pooled / size_ref[...]).astype(jnp.bfloat16)
    step = D // CHUNKS
    total = 0.0
    for chunk in range(CHUNKS):
        wait(chunk)
        part = slice(chunk * step, (chunk + 1) * step)
        total = total + product(pooled_ref[:, part], weight[part, :D])
    out_ref[...] = total
    project_ref[...] = weight[:, D:]
    sums = Sums(sums_ref)
    for columns in (slice(k, k + 512) for k in range(0, D, 512)):
        pre = out_ref[:, columns]
        sums.add(columns, pre, pre * pre)
    sums.store()


def embed_kernel(count, pre_ref, norm_ref, project_ref, bias_ref, *refs):
    term_refs, *refs = refs
    act_ref, unit_ref, inverse_ref, low_ref = refs
    factors = norm_factors(term_refs, norm_ref, 2, count)
    for high, columns in tiles(pre_ref.shape[0], D, pre_ref.shape[0], 512):
        _, shifted = normalize(pre_ref[high, columns], factors, columns)
        act_ref[high, columns] = silu(shifted).astype(jnp.bfloat16)
    embed = product(act_ref[...], project_ref[...]) + bias_ref[...]
    inverse = lax.rsqrt(jnp.sum(embed * embed, 1, keepdims=True) + EPS_UNIT)
    unit = embed * inverse
    unit_ref[...] = unit
    inverse_ref[...] = jnp.broadcast_to(inverse, inverse_ref.shape)
    low_ref[...] = jnp.broadcast_to(unit.astype(jnp.bfloat16)[None], low_ref.shape)


def embed_back_kernel(
    count, grad_ref, unit_ref, inverse_ref, project_ref, pre_ref, norm_ref, *refs
):
    term_refs, *refs = refs
    low_ref, out_ref, sums_ref, bias_ref = refs
    grad, unit = grad_ref[...], unit_ref[...]
    embed_grad = inverse_ref[...] * (grad - unit * jnp.sum(grad * unit, 1, keepdims=True))
    low_ref[...] = embed_grad.astype(jnp.bfloat16)
    bias_ref[...] = jnp.sum(embed_grad, 0, keepdims=True)
    factors = norm_factors(term_refs, norm_ref, 2, count)
    sums = Sums(sums_ref)
    for columns in (slice(k, k + 512) for k in range(0, D, 512)):
        back = product_bt(low_ref[...], project_ref[columns, :])
        head_unit, shifted = normalize(pre_ref[:, columns], factors, columns)
        back = back * silu_slope(shifted)
        out_ref[:, columns] = back
        sums.add(columns, back, back * head_unit)
    sums.store()


def pool_back_kernel(
    weights,
    crop_count,
    count,
    grad_ref,
    head_pre_ref,
    pre_ref,
    x_ref,
    norm_ref,
    spread_ref,
    size_ref,
    *refs,
):
    head_terms, head_back, pre_terms, *refs = refs
    inputs, refs = refs[:weights], refs[weights:]
    low_ref, own_ref, other_ref, sums_ref, total_ref, weight, sems = refs
    wait = fetch_weight(inputs, weight, sems, CHUNKS)
    step = D // CHUNKS
    head_factors = norm_factors(head_terms, norm_ref, 2, crop_count)
    totals = jnp.sum(head_back[...], 0)
    total_ref[...] = totals
    for columns in (slice(k, k + 512) for k in range(0, D, 512)):
        unit, _ = normalize(head_pre_ref[:, columns], head_factors, columns)
        grad = norm_backward(
            grad_ref[:, columns], unit, head_factors, totals, crop_count, columns
        )
        low_ref[:, columns] = grad.astype(jnp.bfloat16)
    factors = norm_factors(pre_terms, norm_ref, 0, count)
    sums = Sums(sums_ref)
    own_rows = own_ref.shape[0]
    for chunk in range(CHUNKS):
        wait(chunk)
        part = slice(chunk * step, (chunk + 1) * step)
        pooled = product_bt(low_ref[...], weight[part, :D]) / size_ref[...]
        high_part, rest_part = split(pooled)
        for rows, columns in tiles(2 * own_rows, part.stop - part.start, 48, 256):
            across = slice(part.start + columns.start, part.start + columns.stop)
            spread = spread_ref[rows, :]
            out_grad = product(spread, high_part[:, columns]) + product(
                spread, rest_part[:, columns]
            )
            unit, shifted = normalize(pre_ref[rows, across], factors, across)
            joined = shifted + x_ref[rows, across].astype(jnp.float32)
            joined_grad = out_grad * silu_slope(joined)
            if rows.start < own_rows:
                own_ref[rows, across] = joined_grad
            else:
                other_ref[rows.start - own_rows : rows.stop - own_rows, across] = joined_grad
            sums.add(across, joined_grad, joined_grad * unit)
    sums.store()


def column_halves(low_ref, core, kept_ref, sent_ref):
    half = kept_ref.shape[1]
    for out_ref, which in ((kept_ref, core[0]), (sent_ref, 1 - core[0])):
        out_ref[...] = low_ref[:, pl.ds(pl.multiple_of(which * half, half), half)]


def expand_back_kernel(
    count, core, own_ref, other_ref, pre_ref, wide_ref, weight_ref, before_ref, mid_ref, bias_ref, *refs
):
    pre_terms, back_terms, before_terms, *refs = refs
    kept_ref, sent_ref, out_ref, sums_ref, total_ref, low_ref = refs
    factors = norm_factors(pre_terms, wide_ref, 0, count)
    totals = jnp.sum(back_terms[...], 0)
    total_ref[...] = totals
    own_rows = own_ref.shape[0]
    for rows, columns in tiles(2 * own_rows, D, 48, 512):
        unit, _ = normalize(pre_ref[rows, columns], factors, columns)
        if rows.start < own_rows:
            grad = own_ref[rows, columns]
        else:
            grad = other_ref[rows.start - own_rows : rows.stop - own_rows, columns]
        grad = norm_backward(grad, unit, factors, totals, count, columns)
        low_ref[rows, columns] = grad.astype(jnp.bfloat16)
    column_halves(low_ref, core, kept_ref, sent_ref)
    factors = norm_factors(before_terms, mid_ref, 2, count)
    sums = Sums(sums_ref)
    for columns in (slice(k, k + 256) for k in range(0, MID, 256)):
        back = product_bt(low_ref[...], weight_ref[columns, :D])
        unit, shifted = normalize(before_ref[:, columns], factors, columns)
        back = back * silu_slope(shifted)
        out_ref[:, columns] = back
        sums.add(columns, back, back * unit)
    sums.store()
    bias = jnp.concatenate([bias_ref[...], jnp.zeros_like(bias_ref)], 0)
    for copy in range(sums_ref.shape[0]):
        sums_ref[copy, :, MID:] = bias


def spatial_back_kernel(
    count, core, grad_ref, pre_ref, norm_ref, weight_ref, before_ref, valid_ref, *refs
):
    pre_terms, back_terms, before_terms, *refs = refs
    kept_ref, sent_ref, out_ref, sums_ref, total_ref, slots, low_ref = refs
    rows = grad_ref.shape[0]
    factors = norm_factors(pre_terms, norm_ref, 2, count)
    totals = jnp.sum(back_terms[...], 0)
    total_ref[...] = totals
    for high, columns in tiles(rows, MID, 48, 512):
        unit, _ = normalize(pre_ref[high, columns], factors, columns)
        grad = norm_backward(grad_ref[high, columns], unit, factors, totals, count, columns)
        low_ref[high, columns] = grad.astype(jnp.bfloat16)
    column_halves(low_ref, core, kept_ref, sent_ref)
    edge = jnp.zeros((EDGE, MID), jnp.float32)
    for place in range(9):
        slots[place, 0:EDGE, :] = edge
        slots[place, EDGE + rows :, :] = edge
        for columns in (slice(k, k + 256) for k in range(0, MID, 256)):
            patch = product_bt(
                low_ref[...],
                weight_ref[place * MID + columns.start : place * MID + columns.stop, :],
            )
            slots[place, EDGE : EDGE + rows, columns] = patch * valid_ref[:, place : place + 1]
    factors = norm_factors(before_terms, norm_ref, 0, count)
    sums = Sums(sums_ref)
    for high, columns in tiles(rows, MID, 48, 256):
        back = 0.0
        for place in range(9):
            start = EDGE - neighbour(place, rows // (2 * SIDE * SIDE)) + high.start
            back = back + slots[place, start : start + high.stop - high.start, columns]
        unit, shifted = normalize(before_ref[high, columns], factors, columns)
        back = back * silu_slope(shifted)
        out_ref[high, columns] = back
        sums.add(columns, back, back * unit)
    sums.store()


def reduce_back_kernel(
    count,
    core,
    grad_ref,
    pre_ref,
    norm_ref,
    pre_terms,
    back_terms,
    low_ref,
    other_ref,
    kept_ref,
    sent_ref,
    total_ref,
):
    rows = grad_ref.shape[0]
    factors = norm_factors(pre_terms, norm_ref, 0, count)
    totals = jnp.sum(back_terms[...], 0)
    total_ref[...] = totals
    for high, columns in tiles(rows, MID, 48, 512):
        unit, _ = normalize(pre_ref[high, columns], factors, columns)
        grad = norm_backward(grad_ref[high, columns], unit, factors, totals, count, columns)
        low_ref[high, columns] = grad.astype(jnp.bfloat16)
    other_ref[...] = low_ref[rows // 2 :, :]
    column_halves(low_ref, core, kept_ref, sent_ref)


def arrange_kernel(core, canvases_ref, own_ref, other_ref, rows_ref):
    _, _, _, canvas_count, _ = canvases_ref.shape
    for which, out_ref in enumerate((own_ref, other_ref)):
        micro = core[0] if which == 0 else 1 - core[0]
        for pixel in range(SIDE * SIDE):
            rows = slice(pixel * canvas_count, (pixel + 1) * canvas_count)
            values = canvases_ref[micro, pixel // SIDE, pixel % SIDE]
            rows_ref[rows, :] = values.astype(jnp.float32)
        out_ref[...] = rows_ref[...].astype(jnp.bfloat16)


def input_grad_kernel(
    core, own_ref, other_ref, low_ref, other_low_ref, weight_ref, out_ref, rows_ref
):
    own_rows = own_ref.shape[0]
    canvas_count = out_ref.shape[3]
    for which in range(2):
        micro = core[0] if which == 0 else 1 - core[0]
        grad_ref = own_ref if which == 0 else other_ref
        low = low_ref[:own_rows, :] if which == 0 else other_low_ref[...]
        for columns in (slice(k, k + 512) for k in range(0, D, 512)):
            rows_ref[:, columns] = grad_ref[:, columns] + product_bt(low, weight_ref[columns, :])
        for pixel in range(SIDE * SIDE):
            rows = slice(pixel * canvas_count, (pixel + 1) * canvas_count)
            out_ref[micro, pixel // SIDE, pixel % SIDE] = rows_ref[rows, :]


def proto_grad_kernel(first_ref, second_ref, out_ref):
    rows = out_ref.shape[0]
    for k in range(0, rows, 128):
        stop = min(k + 128, rows)
        total = first_ref[:, k : k + 128] + second_ref[:, k : k + 128]
        out_ref[k:stop, :] = total.T[: stop - k, :]


def inside_canvas(own_canvases):
    valid = np.zeros((2, SIDE, SIDE, own_canvases, 16), np.float32)
    for place in range(9):
        down, right = place // 3 - 1, place % 3 - 1
        for y in range(SIDE):
            for x in range(SIDE):
                valid[:, y, x, :, place] = 0 <= y + down < SIDE and 0 <= x + right < SIDE
    return jnp.asarray(valid.reshape(-1, 16))


def neighbour(place, own_canvases):
    return ((place // 3 - 1) * SIDE + place % 3 - 1) * own_canvases


EDGE = 32


def add_columns(total_ref, columns, values):
    rows, width = values.shape
    total_ref[:, columns] += jnp.sum(values.reshape(rows // 8, 8, width), 0)


def codes_kernel(
    crops,
    device_crops,
    place,
    units_ref,
    side_ref,
    prototypes_ref,
    loss_ref,
    proto_grad_ref,
    unit_grad_ref,
    proto_ref,
    partner_ref,
    codes_ref,
    heat_ref,
    score_ref,
    total_ref,
    scale_ref,
    inverse_ref,
    *,
    factor,
):
    rows_all, width = codes_ref.shape
    own = unit_grad_ref.shape[0]
    chunks = [slice(k, k + LANES) for k in range(0, width, LANES)]
    real = lax.broadcasted_iota(jnp.int32, (1, width), 1) < PROTOS

    dim = units_ref.shape[1]
    proto_ref[PROTOS // 16 * 16 :, :] = jnp.zeros((width - PROTOS // 16 * 16, dim), jnp.bfloat16)
    proto_ref[:PROTOS, :] = prototypes_ref[...]

    queue_rows = side_ref.shape[0]
    device_rows = queue_rows // (crops // device_crops)
    crop = lax.broadcasted_iota(jnp.int32, (crops, queue_rows), 0)
    holder = crop // device_crops ^ place[1]
    row = lax.broadcasted_iota(jnp.int32, (crops, queue_rows), 1)
    holds = (row == holder * device_rows).astype(jnp.bfloat16)
    found = product(holds, side_ref[:, dim:])
    crop = lax.broadcasted_iota(jnp.int32, found.shape, 0)
    lane = lax.broadcasted_iota(jnp.int32, found.shape, 1)
    here = lane == place[1] * device_crops + crop % device_crops
    partner = jnp.sum(jnp.where(here, found, 0.0), 1, keepdims=True)
    partner_ref[...] = partner.astype(jnp.int32)

    def scores(rows, columns, queue=False):
        left = side_ref[rows, :dim] if queue else units_ref[rows, :]
        return product_bt(left, proto_ref[columns, :])

    def keep(values, columns):
        if columns.stop <= PROTOS:
            return values
        lanes = columns.start + lax.broadcasted_iota(jnp.int32, values.shape, 1)
        return jnp.where(lanes < PROTOS, values, 0.0)

    def fold(values):
        return sum(values[:, k : k + 128] for k in range(0, values.shape[1], 128))

    total_ref[...] = jnp.zeros_like(total_ref)

    for queue, start, count in ((False, 0, crops), (True, crops, queue_rows)):

        def first(i, carry):
            rows = pl.ds(pl.multiple_of(i * 128, 128), 128)
            target = pl.ds(pl.multiple_of(start + i * 128, 128), 128)
            for columns in chunks:
                score = scores(rows, columns, queue)
                powers = keep(jnp.exp(score * (1.0 / SINK_EPS)), columns)
                codes_ref[target, columns] = powers
                add_columns(total_ref, columns, powers)
            return carry

        lax.fori_loop(0, count // 128, first, 0)

    def column_factors(turn):
        total = jnp.sum(total_ref[...], 0, keepdims=True)
        total = jnp.where(real, total, 1.0)
        if turn == 0:
            scale = jnp.where(total > 1e30, 2.0**-64, 1.0)
            scale_ref[...] = jnp.broadcast_to(scale, scale_ref.shape)
            total = total * scale
        inverse_ref[...] = jnp.broadcast_to(1.0 / total, inverse_ref.shape)

    def divided(turn, rows, columns):
        values = codes_ref[rows, columns]
        if turn == 0:
            values = values * scale_ref[0:1, columns]
        return values * inverse_ref[0:1, columns]

    def row_inverse(turn, rows):
        part = sum(fold(divided(turn, rows, columns)) for columns in chunks)
        return 1.0 / jnp.sum(part, 1, keepdims=True)

    for turn in range(SINK_ITERS - 1):
        column_factors(turn)
        total_ref[...] = jnp.zeros_like(total_ref)

        def both(i, carry):
            rows = pl.ds(pl.multiple_of(i * 64, 64), 64)
            inverse = row_inverse(turn, rows)
            for columns in chunks:
                values = divided(turn, rows, columns) * inverse
                codes_ref[rows, columns] = values
                add_columns(total_ref, columns, values)
            return carry

        lax.fori_loop(0, rows_all // 64, both, 0)

    column_factors(SINK_ITERS - 1)
    loss_ref[...] = jnp.zeros_like(loss_ref)
    block = 128

    def last(i, carry):
        rows = pl.ds(pl.multiple_of(i * block, block), block)
        inverse = row_inverse(SINK_ITERS - 1, rows)
        row = lax.broadcasted_iota(jnp.int32, (block, block), 0)
        column = lax.broadcasted_iota(jnp.int32, (block, block), 1)
        pick = (column == (row // CROPS) * CROPS + partner_ref[rows, :]).astype(jnp.bfloat16)
        pick = jnp.concatenate([pick, pick], 1)
        heat_part = jnp.zeros((block, 128), jnp.float32)
        target_part = jnp.zeros((block, 128), jnp.float32)
        loss_part = jnp.zeros((block, 128), jnp.float32)
        for columns in chunks:
            score = scores(rows, columns)
            heat = keep(jnp.exp(score * (1.0 / SOFTMAX_HEAT)), columns)
            heat_ref[:, columns] = heat
            heat_part += fold(heat)
            codes = divided(SINK_ITERS - 1, rows, columns) * inverse
            high = codes.astype(jnp.bfloat16)
            rest = (codes - high.astype(jnp.float32)).astype(jnp.bfloat16)
            target = product(pick, jnp.concatenate([high, rest], 0))
            codes_ref[rows, columns] = target
            target_part += fold(target)
            loss_part += fold(target * score)
        heat_sum = jnp.sum(heat_part, 1, keepdims=True)
        target_sum = jnp.sum(target_part, 1, keepdims=True)
        row_loss = (
            target_sum * jnp.log(heat_sum)
            - jnp.sum(loss_part, 1, keepdims=True) * (1.0 / SOFTMAX_HEAT)
        )
        loss_ref[...] += jnp.broadcast_to(jnp.sum(row_loss, 0, keepdims=True), loss_ref.shape)
        ratio = target_sum / heat_sum * factor
        for columns in chunks:
            grad = heat_ref[:, columns] * ratio - codes_ref[rows, columns] * factor
            score_ref[rows, columns] = grad.astype(jnp.bfloat16)
        return carry

    lax.fori_loop(0, crops // block, last, 0)
    for columns in chunks:
        proto_grad_ref[:, columns] = product_t(units_ref[...], score_ref[:, columns])
    mine = pl.ds(pl.multiple_of(place[0], own), own)
    unit_grad_ref[...] = product(score_ref[mine, :], proto_ref[...])


def gathered_loss(units, side, prototypes, place, own, device_crops, loss_factor_weight):
    crops, dim = units.shape
    width = -(-PROTOS // LANES) * LANES
    rows_all = crops + side.shape[0]
    f32, bf16 = jnp.float32, jnp.bfloat16
    loss, proto_grad, unit_grad = kernel_call(
        lambda *refs: codes_kernel(
            crops, device_crops, *refs, factor=loss_factor_weight / SOFTMAX_HEAT
        ),
        [((8, 128), f32), ((dim, width), f32), ((own, dim), f32)],
        [Scalars(place), units, side, prototypes],
        scratch=[
            pltpu.VMEM((width, dim), bf16),
            pltpu.VMEM((crops, 1), jnp.int32),
            pltpu.VMEM((rows_all, width), f32),
            pltpu.VMEM((128, width), f32),
            pltpu.VMEM((crops, width), bf16),
            pltpu.VMEM((8, width), f32),
            pltpu.VMEM((8, width), f32),
            pltpu.VMEM((8, width), f32),
        ],
        flops=2 * width * (rows_all * dim + 6 * crops * dim),
        transcendentals=width * (rows_all + crops),
        limit=24,
    )
    return loss[0, 0], proto_grad, unit_grad


def sinkhorn(batch_codes, stored_codes, total):
    for turn in range(SINK_ITERS):
        column_totals = total(jnp.sum(batch_codes, 0) + jnp.sum(stored_codes, 0))
        batch_codes = batch_codes / column_totals
        stored_codes = stored_codes / column_totals
        batch_codes = batch_codes / jnp.sum(batch_codes, 1, keepdims=True)
        stored_codes = stored_codes / jnp.sum(stored_codes, 1, keepdims=True)
    return batch_codes


def swapped_loss(scores, codes, pick, loss_factor_weight):
    rows = scores.shape[0]
    target = jnp.einsum(
        "cab,cbk->cak", pick, codes.reshape(rows // CROPS, CROPS, PROTOS), precision=HIGH
    ).reshape(rows, PROTOS)
    log_likelihoods = jax.nn.log_softmax(scores / SOFTMAX_HEAT, axis=1)
    score_grad = (jnp.exp(log_likelihoods) * jnp.sum(target, 1, keepdims=True) - target) * (
        loss_factor_weight / SOFTMAX_HEAT
    )
    return -jnp.sum(target * log_likelihoods), score_grad.astype(jnp.bfloat16)


def per_device(
    canvases,
    crop_map,
    partner,
    queue,
    w_reduce,
    w_spatial,
    w_expand,
    w_hidden,
    w_project,
    norm_mid,
    norm_wide,
    bias_out,
    prototypes,
):
    f32, bf16 = jnp.float32, jnp.bfloat16
    size = lax.axis_size("dp")
    me_dp, me_core = lax.axis_index("dp"), lax.axis_index("shard")
    core = Scalars(me_core.astype(jnp.int32).reshape(1))
    own_canvases = canvases.shape[1]
    canvas_count = 2 * own_canvases
    pixels = SIDE * SIDE
    own_rows = own_canvases * pixels
    local_rows = canvas_count * pixels
    local_crops = canvas_count * CROPS
    pixel_total = float(local_rows * size)
    crop_count = local_crops * size
    crop_total = float(crop_count)
    loss_factor_weight = 1.0 / (MICRO * crop_total)
    crop_ids = jnp.arange(CROPS, dtype=jnp.int32)
    valid = inside_canvas(own_canvases)
    proj = bias_out.shape[0]
    partner_size = partner.size
    copies = copies_of(size)
    by_steps = size == STEPS_DP
    if by_steps:
        slots = relative_slots(size)
        chip_slots = lax.dynamic_slice_in_dim(slots.reshape(size, 2), me_core, 1, 1)[:, 0]

    def both_cores(values):
        mine = lax.dynamic_index_in_dim(values, me_core, 0, keepdims=False)
        other = lax.dynamic_index_in_dim(values, 1 - me_core, 0, keepdims=False)
        return jnp.concatenate([mine, swap_cores(other)], 0)

    def gather_whole(shard):
        return Gathered(lax.all_gather(shard, BOTH, axis=0, tiled=True))

    head_shard = jnp.concatenate([w_hidden, w_project], 1)
    beside = queue.shape[1]
    gathered_codes = (
        crop_count * PROTOS * 4 <= GATHERED_CODES_BYTES
        and queue.shape[0] == w_expand.shape[0]
        and partner_size <= beside
    )
    if gathered_codes:
        partners = jnp.pad(
            partner.astype(bf16).reshape(1, -1),
            ((0, 0), (0, beside - partner_size)),
        )
        partners = jnp.broadcast_to(partners, (queue.shape[0], beside))
        w_expand = jnp.concatenate([w_expand, queue, partners], 1)

    labels = both_cores(jnp.concatenate([crop_map, partner], 2))
    crop_map, partner = labels[:, :pixels], labels[:, pixels:]
    crop_of = jnp.arange(local_crops, dtype=jnp.int32)
    pixel_crop = crop_map + CROPS * jnp.arange(canvas_count, dtype=jnp.int32)[:, None]
    pixel_crop = pixel_crop.reshape(2, own_canvases, pixels).swapaxes(1, 2).reshape(local_rows)
    pool = (crop_of[:, None] == pixel_crop[None, :]).astype(bf16)
    spread = (pixel_crop[:, None] == crop_of[None, :]).astype(bf16)
    crop_sizes = jnp.sum(pool.astype(f32), 1, keepdims=True)

    half_rows = ((own_rows, D), bf16)
    own_x, other_x = kernel_call(
        arrange_kernel,
        [half_rows, half_rows],
        [core, canvases.transpose(0, 2, 3, 1, 4)],
        scratch=[pltpu.VMEM((own_rows, D), f32)],
    )
    input_rows = join([(own_x[None], swap_cores(other_x)[None])])[0].reshape(local_rows, D)

    if by_steps:
        reduce_part = Gathering(w_reduce, size)
        gather_step([reduce_part])
        spatial_part = Gathering(hold(w_spatial, [reduce_part.held]), size)
        gather_step([reduce_part], [pool, spread, crop_sizes, input_rows])
        head_held = lax.all_gather(hold(head_shard, [reduce_part.held]), "dp", axis=0)
        gather_step([reduce_part, spatial_part])
        expand_part = Gathering(hold(w_expand, [spatial_part.held]), size)
        reduce_all = reduce_part.finish(slots)
    else:
        reduce_all = gather_whole(w_reduce)

    mid_rows, wide_rows = ((local_rows, MID), f32), ((local_rows, D), f32)
    mid_sums, wide_sums = ((copies, 2, MID), f32), ((copies, 2, D), f32)

    def weight_out(weight):
        return (weight.shape, bf16, FAR)

    pre_one, sums, full_reduce = kernel_call(
        lambda *refs: reduce_kernel(reduce_all.count, *refs),
        [mid_rows, mid_sums, weight_out(reduce_all)],
        [input_rows] + reduce_all.inputs(),
        scratch=reduce_all.scratch() + [pltpu.SemaphoreType.DMA],
        flops=2 * local_rows * D * MID,
    )
    terms_one = terms_over_dp(sums)
    if by_steps:
        gather_step([spatial_part, expand_part], [sums])
        gather_step([spatial_part], [terms_one])
        spatial_all = spatial_part.finish(slots)
    else:
        spatial_all, expand_all = gather_whole(w_spatial), gather_whole(w_expand)

    pre_two, sums, image_patches, full_spatial = kernel_call(
        lambda *refs: spatial_kernel(spatial_all.count, pixel_total, *refs),
        [
            mid_rows,
            mid_sums,
            ((local_rows, 9 * MID), bf16, FAR),
            weight_out(spatial_all),
        ],
        [pre_one, norm_mid, valid, terms_one] + spatial_all.inputs(),
        scratch=[
            pltpu.VMEM((local_rows + 2 * EDGE, MID), f32),
            pltpu.VMEM((local_rows, 9 * MID), bf16),
            pltpu.SemaphoreType.DMA,
        ]
        + spatial_all.scratch()
        + [pltpu.SemaphoreType.DMA],
        flops=2 * local_rows * 9 * MID * MID,
    )
    terms_two = terms_over_dp(sums)
    if by_steps:
        gather_step([expand_part], [sums])
        gather_step([expand_part], [terms_two])
        expand_all = expand_part.finish(slots)

    side = ((expand_all.shape[0], max(expand_all.shape[1] - D, 128)), bf16)
    act_two, pre_three, sums, full_expand, side = kernel_call(
        lambda *refs: expand_kernel(expand_all.count, pixel_total, *refs),
        [((local_rows, MID), bf16), wide_rows, wide_sums, weight_out(expand_all), side],
        [pre_two, norm_mid, terms_two] + expand_all.inputs(),
        scratch=expand_all.scratch() + [pltpu.SemaphoreType.DMA],
        flops=2 * local_rows * D * MID,
    )
    terms_three = terms_over_dp(sums)
    if by_steps:
        head_held, _ = lax.optimization_barrier((head_held, sums))
        head = other_core_dp(head_held, size)
    else:
        head = gather_whole(head_shard)

    crop_rows = ((local_crops, D), f32)
    pooled_low, pre_head, sums, full_project = kernel_call(
        lambda *refs: pool_kernel(head.count, pixel_total, *refs),
        [((local_crops, D), bf16), crop_rows, wide_sums, ((D, proj), bf16)],
        [pre_three, input_rows, norm_wide, pool, crop_sizes, terms_three] + head.inputs(),
        scratch=[pltpu.VMEM((local_rows, 256), bf16), pltpu.VMEM((local_rows, 256), bf16)]
        + head.scratch(CHUNKS),
        flops=2 * local_crops * D * D,
        transcendentals=local_rows * D,
    )
    terms_head = terms_over_dp(sums)

    embed_rows = ((local_crops, proj), f32)
    act_head, unit_embed, inv_length, unit_low = kernel_call(
        lambda *refs: embed_kernel(crop_total, *refs),
        [
            ((local_crops, D), bf16),
            embed_rows,
            embed_rows,
            ((copies, local_crops, proj), bf16),
        ],
        [pre_head, norm_wide, Streamed(full_project), bias_out.reshape(1, proj), terms_head],
        flops=2 * local_crops * D * proj,
    )

    if gathered_codes:
        all_units = lax.all_to_all(unit_low, "dp", 0, 0).reshape(crop_count, proj)
        loss_part, proto_part, unit_grad = gathered_loss(
            all_units,
            side,
            prototypes,
            jnp.stack([me_dp * local_crops, me_core]).astype(jnp.int32),
            local_crops,
            own_canvases * CROPS,
            loss_factor_weight,
        )
    else:
        chip_queue = jnp.concatenate([queue, swap_cores(queue)], 0)
        queue_codes = jnp.exp(product_bt(chip_queue, prototypes) / SINK_EPS)
        pick = (partner[:, :, None] == crop_ids[None, None, :]).astype(f32)
        all_units = unit_low
        scores = product_bt(unit_low[0], prototypes)
        codes = sinkhorn(
            jnp.exp(scores / SINK_EPS), queue_codes, lambda sums: lax.psum(sums, "dp")
        )
        loss_part, score_low = swapped_loss(scores, codes, pick, loss_factor_weight)
        proto_part, loss_part = lax.psum((product_t(unit_low[0], score_low), loss_part), "dp")
        unit_grad = product(score_low, prototypes)

    embed_low, head_act_grad, sums, bias_part = kernel_call(
        lambda *refs: embed_back_kernel(crop_total, *refs),
        [((local_crops, proj), bf16), crop_rows, wide_sums, ((1, proj), f32)],
        [
            unit_grad,
            unit_embed,
            inv_length,
            Streamed(full_project),
            Streamed(pre_head),
            norm_wide,
            terms_head,
        ],
        flops=2 * local_crops * D * proj,
    )
    back_head = terms_over_dp(sums)

    left = lax.all_gather(pooled_low, "dp", axis=0, tiled=True)

    own_part = ((own_rows, D), f32)
    head_low, own_grad, other_grad, sums, total_head = kernel_call(
        lambda *refs: pool_back_kernel(head.count, crop_total, pixel_total, *refs),
        [((local_crops, D), bf16), own_part, own_part, wide_sums, ((2, D), f32)],
        [
            head_act_grad,
            pre_head,
            Streamed(pre_three),
            Streamed(input_rows),
            norm_wide,
            spread,
            crop_sizes,
            terms_head,
            back_head,
            terms_three,
        ]
        + head.inputs(),
        scratch=head.scratch(CHUNKS),
        flops=2 * local_crops * D * D,
        transcendentals=local_rows * D,
        after=[left],
    )
    back_three = terms_over_dp(sums)
    other_grad, _ = lax.optimization_barrier((other_grad, back_three))
    peer_grad = swap_cores(other_grad)

    right = lax.all_gather(head_low, "dp", axis=0, tiled=True)

    def low_halves(width):
        return [((local_rows, width // 2), bf16)] * 2

    three_kept, three_sent, two_act_grad, sums, total_three = kernel_call(
        lambda *refs: expand_back_kernel(pixel_total, *refs),
        [*low_halves(D), mid_rows, ((copies, 2, MID + proj), f32), ((2, D), f32)],
        [
            core,
            own_grad,
            other_grad,
            Streamed(pre_three),
            norm_wide,
            Streamed(full_expand),
            Streamed(pre_two),
            norm_mid,
            bias_part,
            terms_three,
            back_three,
            terms_two,
        ],
        scratch=[pltpu.VMEM((local_rows, D), bf16)],
        flops=2 * local_rows * D * MID,
    )
    back_two = terms_over_dp(sums)
    before_two = []
    if by_steps:
        expand_sum = weight_grad(
            (act_two, swap_cores(act_two)),
            (three_kept, swap_cores(three_sent)),
            chip_slots,
            size,
            back_two,
            (
                (act_head, swap_cores(act_head)),
                (embed_low, swap_cores(embed_low)),
                core,
            ),
            after=[sums],
        )
        before_two = [expand_sum.kept]

    two_kept, two_sent, one_act_grad, sums, total_two = kernel_call(
        lambda *refs: spatial_back_kernel(pixel_total, *refs),
        [*low_halves(MID), mid_rows, mid_sums, ((2, MID + proj), f32)],
        [
            core,
            two_act_grad,
            Streamed(pre_two),
            norm_mid,
            Streamed(full_spatial),
            Streamed(pre_one),
            valid,
            terms_two,
            back_two,
            terms_one,
        ],
        scratch=[
            pltpu.VMEM((9, local_rows + 2 * EDGE, MID), f32),
            pltpu.VMEM((local_rows, MID), bf16),
        ],
        flops=2 * local_rows * 9 * MID * MID,
        after=before_two,
    )
    before_one = []
    if by_steps:
        spatial_sum = weight_grad(
            (image_patches, swap_cores(image_patches)),
            (two_kept, swap_cores(two_sent)),
            chip_slots,
            size,
            two_kept,
            after=[expand_sum.received],
        )
        expand_sum.second(after=[spatial_sum.kept])
        sums, _ = lax.optimization_barrier((sums, spatial_sum.kept))
        before_one = [expand_sum.kept]

    back_one = terms_over_dp(sums)
    one_low, other_low, one_kept, one_sent, total_one = kernel_call(
        lambda *refs: reduce_back_kernel(pixel_total, *refs),
        [
            ((local_rows, MID), bf16),
            ((own_rows, MID), bf16),
            *low_halves(MID),
            ((2, MID), f32),
        ],
        [core, one_act_grad, Streamed(pre_one), norm_mid, terms_one, back_one],
        after=before_one,
    )
    if by_steps:
        spatial_sum.second([one_low])
        reduce_sum = weight_grad(
            (input_rows, swap_cores(input_rows)),
            (one_kept, swap_cores(one_sent)),
            chip_slots,
            size,
            one_low,
            after=[spatial_sum.kept, right],
        )

    proto_other = swap_cores(proto_part)
    other_low = swap_cores(other_low)
    late = []
    if by_steps:
        expand_sum.third([reduce_sum.kept])
        spatial_sum.third([expand_sum.kept])
        reduce_sum.second([spatial_sum.kept])
        late = [reduce_sum.kept]
    by_pixel = kernel_call(
        input_grad_kernel,
        [((MICRO, SIDE, SIDE, own_canvases, D), f32)],
        [core, own_grad, peer_grad, one_low, other_low, full_reduce],
        scratch=[pltpu.VMEM((own_rows, D), f32)],
        flops=2 * local_rows * D * MID,
        after=late,
    )[0]
    if by_steps:
        reduce_sum.third([by_pixel])
        late = [reduce_sum.kept]
    left, right, _ = lax.optimization_barrier((left, right, late))
    if gathered_codes:
        proto_grad = kernel_call(
            proto_grad_kernel,
            [(prototypes.shape, f32)],
            [Loaded(proto_part), Loaded(proto_other)],
            after=late,
        )[0]
    else:
        proto_grad = (proto_part + proto_other).T
    chip_rows = 2 * w_hidden.shape[0]
    hidden_part = product_t(
        lax.dynamic_slice_in_dim(left, me_dp * chip_rows, chip_rows, 1), right
    )

    def own_half(part):
        half = chip_rows // 2
        mine = lax.dynamic_slice_in_dim(part, me_core * half, half, 0)
        other = lax.dynamic_slice_in_dim(part, (1 - me_core) * half, half, 0)
        return mine + swap_cores(other)

    grad_hidden = own_half(hidden_part)
    if by_steps:
        grad_spatial, grad_reduce = swap_columns(spatial_sum.finish(), reduce_sum.finish())
        total = expand_sum.finish()
        (grad_expand,) = swap_columns(total[:, : D // 2])
        grad_project = jnp.concatenate(
            [total[:, k : k + proj] for k in range(D // 2, total.shape[1], proj)], 0
        )
    else:

        def scatter(first, kept, sent):
            lows = jnp.concatenate(
                [jnp.where(me_core == 0, kept, sent), jnp.where(me_core == 0, sent, kept)], 1
            )
            return lax.psum_scatter(
                product_t(first, lows), BOTH, scatter_dimension=0, tiled=True
            )

        grad_reduce = scatter(input_rows, one_kept, one_sent)
        grad_spatial = scatter(image_patches, two_kept, two_sent)
        grad_expand = scatter(act_two, three_kept, three_sent)
        grad_project = lax.psum_scatter(
            product_t(act_head, embed_low), BOTH, scatter_dimension=0, tiled=True
        )

    totals = (total_one, total_two, total_three, total_head)
    (total_one, total_two, total_three, total_head), _ = lax.optimization_barrier((totals, late))
    narrow = jnp.concatenate(
        [
            jnp.stack([total_one[1], total_one[0], total_two[1, :MID], total_two[0, :MID]])
            .reshape(-1),
            jnp.stack([total_three[1], total_three[0], total_head[1], total_head[0]]).reshape(-1),
            total_two[0, MID:],
            jnp.broadcast_to(loss_part, (128,)),
        ]
    )
    narrow = narrow + swap_cores(narrow)
    mid_end, wide_end = norm_mid.size, norm_mid.size + norm_wide.size
    bias_end = wide_end + proj
    return (
        narrow[bias_end] * loss_factor_weight,
        by_pixel.transpose(0, 3, 1, 2, 4),
        grad_reduce,
        grad_spatial,
        grad_expand,
        grad_hidden,
        grad_project,
        narrow[:mid_end].reshape(norm_mid.shape),
        narrow[mid_end:wide_end].reshape(norm_wide.shape),
        narrow[wide_end:bias_end],
        proto_grad,
    )


def solution(mesh):
    return jax.shard_map(
        per_device,
        mesh=mesh,
        in_specs=(
            P(None, ("dp", "shard"), None, None, None),
            P(None, ("dp", "shard"), None),
            P(None, ("dp", "shard"), None),
            P(("dp", "shard"), None),
            P(("dp", "shard"), None),
            P(("dp", "shard"), None),
            P(("dp", "shard"), None),
            P(("dp", "shard"), None),
            P(("dp", "shard"), None),
            P(),
            P(),
            P(),
            P(),
        ),
        out_specs=(
            P(),
            P(None, ("dp", "shard"), None, None, None),
            P(("dp", "shard"), None),
            P(("dp", "shard"), None),
            P(("dp", "shard"), None),
            P(("dp", "shard"), None),
            P(("dp", "shard"), None),
            P(),
            P(),
            P(),
            P(),
        ),
        check_vma=False,
    )
```

```python
import dataclasses

import jax
import jax.numpy as jnp
import numpy as np
from jax import lax
from jax.experimental import pallas as pl
from jax.experimental.pallas import tpu as pltpu
from jax.sharding import PartitionSpec as P

D = 2048
MID = 512
PROTOS = 3000
SIDE = 6
CROPS = 4
SINK_ITERS = 3
MICRO = 2


EPS_NORM = 1e-05
EPS_UNIT = 1e-06
SOFTMAX_HEAT = 0.1
SINK_EPS = 0.05
HIGH = lax.Precision.HIGHEST
BOTH = ("dp", "shard")
GATHERED_CODES_BYTES = 32 * 2**20
MIB = 2**20
LANES = 512
CHUNKS = 4


def product(left, right):
    return jnp.dot(left, right, preferred_element_type=jnp.float32)


def product_t(left, right):
    return lax.dot_general(
        left, right, (((0,), (0,)), ((), ())), preferred_element_type=jnp.float32
    )


def product_bt(left, right):
    return lax.dot_general(
        left, right, (((1,), (1,)), ((), ())), preferred_element_type=jnp.float32
    )


def silu_slope(values):
    sigmoid_value = jax.nn.sigmoid(values)
    return sigmoid_value * (1.0 + values * (1.0 - sigmoid_value))


@dataclasses.dataclass
class Scalars:
    array: jax.Array


@dataclasses.dataclass
class Left:
    array: jax.Array


@dataclasses.dataclass
class Loaded:
    array: jax.Array


@dataclasses.dataclass
class Streamed:
    array: jax.Array


class Arriving:
    def __init__(self, ref, copy):
        self.ref, self.copy = ref, copy
        self.shape = ref.shape

    def __getitem__(self, index):
        if self.copy is not None:
            self.copy.wait()
            self.copy = None
        return self.ref[index]


FAR, PUT_FAR = "far", "put far"


def kernel_call(body, outs, args, scratch=(), flops=0, transcendentals=0, limit=17, after=()):
    spaces = {Scalars: pltpu.SMEM, Left: pltpu.HBM, Streamed: pltpu.HBM}
    in_spaces = [spaces.get(type(a), pltpu.VMEM) for a in args] + [pltpu.HBM] * len(after)
    after = [pltpu.with_memory_space_constraint(a, pltpu.HBM) for a in after]
    arrays = []
    for a in args:
        if isinstance(a, (Left, Loaded, Streamed)):
            a = pltpu.with_memory_space_constraint(a.array, pltpu.HBM)
        arrays.append(a.array if isinstance(a, Scalars) else a)
    used = len(arrays)
    out_spaces = [pltpu.HBM if FAR in out else pltpu.VMEM for out in outs]

    streamed = [i for i, a in enumerate(args) if isinstance(a, Streamed)]
    scratch = list(scratch)
    own_scratch = len(scratch)
    for i in streamed:
        scratch += [pltpu.VMEM(arrays[i].shape, arrays[i].dtype), pltpu.SemaphoreType.DMA]

    def kernel(*refs):
        inputs, refs = list(refs[:used]), refs[used + len(after) :]
        mine = len(outs) + own_scratch
        for k, i in enumerate(streamed):
            buffer, sem = refs[mine + 2 * k : mine + 2 * k + 2]
            copy = pltpu.make_async_copy(inputs[i], buffer, sem)
            copy.start()
            inputs[i] = Arriving(buffer, copy)
        body(*inputs, *refs[:mine])

    moved = sum(a.size * a.dtype.itemsize for a in arrays)
    return pl.pallas_call(
        kernel,
        out_shape=[
            jax.ShapeDtypeStruct(*out) if len(out) == 2 else pltpu.HBM(*out[:2]) for out in outs
        ],
        in_specs=[pl.BlockSpec(memory_space=space) for space in in_spaces],
        out_specs=[pl.BlockSpec(memory_space=space) for space in out_spaces],
        scratch_shapes=list(scratch),
        compiler_params=pltpu.CompilerParams(vmem_limit_bytes=limit * MIB),
        cost_estimate=pl.CostEstimate(
            flops=int(flops), bytes_accessed=int(moved), transcendentals=int(transcendentals)
        ),
    )(*arrays, *after)


def join_kernel(counts, *refs):
    outs = refs[sum(counts) :]
    start = 0
    for count, joined in zip(counts, outs):
        parts = refs[start : start + count]
        start += count
        length = parts[0].shape[0]

        def move(i, carry):
            for k, part in enumerate(parts):
                joined[i + k * length] = part[i]
            return carry

        lax.fori_loop(0, length, move, 0)


def join(groups, after=()):
    counts = [len(group) for group in groups]
    outs = [
        ((len(group) * group[0].shape[0],) + group[0].shape[1:], group[0].dtype)
        for group in groups
    ]
    return kernel_call(
        lambda *refs: join_kernel(counts, *refs),
        outs,
        [part for group in groups for part in group],
        after=after,
    )


def hold_kernel(source, target):
    target[...] = source[...]


def hold(values, after=()):
    return kernel_call(hold_kernel, [(values.shape, values.dtype)], [values], after=after)[0]


def add_parts_kernel(kept, received, *totals):
    length = totals[0].shape[0]

    def move(i, carry):
        for k, out_ref in enumerate(totals):
            place = i + k * length
            total = kept[place].astype(jnp.float32) + received[place].astype(jnp.float32)
            out_ref[i] = total.astype(out_ref.dtype)
        return carry

    lax.fori_loop(0, length, move, 0)


def add_parts(kept, received, count, after=()):
    shape = (kept.shape[0] // count,) + kept.shape[1:]
    kept, *sent = kernel_call(
        add_parts_kernel,
        [(shape, jnp.float32, PUT_FAR)] + [(shape, jnp.bfloat16, PUT_FAR)] * (count - 1),
        [Loaded(kept), Loaded(received)],
        after=after,
    )
    return kept, sent


def swap_cores(values):
    return lax.ppermute(values, "shard", [(0, 1), (1, 0)])


def flip_dp(values, bits, size):
    return lax.ppermute(values, "dp", [(i, i ^ bits) for i in range(size)])


def flip_both(values, dp_bits, size):
    pairs = [(2 * i + c, 2 * (i ^ dp_bits[c]) + c) for i in range(size) for c in range(2)]
    return lax.ppermute(values, BOTH, pairs)


def copies_of(size):
    return size if size <= STEPS_DP else 1


def terms_over_dp(copies):
    if copies.shape[0] > 1:
        return lax.all_to_all(copies, "dp", 0, 0)
    return lax.psum(copies, "dp")


Z_BITS = (8, 4, 12)
XY_BITS = ((2, 1), (1, 2))
STEPS_DP = 16


def relative_slots(size):
    me_dp, me_core = lax.axis_index("dp"), lax.axis_index("shard")
    device = jnp.arange(2 * size, dtype=jnp.int32)
    apart_dp, apart_core = (device // 2) ^ me_dp, (device % 2) ^ me_core
    holder = device % 2
    on = lambda bit: jnp.where((apart_dp & bit) != 0, 1, 0)
    low, high = (jnp.where(holder == 0, on(zero), on(one)) for zero, one in XY_BITS)
    slot = on(Z_BITS[0]) + 2 * on(Z_BITS[1]) + 4 * low + 8 * high + size * apart_core
    return slot.astype(jnp.int32)


class Gathering:
    def __init__(self, shard, size):
        self.size = size
        self.held = shard[None]
        self.step = 0

    def send(self):
        step, held = self.step, self.held
        self.step += 1
        if step == 0:
            return [held] + [flip_dp(held, bits, self.size) for bits in Z_BITS]
        return [held, flip_both(held, XY_BITS[step - 1], self.size)]

    def finish(self, slots):
        return Gathered(self.held, swap_cores(self.held), slots)


def gather_step(parts, after=()):
    joined = join([part.send() for part in parts], after)
    for part, held in zip(parts, joined):
        part.held = held


def other_core_dp(held, size):
    device = jnp.arange(2 * size, dtype=jnp.int32)
    other = (device % 2) != lax.axis_index("shard")
    slots = jnp.where(other, size, 0) + device // 2
    return Gathered(held, swap_cores(held), slots.astype(jnp.int32))


class Scattering:
    def __init__(self, kept, sent, size):
        self.size = size
        self.kept, self.sent = kept, sent

    def first(self, before):
        sent, _ = lax.optimization_barrier((self.sent, before))
        self.received = flip_both(sent, XY_BITS[1], self.size)

    def second(self, after=()):
        self.kept, sent = add_parts(self.kept, self.received, 2, after)
        self.received = flip_both(sent[0], XY_BITS[0], self.size)

    def third(self, after=()):
        self.kept, sent = add_parts(self.kept, self.received, 4, after)
        self.received = [flip_dp(part, bits, self.size) for part, bits in zip(sent, Z_BITS)]

    def finish(self):
        one, two, three = (part[0].astype(jnp.float32) for part in self.received)
        return (self.kept[0] + one) + (two + three)


@dataclasses.dataclass
class Gathered:
    held: jax.Array
    other: jax.Array | None = None
    slots: jax.Array | None = None

    @property
    def count(self):
        return 1 if self.other is None else 3

    @property
    def shape(self):
        if self.other is None:
            return self.held.shape
        half, rows, width = self.held.shape
        return (2 * half * rows, width)

    def inputs(self):
        if self.other is None:
            return [Left(self.held)]
        return [Scalars(self.slots), Left(self.held), Left(self.other)]

    def scratch(self, chunks=1):
        copies = chunks if self.other is None else 2 * self.held.shape[0]
        return [pltpu.VMEM(self.shape, jnp.bfloat16), pltpu.SemaphoreType.DMA((copies,))]


def fetch_weight(inputs, weight, sems, chunks=1):
    count = sems.shape[0]
    rows = weight.shape[0] // count
    each = count // chunks

    def copy(source, i):
        target = weight.at[pl.ds(pl.multiple_of(i * rows, rows), rows)]
        return pltpu.make_async_copy(source, target, sems.at[i])

    if len(inputs) == 1:
        copies = [copy(inputs[0].at[pl.ds(i * rows, rows)], i) for i in range(count)]
        for one in copies:
            one.start()

        def wait_ordered(chunk):
            for one in copies[chunk * each : (chunk + 1) * each]:
                one.wait()

        return wait_ordered

    table, held, other = inputs
    half = held.shape[0]

    def begin(i, carry):
        slot = table[i]

        @pl.when(slot < half)
        def _():
            copy(held.at[slot], i).start()

        @pl.when(slot >= half)
        def _():
            copy(other.at[slot - half], i).start()

        return carry

    lax.fori_loop(0, count, begin, 0)

    def wait(chunk):
        def finish(i, carry):
            copy(held.at[0], i).wait()
            return carry

        lax.fori_loop(chunk * each, (chunk + 1) * each, finish, 0)

    return wait


def weight_grad_kernel(beside, table, *refs):
    left, left_peer, right, right_peer = refs[:4]
    if beside:
        second, second_peer, second_right, second_right_peer, core = refs[4:9]
        kept_ref, sent_ref, total_ref, second_ref = refs[9:]
    else:
        kept_ref, sent_ref, total_ref = refs[4:]
    half, rows, _ = kept_ref.shape
    width = right.shape[1]
    for k in range(0, total_ref.shape[0], 512):
        total_ref[k : k + 512, :] = product_t(left[:, k : k + 512], right[...]) + product_t(
            left_peer[:, k : k + 512], right_peer[...]
        )
    if beside:
        second_ref[...] = product_t(second[...], second_right[...]) + product_t(
            second_peer[...], second_right_peer[...]
        )

    def place(out_ref, slot, i):
        found = total_ref[pl.ds(pl.multiple_of(i * rows, rows), rows), :]
        out_ref[slot, :, :width] = found.astype(out_ref.dtype)
        for part in range(beside):
            start = ((2 * i + core[0]) * beside + part) * rows
            across = second_ref.shape[1]
            columns = slice(width + part * across, width + (part + 1) * across)
            found = second_ref[pl.ds(pl.multiple_of(start, rows), rows), :]
            out_ref[slot, :, columns] = found.astype(out_ref.dtype)

    def move(i, carry):
        slot = table[i]

        @pl.when(slot < half)
        def _():
            place(kept_ref, slot, i)

        @pl.when(slot >= half)
        def _():
            place(sent_ref, slot - half, i)

        return carry

    lax.fori_loop(0, 2 * half, move, 0)


def weight_grad(left, right, slots, size, second=None, after=()):
    depth, width = left[0].shape[1], right[0].shape[1]
    rows = depth // size
    args = [Scalars(slots), *left, *right]
    scratch, beside, extra = [pltpu.VMEM((depth, width), jnp.float32)], 0, 0
    if second is not None:
        (second_left, second_right, core) = second
        args += [*second_left, *second_right, core]
        second_shape = (second_left[0].shape[1], second_right[0].shape[1])
        beside = second_shape[0] // (2 * depth)
        extra = beside * second_shape[1]
        scratch.append(pltpu.VMEM(second_shape, jnp.float32))
    shape = (size // 2, rows, width + extra)
    kept, sent = kernel_call(
        lambda *refs: weight_grad_kernel(beside, *refs),
        [(shape, jnp.float32, PUT_FAR), (shape, jnp.bfloat16, PUT_FAR)],
        args,
        scratch=scratch,
        flops=4 * left[0].shape[0] * depth * width,
        after=after,
    )
    return Scattering(kept, sent, size)


def swap_columns(*totals):
    me = lax.axis_index("shard")

    def half_of(core):
        halves = [total.shape[0] // 2 for total in totals]
        return jnp.concatenate(
            [
                lax.dynamic_slice_in_dim(total, core * half, half, 0)
                for total, half in zip(totals, halves)
            ]
        )

    mine, other = half_of(me), swap_cores(half_of(1 - me))
    first, second = jnp.where(me == 0, mine, other), jnp.where(me == 0, other, mine)
    both, found, start = jnp.concatenate([first, second], 1), [], 0
    for total in totals:
        found.append(both[start : start + total.shape[0] // 2])
        start += total.shape[0] // 2
    return found


def tiles(rows, width, high, wide):
    for r in range(0, rows, high):
        for k in range(0, width, wide):
            yield slice(r, r + high), slice(k, k + wide)


def norm_factors(terms, norm_ref, row, count):
    totals = jnp.sum(terms[...], 0)
    average = totals[0:1] / count
    inverse = lax.rsqrt(totals[1:2] / count - average * average + EPS_NORM)
    return average, inverse, norm_ref[row : row + 1, :], norm_ref[row + 1 : row + 2, :]


def normalize(values, factors, columns):
    average, inverse, gain, shift = (part[:, columns] for part in factors)
    unit = (values - average) * inverse
    return unit, gain * unit + shift


def silu(values):
    return values * jax.nn.sigmoid(values)


def norm_backward(grad, unit, factors, totals, count, columns):
    _, inverse, gain, _ = (part[:, columns] for part in factors)
    mean_grad = totals[0:1, columns] / count
    mean_product = totals[1:2, columns] / count
    return gain * inverse * (grad - mean_grad - unit * mean_product)


class Sums:
    def __init__(self, out_ref):
        self.out_ref = out_ref
        self.parts = {}

    def add(self, columns, first, second):
        key = (columns.start, columns.stop)
        fold = lambda v: jnp.sum(v.reshape(v.shape[0] // 8, 8, v.shape[1]), 0)
        first, second = fold(first), fold(second)
        if key in self.parts:
            first, second = self.parts[key][0] + first, self.parts[key][1] + second
        self.parts[key] = (first, second)

    def store(self):
        for (start, stop), (first, second) in self.parts.items():
            first = jnp.sum(first, 0, keepdims=True)
            second = jnp.sum(second, 0, keepdims=True)
            for copy in range(self.out_ref.shape[0]):
                self.out_ref[copy, 0:1, start:stop] = first
                self.out_ref[copy, 1:2, start:stop] = second


def reduce_kernel(weights, x_ref, *refs):
    inputs, refs = refs[:weights], refs[weights:]
    pre_ref, sums_ref, weight_out, weight, sems, out_sem = refs
    fetch_weight(inputs, weight, sems)(0)
    copy_out = pltpu.make_async_copy(weight, weight_out, out_sem)
    copy_out.start()
    sums = Sums(sums_ref)
    for columns in (slice(k, k + 256) for k in range(0, MID, 256)):
        pre = product(x_ref[...], weight[:, columns])
        pre_ref[:, columns] = pre
        sums.add(columns, pre, pre * pre)
    sums.store()
    copy_out.wait()


def spatial_kernel(weights, count, pre_ref, norm_ref, valid_ref, *refs):
    term_refs, *refs = refs
    inputs, refs = refs[:weights], refs[weights:]
    out_ref, sums_ref, patches_out, weight_out, padded, patches, sem, weight, sems, out_sem = refs
    wait = fetch_weight(inputs, weight, sems)
    rows = pre_ref.shape[0]
    factors = norm_factors(term_refs, norm_ref, 0, count)
    edge = jnp.zeros((EDGE, MID), jnp.float32)
    padded[0:EDGE, :] = edge
    padded[EDGE + rows :, :] = edge
    for high, columns in tiles(rows, MID, 48, 512):
        _, shifted = normalize(pre_ref[high, columns], factors, columns)
        low = silu(shifted).astype(jnp.bfloat16)
        padded[EDGE + high.start : EDGE + high.stop, columns] = low.astype(jnp.float32)
    for place in range(9):
        offset = EDGE + neighbour(place, rows // (2 * SIDE * SIDE))
        for high, columns in tiles(rows, MID, 48, 512):
            values = padded[offset + high.start : offset + high.stop, columns]
            values = values * valid_ref[high, place : place + 1]
            patches[high, place * MID : (place + 1) * MID] = values.astype(jnp.bfloat16)
    copy = pltpu.make_async_copy(patches, patches_out, sem)
    copy.start()
    wait(0)
    copy_out = pltpu.make_async_copy(weight, weight_out, out_sem)
    copy_out.start()
    sums = Sums(sums_ref)
    for columns in (slice(k, k + 256) for k in range(0, MID, 256)):
        pre = product(patches[...], weight[:, columns])
        out_ref[:, columns] = pre
        sums.add(columns, pre, pre * pre)
    sums.store()
    copy.wait()
    copy_out.wait()


def expand_kernel(weights, count, pre_ref, norm_ref, *refs):
    term_refs, *refs = refs
    inputs, refs = refs[:weights], refs[weights:]
    act_ref, out_ref, sums_ref, weight_out, side_ref, weight, sems, out_sem = refs
    wait = fetch_weight(inputs, weight, sems)
    factors = norm_factors(term_refs, norm_ref, 2, count)
    for high, columns in tiles(pre_ref.shape[0], MID, 48, 512):
        _, shifted = normalize(pre_ref[high, columns], factors, columns)
        act_ref[high, columns] = silu(shifted).astype(jnp.bfloat16)
    wait(0)
    copy_out = pltpu.make_async_copy(weight, weight_out, out_sem)
    copy_out.start()
    if weight.shape[1] > D:
        side_ref[...] = weight[:, D:]
    else:
        side_ref[...] = jnp.zeros_like(side_ref)
    sums = Sums(sums_ref)
    for columns in (slice(k, k + 256) for k in range(0, D, 256)):
        pre = product(act_ref[...], weight[:, columns])
        out_ref[:, columns] = pre
        sums.add(columns, pre, pre * pre)
    sums.store()
    copy_out.wait()


def split(values):
    high = values.astype(jnp.bfloat16)
    return high, (values - high.astype(jnp.float32)).astype(jnp.bfloat16)


def pool_kernel(weights, count, pre_ref, x_ref, norm_ref, pool_ref, size_ref, *refs):
    term_refs, *refs = refs
    inputs, refs = refs[:weights], refs[weights:]
    pooled_ref, out_ref, sums_ref, project_ref, high_ref, rest_ref, weight, sems = refs
    wait = fetch_weight(inputs, weight, sems, CHUNKS)
    factors = norm_factors(term_refs, norm_ref, 0, count)
    rows = pre_ref.shape[0]
    for k in range(0, D, 256):
        for high, columns in tiles(rows, 256, 96, 256):
            across = slice(k + columns.start, k + columns.stop)
            _, shifted = normalize(pre_ref[high, across], factors, across)
            block = silu(shifted + x_ref[high, across].astype(jnp.float32))
            high_ref[high, columns], rest_ref[high, columns] = split(block)
        pooled = product(pool_ref[...], high_ref[...]) + product(pool_ref[...], rest_ref[...])
        pooled_ref[:, k : k + 256] = (pooled / size_ref[...]).astype(jnp.bfloat16)
    step = D // CHUNKS
    total = 0.0
    for chunk in range(CHUNKS):
        wait(chunk)
        part = slice(chunk * step, (chunk + 1) * step)
        total = total + product(pooled_ref[:, part], weight[part, :D])
    out_ref[...] = total
    project_ref[...] = weight[:, D:]
    sums = Sums(sums_ref)
    for columns in (slice(k, k + 512) for k in range(0, D, 512)):
        pre = out_ref[:, columns]
        sums.add(columns, pre, pre * pre)
    sums.store()


def embed_kernel(count, pre_ref, norm_ref, project_ref, bias_ref, pooled_ref, *refs):
    term_refs, *refs = refs
    act_ref, unit_ref, inverse_ref, low_ref = refs
    factors = norm_factors(term_refs, norm_ref, 2, count)
    for high, columns in tiles(pre_ref.shape[0], D, pre_ref.shape[0], 512):
        _, shifted = normalize(pre_ref[high, columns], factors, columns)
        act_ref[high, columns] = silu(shifted).astype(jnp.bfloat16)
    embed = product(act_ref[...], project_ref[...]) + bias_ref[...]
    inverse = lax.rsqrt(jnp.sum(embed * embed, 1, keepdims=True) + EPS_UNIT)
    unit = embed * inverse
    unit_ref[...] = unit
    inverse_ref[...] = jnp.broadcast_to(inverse, inverse_ref.shape)
    low = unit.astype(jnp.bfloat16)
    copies, rows, _ = low_ref.shape
    crops = low.shape[0]
    for copy in range(copies):
        low_ref[copy, :crops, :] = low
        if rows > crops:
            width = D // copies
            low_ref[copy, crops:, :] = pooled_ref[:, copy * width : (copy + 1) * width]


def embed_back_kernel(
    count, grad_ref, unit_ref, inverse_ref, project_ref, pre_ref, norm_ref, *refs
):
    term_refs, *refs = refs
    low_ref, out_ref, sums_ref, bias_ref = refs
    grad, unit = grad_ref[...], unit_ref[...]
    embed_grad = inverse_ref[...] * (grad - unit * jnp.sum(grad * unit, 1, keepdims=True))
    low_ref[...] = embed_grad.astype(jnp.bfloat16)
    bias_ref[...] = jnp.sum(embed_grad, 0, keepdims=True)
    factors = norm_factors(term_refs, norm_ref, 2, count)
    sums = Sums(sums_ref)
    for columns in (slice(k, k + 512) for k in range(0, D, 512)):
        back = product_bt(low_ref[...], project_ref[columns, :])
        head_unit, shifted = normalize(pre_ref[:, columns], factors, columns)
        back = back * silu_slope(shifted)
        out_ref[:, columns] = back
        sums.add(columns, back, back * head_unit)
    sums.store()


def pool_back_kernel(
    weights,
    crop_count,
    count,
    grad_ref,
    head_pre_ref,
    pre_ref,
    x_ref,
    norm_ref,
    spread_ref,
    size_ref,
    *refs,
):
    head_terms, head_back, pre_terms, *refs = refs
    inputs, refs = refs[:weights], refs[weights:]
    low_ref, own_ref, other_ref, sums_ref, total_ref, weight, sems = refs
    wait = fetch_weight(inputs, weight, sems, CHUNKS)
    step = D // CHUNKS
    head_factors = norm_factors(head_terms, norm_ref, 2, crop_count)
    totals = jnp.sum(head_back[...], 0)
    total_ref[...] = totals
    for columns in (slice(k, k + 512) for k in range(0, D, 512)):
        unit, _ = normalize(head_pre_ref[:, columns], head_factors, columns)
        grad = norm_backward(
            grad_ref[:, columns], unit, head_factors, totals, crop_count, columns
        )
        low_ref[:, columns] = grad.astype(jnp.bfloat16)
    factors = norm_factors(pre_terms, norm_ref, 0, count)
    sums = Sums(sums_ref)
    own_rows = own_ref.shape[0]
    for chunk in range(CHUNKS):
        wait(chunk)
        part = slice(chunk * step, (chunk + 1) * step)
        pooled = product_bt(low_ref[...], weight[part, :D]) / size_ref[...]
        high_part, rest_part = split(pooled)
        for rows, columns in tiles(2 * own_rows, part.stop - part.start, 48, 256):
            across = slice(part.start + columns.start, part.start + columns.stop)
            spread = spread_ref[rows, :]
            out_grad = product(spread, high_part[:, columns]) + product(
                spread, rest_part[:, columns]
            )
            unit, shifted = normalize(pre_ref[rows, across], factors, across)
            joined = shifted + x_ref[rows, across].astype(jnp.float32)
            joined_grad = out_grad * silu_slope(joined)
            if rows.start < own_rows:
                own_ref[rows, across] = joined_grad
            else:
                other_ref[rows.start - own_rows : rows.stop - own_rows, across] = joined_grad
            sums.add(across, joined_grad, joined_grad * unit)
    sums.store()


def column_halves(low_ref, core, kept_ref, sent_ref):
    half = kept_ref.shape[1]
    for out_ref, which in ((kept_ref, core[0]), (sent_ref, 1 - core[0])):
        out_ref[...] = low_ref[:, pl.ds(pl.multiple_of(which * half, half), half)]


def expand_back_kernel(
    count, core, own_ref, other_ref, pre_ref, wide_ref, weight_ref, before_ref, mid_ref, bias_ref, *refs
):
    pre_terms, back_terms, before_terms, *refs = refs
    kept_ref, sent_ref, out_ref, sums_ref, total_ref, low_ref = refs
    factors = norm_factors(pre_terms, wide_ref, 0, count)
    totals = jnp.sum(back_terms[...], 0)
    total_ref[...] = totals
    own_rows = own_ref.shape[0]
    for rows, columns in tiles(2 * own_rows, D, 48, 512):
        unit, _ = normalize(pre_ref[rows, columns], factors, columns)
        if rows.start < own_rows:
            grad = own_ref[rows, columns]
        else:
            grad = other_ref[rows.start - own_rows : rows.stop - own_rows, columns]
        grad = norm_backward(grad, unit, factors, totals, count, columns)
        low_ref[rows, columns] = grad.astype(jnp.bfloat16)
    column_halves(low_ref, core, kept_ref, sent_ref)
    factors = norm_factors(before_terms, mid_ref, 2, count)
    sums = Sums(sums_ref)
    for columns in (slice(k, k + 256) for k in range(0, MID, 256)):
        back = product_bt(low_ref[...], weight_ref[columns, :D])
        unit, shifted = normalize(before_ref[:, columns], factors, columns)
        back = back * silu_slope(shifted)
        out_ref[:, columns] = back
        sums.add(columns, back, back * unit)
    sums.store()
    bias = jnp.concatenate([bias_ref[...], jnp.zeros_like(bias_ref)], 0)
    for copy in range(sums_ref.shape[0]):
        sums_ref[copy, :, MID:] = bias


def spatial_back_kernel(
    count, core, grad_ref, pre_ref, norm_ref, weight_ref, before_ref, valid_ref, *refs
):
    pre_terms, back_terms, before_terms, *refs = refs
    kept_ref, sent_ref, out_ref, sums_ref, total_ref, slots, low_ref = refs
    rows = grad_ref.shape[0]
    factors = norm_factors(pre_terms, norm_ref, 2, count)
    totals = jnp.sum(back_terms[...], 0)
    total_ref[...] = totals
    for high, columns in tiles(rows, MID, 48, 512):
        unit, _ = normalize(pre_ref[high, columns], factors, columns)
        grad = norm_backward(grad_ref[high, columns], unit, factors, totals, count, columns)
        low_ref[high, columns] = grad.astype(jnp.bfloat16)
    column_halves(low_ref, core, kept_ref, sent_ref)
    edge = jnp.zeros((EDGE, MID), jnp.float32)
    for place in range(9):
        slots[place, 0:EDGE, :] = edge
        slots[place, EDGE + rows :, :] = edge
        for columns in (slice(k, k + 256) for k in range(0, MID, 256)):
            patch = product_bt(
                low_ref[...],
                weight_ref[place * MID + columns.start : place * MID + columns.stop, :],
            )
            slots[place, EDGE : EDGE + rows, columns] = patch * valid_ref[:, place : place + 1]
    factors = norm_factors(before_terms, norm_ref, 0, count)
    sums = Sums(sums_ref)
    for high, columns in tiles(rows, MID, 48, 256):
        back = 0.0
        for place in range(9):
            start = EDGE - neighbour(place, rows // (2 * SIDE * SIDE)) + high.start
            back = back + slots[place, start : start + high.stop - high.start, columns]
        unit, shifted = normalize(before_ref[high, columns], factors, columns)
        back = back * silu_slope(shifted)
        out_ref[high, columns] = back
        sums.add(columns, back, back * unit)
    sums.store()


def reduce_back_kernel(
    count,
    core,
    grad_ref,
    pre_ref,
    norm_ref,
    pre_terms,
    back_terms,
    low_ref,
    other_ref,
    kept_ref,
    sent_ref,
    total_ref,
):
    rows = grad_ref.shape[0]
    factors = norm_factors(pre_terms, norm_ref, 0, count)
    totals = jnp.sum(back_terms[...], 0)
    total_ref[...] = totals
    for high, columns in tiles(rows, MID, 48, 512):
        unit, _ = normalize(pre_ref[high, columns], factors, columns)
        grad = norm_backward(grad_ref[high, columns], unit, factors, totals, count, columns)
        low_ref[high, columns] = grad.astype(jnp.bfloat16)
    other_ref[...] = low_ref[rows // 2 :, :]
    column_halves(low_ref, core, kept_ref, sent_ref)


def arrange_kernel(core, canvases_ref, own_ref, other_ref, rows_ref):
    _, _, _, canvas_count, _ = canvases_ref.shape
    for which, out_ref in enumerate((own_ref, other_ref)):
        micro = core[0] if which == 0 else 1 - core[0]
        for pixel in range(SIDE * SIDE):
            rows = slice(pixel * canvas_count, (pixel + 1) * canvas_count)
            values = canvases_ref[micro, pixel // SIDE, pixel % SIDE]
            rows_ref[rows, :] = values.astype(jnp.float32)
        out_ref[...] = rows_ref[...].astype(jnp.bfloat16)


def input_grad_kernel(
    core, own_ref, other_ref, low_ref, other_low_ref, weight_ref, out_ref, rows_ref
):
    own_rows = own_ref.shape[0]
    canvas_count = out_ref.shape[3]
    for which in range(2):
        micro = core[0] if which == 0 else 1 - core[0]
        grad_ref = own_ref if which == 0 else other_ref
        low = low_ref[:own_rows, :] if which == 0 else other_low_ref[...]
        for columns in (slice(k, k + 512) for k in range(0, D, 512)):
            rows_ref[:, columns] = grad_ref[:, columns] + product_bt(low, weight_ref[columns, :])
        for pixel in range(SIDE * SIDE):
            rows = slice(pixel * canvas_count, (pixel + 1) * canvas_count)
            out_ref[micro, pixel // SIDE, pixel % SIDE] = rows_ref[rows, :]


def proto_grad_kernel(first_ref, second_ref, out_ref):
    rows = out_ref.shape[0]
    for k in range(0, rows, 128):
        stop = min(k + 128, rows)
        total = first_ref[:, k : k + 128] + second_ref[:, k : k + 128]
        out_ref[k:stop, :] = total.T[: stop - k, :]


def inside_canvas(own_canvases):
    valid = np.zeros((2, SIDE, SIDE, own_canvases, 16), np.float32)
    for place in range(9):
        down, right = place // 3 - 1, place % 3 - 1
        for y in range(SIDE):
            for x in range(SIDE):
                valid[:, y, x, :, place] = 0 <= y + down < SIDE and 0 <= x + right < SIDE
    return jnp.asarray(valid.reshape(-1, 16))


def neighbour(place, own_canvases):
    return ((place // 3 - 1) * SIDE + place % 3 - 1) * own_canvases


EDGE = 32


def add_columns(total_ref, columns, values):
    rows, width = values.shape
    total_ref[:, columns] += jnp.sum(values.reshape(rows // 8, 8, width), 0)


def codes_kernel(
    crops,
    device_crops,
    place,
    sent_ref,
    side_ref,
    prototypes_ref,
    loss_ref,
    proto_grad_ref,
    unit_grad_ref,
    units_ref,
    proto_ref,
    partner_ref,
    codes_ref,
    heat_ref,
    score_ref,
    total_ref,
    scale_ref,
    inverse_ref,
    *,
    factor,
):
    rows_all, width = codes_ref.shape
    own = unit_grad_ref.shape[0]
    chunks = [slice(k, k + LANES) for k in range(0, width, LANES)]
    real = lax.broadcasted_iota(jnp.int32, (1, width), 1) < PROTOS

    dim = units_ref.shape[1]
    for i in range(sent_ref.shape[0]):
        units_ref[i * own : (i + 1) * own, :] = sent_ref[i, :own, :]
    proto_ref[PROTOS // 16 * 16 :, :] = jnp.zeros((width - PROTOS // 16 * 16, dim), jnp.bfloat16)
    proto_ref[:PROTOS, :] = prototypes_ref[...]

    queue_rows = side_ref.shape[0]
    device_rows = queue_rows // (crops // device_crops)
    crop = lax.broadcasted_iota(jnp.int32, (crops, queue_rows), 0)
    holder = crop // device_crops ^ place[1]
    row = lax.broadcasted_iota(jnp.int32, (crops, queue_rows), 1)
    holds = (row == holder * device_rows).astype(jnp.bfloat16)
    found = product(holds, side_ref[:, dim:])
    crop = lax.broadcasted_iota(jnp.int32, found.shape, 0)
    lane = lax.broadcasted_iota(jnp.int32, found.shape, 1)
    here = lane == place[1] * device_crops + crop % device_crops
    partner = jnp.sum(jnp.where(here, found, 0.0), 1, keepdims=True)
    partner_ref[...] = partner.astype(jnp.int32)

    def scores(rows, columns, queue=False):
        left = side_ref[rows, :dim] if queue else units_ref[rows, :]
        return product_bt(left, proto_ref[columns, :])

    def keep(values, columns):
        if columns.stop <= PROTOS:
            return values
        lanes = columns.start + lax.broadcasted_iota(jnp.int32, values.shape, 1)
        return jnp.where(lanes < PROTOS, values, 0.0)

    def fold(values):
        return sum(values[:, k : k + 128] for k in range(0, values.shape[1], 128))

    total_ref[...] = jnp.zeros_like(total_ref)

    for queue, start, count in ((False, 0, crops), (True, crops, queue_rows)):

        def first(i, carry):
            rows = pl.ds(pl.multiple_of(i * 128, 128), 128)
            target = pl.ds(pl.multiple_of(start + i * 128, 128), 128)
            for columns in chunks:
                score = scores(rows, columns, queue)
                powers = keep(jnp.exp(score * (1.0 / SINK_EPS)), columns)
                codes_ref[target, columns] = powers
                add_columns(total_ref, columns, powers)
            return carry

        lax.fori_loop(0, count // 128, first, 0)

    def column_factors(turn):
        total = jnp.sum(total_ref[...], 0, keepdims=True)
        total = jnp.where(real, total, 1.0)
        if turn == 0:
            scale = jnp.where(total > 1e30, 2.0**-64, 1.0)
            scale_ref[...] = jnp.broadcast_to(scale, scale_ref.shape)
            total = total * scale
        inverse_ref[...] = jnp.broadcast_to(1.0 / total, inverse_ref.shape)

    def divided(turn, rows, columns):
        values = codes_ref[rows, columns]
        if turn == 0:
            values = values * scale_ref[0:1, columns]
        return values * inverse_ref[0:1, columns]

    def row_inverse(turn, rows):
        part = sum(fold(divided(turn, rows, columns)) for columns in chunks)
        return 1.0 / jnp.sum(part, 1, keepdims=True)

    for turn in range(SINK_ITERS - 1):
        column_factors(turn)
        total_ref[...] = jnp.zeros_like(total_ref)

        def both(i, carry):
            rows = pl.ds(pl.multiple_of(i * 64, 64), 64)
            inverse = row_inverse(turn, rows)
            for columns in chunks:
                values = divided(turn, rows, columns) * inverse
                codes_ref[rows, columns] = values
                add_columns(total_ref, columns, values)
            return carry

        lax.fori_loop(0, rows_all // 64, both, 0)

    column_factors(SINK_ITERS - 1)
    loss_ref[...] = jnp.zeros_like(loss_ref)
    block = 128

    def last(i, carry):
        rows = pl.ds(pl.multiple_of(i * block, block), block)
        inverse = row_inverse(SINK_ITERS - 1, rows)
        row = lax.broadcasted_iota(jnp.int32, (block, block), 0)
        column = lax.broadcasted_iota(jnp.int32, (block, block), 1)
        pick = (column == (row // CROPS) * CROPS + partner_ref[rows, :]).astype(jnp.bfloat16)
        pick = jnp.concatenate([pick, pick], 1)
        heat_part = jnp.zeros((block, 128), jnp.float32)
        target_part = jnp.zeros((block, 128), jnp.float32)
        loss_part = jnp.zeros((block, 128), jnp.float32)
        for columns in chunks:
            score = scores(rows, columns)
            heat = keep(jnp.exp(score * (1.0 / SOFTMAX_HEAT)), columns)
            heat_ref[:, columns] = heat
            heat_part += fold(heat)
            codes = divided(SINK_ITERS - 1, rows, columns) * inverse
            high = codes.astype(jnp.bfloat16)
            rest = (codes - high.astype(jnp.float32)).astype(jnp.bfloat16)
            target = product(pick, jnp.concatenate([high, rest], 0))
            codes_ref[rows, columns] = target
            target_part += fold(target)
            loss_part += fold(target * score)
        heat_sum = jnp.sum(heat_part, 1, keepdims=True)
        target_sum = jnp.sum(target_part, 1, keepdims=True)
        row_loss = (
            target_sum * jnp.log(heat_sum)
            - jnp.sum(loss_part, 1, keepdims=True) * (1.0 / SOFTMAX_HEAT)
        )
        loss_ref[...] += jnp.broadcast_to(jnp.sum(row_loss, 0, keepdims=True), loss_ref.shape)
        ratio = target_sum / heat_sum * factor
        for columns in chunks:
            grad = heat_ref[:, columns] * ratio - codes_ref[rows, columns] * factor
            score_ref[rows, columns] = grad.astype(jnp.bfloat16)
        return carry

    lax.fori_loop(0, crops // block, last, 0)
    for columns in chunks:
        proto_grad_ref[:, columns] = product_t(units_ref[...], score_ref[:, columns])
    mine = pl.ds(pl.multiple_of(place[0], own), own)
    unit_grad_ref[...] = product(score_ref[mine, :], proto_ref[...])


def gathered_loss(units, side, prototypes, place, own, device_crops, loss_factor_weight):
    crops, dim = units.shape[0] * own, units.shape[2]
    width = -(-PROTOS // LANES) * LANES
    rows_all = crops + side.shape[0]
    f32, bf16 = jnp.float32, jnp.bfloat16
    loss, proto_grad, unit_grad = kernel_call(
        lambda *refs: codes_kernel(
            crops, device_crops, *refs, factor=loss_factor_weight / SOFTMAX_HEAT
        ),
        [((8, 128), f32), ((dim, width), f32, PUT_FAR), ((own, dim), f32)],
        [Scalars(place), units, Loaded(side), Loaded(prototypes)],
        scratch=[
            pltpu.VMEM((crops, dim), bf16),
            pltpu.VMEM((width, dim), bf16),
            pltpu.VMEM((crops, 1), jnp.int32),
            pltpu.VMEM((rows_all, width), f32),
            pltpu.VMEM((128, width), f32),
            pltpu.VMEM((crops, width), bf16),
            pltpu.VMEM((8, width), f32),
            pltpu.VMEM((8, width), f32),
            pltpu.VMEM((8, width), f32),
        ],
        flops=2 * width * (rows_all * dim + 6 * crops * dim),
        transcendentals=width * (rows_all + crops),
        limit=24,
    )
    return loss[0, 0], proto_grad, unit_grad


def sinkhorn(batch_codes, stored_codes, total):
    for turn in range(SINK_ITERS):
        column_totals = total(jnp.sum(batch_codes, 0) + jnp.sum(stored_codes, 0))
        batch_codes = batch_codes / column_totals
        stored_codes = stored_codes / column_totals
        batch_codes = batch_codes / jnp.sum(batch_codes, 1, keepdims=True)
        stored_codes = stored_codes / jnp.sum(stored_codes, 1, keepdims=True)
    return batch_codes


def swapped_loss(scores, codes, pick, loss_factor_weight):
    rows = scores.shape[0]
    target = jnp.einsum(
        "cab,cbk->cak", pick, codes.reshape(rows // CROPS, CROPS, PROTOS), precision=HIGH
    ).reshape(rows, PROTOS)
    log_likelihoods = jax.nn.log_softmax(scores / SOFTMAX_HEAT, axis=1)
    score_grad = (jnp.exp(log_likelihoods) * jnp.sum(target, 1, keepdims=True) - target) * (
        loss_factor_weight / SOFTMAX_HEAT
    )
    return -jnp.sum(target * log_likelihoods), score_grad.astype(jnp.bfloat16)


def per_device(
    canvases,
    crop_map,
    partner,
    queue,
    w_reduce,
    w_spatial,
    w_expand,
    w_hidden,
    w_project,
    norm_mid,
    norm_wide,
    bias_out,
    prototypes,
):
    f32, bf16 = jnp.float32, jnp.bfloat16
    size = lax.axis_size("dp")
    me_dp, me_core = lax.axis_index("dp"), lax.axis_index("shard")
    core = Scalars(me_core.astype(jnp.int32).reshape(1))
    own_canvases = canvases.shape[1]
    canvas_count = 2 * own_canvases
    pixels = SIDE * SIDE
    own_rows = own_canvases * pixels
    local_rows = canvas_count * pixels
    local_crops = canvas_count * CROPS
    pixel_total = float(local_rows * size)
    crop_count = local_crops * size
    crop_total = float(crop_count)
    loss_factor_weight = 1.0 / (MICRO * crop_total)
    crop_ids = jnp.arange(CROPS, dtype=jnp.int32)
    valid = inside_canvas(own_canvases)
    proj = bias_out.shape[0]
    partner_size = partner.size
    copies = copies_of(size)
    by_steps = size == STEPS_DP
    if by_steps:
        slots = relative_slots(size)
        chip_slots = lax.dynamic_slice_in_dim(slots.reshape(size, 2), me_core, 1, 1)[:, 0]

    def both_cores(values):
        mine = lax.dynamic_index_in_dim(values, me_core, 0, keepdims=False)
        other = lax.dynamic_index_in_dim(values, 1 - me_core, 0, keepdims=False)
        return jnp.concatenate([mine, swap_cores(other)], 0)

    def gather_whole(shard):
        return Gathered(lax.all_gather(shard, BOTH, axis=0, tiled=True))

    head_shard = jnp.concatenate([w_hidden, w_project], 1)
    beside = queue.shape[1]
    gathered_codes = (
        crop_count * PROTOS * 4 <= GATHERED_CODES_BYTES
        and queue.shape[0] == w_expand.shape[0]
        and partner_size <= beside
    )
    if gathered_codes:
        partners = jnp.pad(
            partner.astype(bf16).reshape(1, -1),
            ((0, 0), (0, beside - partner_size)),
        )
        partners = jnp.broadcast_to(partners, (queue.shape[0], beside))
        w_expand = jnp.concatenate([w_expand, queue, partners], 1)

    labels = both_cores(jnp.concatenate([crop_map, partner], 2))
    crop_map, partner = labels[:, :pixels], labels[:, pixels:]
    crop_of = jnp.arange(local_crops, dtype=jnp.int32)
    pixel_crop = crop_map + CROPS * jnp.arange(canvas_count, dtype=jnp.int32)[:, None]
    pixel_crop = pixel_crop.reshape(2, own_canvases, pixels).swapaxes(1, 2).reshape(local_rows)
    pool = (crop_of[:, None] == pixel_crop[None, :]).astype(bf16)
    spread = (pixel_crop[:, None] == crop_of[None, :]).astype(bf16)
    crop_sizes = jnp.sum(pool.astype(f32), 1, keepdims=True)

    half_rows = ((own_rows, D), bf16)
    own_x, other_x = kernel_call(
        arrange_kernel,
        [half_rows, half_rows],
        [core, canvases.transpose(0, 2, 3, 1, 4)],
        scratch=[pltpu.VMEM((own_rows, D), f32)],
    )
    input_rows = join([(own_x[None], swap_cores(other_x)[None])])[0].reshape(local_rows, D)

    if by_steps:
        reduce_part = Gathering(w_reduce, size)
        gather_step([reduce_part])
        spatial_part = Gathering(hold(w_spatial, [reduce_part.held]), size)
        gather_step([reduce_part], [pool, spread, crop_sizes, input_rows])
        head_held = lax.all_gather(hold(head_shard, [reduce_part.held]), "dp", axis=0)
        gather_step([reduce_part, spatial_part])
        expand_part = Gathering(hold(w_expand, [spatial_part.held]), size)
        reduce_all = reduce_part.finish(slots)
    else:
        reduce_all = gather_whole(w_reduce)

    mid_rows, wide_rows = ((local_rows, MID), f32), ((local_rows, D), f32)
    mid_sums, wide_sums = ((copies, 2, MID), f32), ((copies, 2, D), f32, PUT_FAR)

    def weight_out(weight):
        return (weight.shape, bf16, FAR)

    pre_one, sums, full_reduce = kernel_call(
        lambda *refs: reduce_kernel(reduce_all.count, *refs),
        [mid_rows, mid_sums, weight_out(reduce_all)],
        [input_rows] + reduce_all.inputs(),
        scratch=reduce_all.scratch() + [pltpu.SemaphoreType.DMA],
        flops=2 * local_rows * D * MID,
    )
    terms_one = terms_over_dp(sums)
    if by_steps:
        gather_step([spatial_part, expand_part], [sums])
        gather_step([spatial_part], [terms_one])
        spatial_all = spatial_part.finish(slots)
    else:
        spatial_all, expand_all = gather_whole(w_spatial), gather_whole(w_expand)

    pre_two, sums, image_patches, full_spatial = kernel_call(
        lambda *refs: spatial_kernel(spatial_all.count, pixel_total, *refs),
        [
            mid_rows,
            mid_sums,
            ((local_rows, 9 * MID), bf16, FAR),
            weight_out(spatial_all),
        ],
        [pre_one, norm_mid, valid, terms_one] + spatial_all.inputs(),
        scratch=[
            pltpu.VMEM((local_rows + 2 * EDGE, MID), f32),
            pltpu.VMEM((local_rows, 9 * MID), bf16),
            pltpu.SemaphoreType.DMA,
        ]
        + spatial_all.scratch()
        + [pltpu.SemaphoreType.DMA],
        flops=2 * local_rows * 9 * MID * MID,
    )
    terms_two = terms_over_dp(sums)
    if by_steps:
        gather_step([expand_part], [sums])
        gather_step([expand_part], [terms_two])
        expand_all = expand_part.finish(slots)

    side = ((expand_all.shape[0], max(expand_all.shape[1] - D, 128)), bf16, PUT_FAR)
    act_two, pre_three, sums, full_expand, side = kernel_call(
        lambda *refs: expand_kernel(expand_all.count, pixel_total, *refs),
        [
            ((local_rows, MID), bf16, PUT_FAR),
            wide_rows,
            wide_sums,
            weight_out(expand_all),
            side,
        ],
        [pre_two, norm_mid, terms_two] + expand_all.inputs(),
        scratch=expand_all.scratch() + [pltpu.SemaphoreType.DMA],
        flops=2 * local_rows * D * MID,
    )
    terms_three = terms_over_dp(sums)
    if by_steps:
        head_held, _ = lax.optimization_barrier((head_held, sums))
        head = other_core_dp(head_held, size)
    else:
        head = gather_whole(head_shard)

    crop_rows = ((local_crops, D), f32, PUT_FAR)
    pooled_low, pre_head, sums, full_project = kernel_call(
        lambda *refs: pool_kernel(head.count, pixel_total, *refs),
        [
            ((local_crops, D), bf16, PUT_FAR),
            crop_rows,
            wide_sums,
            ((D, proj), bf16, PUT_FAR),
        ],
        [
            pre_three,
            input_rows,
            Loaded(norm_wide),
            Loaded(pool),
            Loaded(crop_sizes),
            terms_three,
        ]
        + head.inputs(),
        scratch=[pltpu.VMEM((local_rows, 256), bf16), pltpu.VMEM((local_rows, 256), bf16)]
        + head.scratch(CHUNKS),
        flops=2 * local_crops * D * D,
        transcendentals=local_rows * D,
    )
    terms_head = terms_over_dp(sums)

    embed_rows = ((local_crops, proj), f32)
    send_pooled = gathered_codes and copies * proj == D
    act_head, unit_embed, inv_length, unit_low = kernel_call(
        lambda *refs: embed_kernel(crop_total, *refs),
        [
            ((local_crops, D), bf16),
            embed_rows,
            embed_rows,
            ((copies, local_crops * (2 if send_pooled else 1), proj), bf16, PUT_FAR),
        ],
        [
            Loaded(pre_head),
            Loaded(norm_wide),
            Streamed(full_project),
            Loaded(bias_out.reshape(1, proj)),
            Streamed(pooled_low),
            terms_head,
        ],
        flops=2 * local_crops * D * proj,
    )

    if gathered_codes:
        all_units = lax.all_to_all(unit_low, "dp", 0, 0)
        loss_part, proto_part, unit_grad = gathered_loss(
            all_units,
            side,
            prototypes,
            jnp.stack([me_dp * local_crops, me_core]).astype(jnp.int32),
            local_crops,
            own_canvases * CROPS,
            loss_factor_weight,
        )
    else:
        chip_queue = jnp.concatenate([queue, swap_cores(queue)], 0)
        queue_codes = jnp.exp(product_bt(chip_queue, prototypes) / SINK_EPS)
        pick = (partner[:, :, None] == crop_ids[None, None, :]).astype(f32)
        all_units = unit_low
        scores = product_bt(unit_low[0], prototypes)
        codes = sinkhorn(
            jnp.exp(scores / SINK_EPS), queue_codes, lambda sums: lax.psum(sums, "dp")
        )
        loss_part, score_low = swapped_loss(scores, codes, pick, loss_factor_weight)
        proto_part, loss_part = lax.psum((product_t(unit_low[0], score_low), loss_part), "dp")
        unit_grad = product(score_low, prototypes)

    embed_low, head_act_grad, sums, bias_part = kernel_call(
        lambda *refs: embed_back_kernel(crop_total, *refs),
        [((local_crops, proj), bf16), crop_rows, wide_sums, ((1, proj), f32)],
        [
            unit_grad,
            unit_embed,
            inv_length,
            Streamed(full_project),
            Streamed(pre_head),
            Loaded(norm_wide),
            terms_head,
        ],
        flops=2 * local_crops * D * proj,
    )
    back_head = terms_over_dp(sums)

    chip_rows = 2 * w_hidden.shape[0]
    if send_pooled:
        left = all_units[:, local_crops:].reshape(crop_count, chip_rows)
    else:
        left = lax.all_gather(pooled_low, "dp", axis=0, tiled=True)
        left = lax.dynamic_slice_in_dim(left, me_dp * chip_rows, chip_rows, 1)

    own_part = ((own_rows, D), f32)
    head_low, own_grad, other_grad, sums, total_head = kernel_call(
        lambda *refs: pool_back_kernel(head.count, crop_total, pixel_total, *refs),
        [((local_crops, D), bf16), own_part, own_part, wide_sums, ((2, D), f32)],
        [
            Loaded(head_act_grad),
            Loaded(pre_head),
            Streamed(pre_three),
            Streamed(input_rows),
            Loaded(norm_wide),
            Loaded(spread),
            Loaded(crop_sizes),
            terms_head,
            back_head,
            terms_three,
        ]
        + head.inputs(),
        scratch=head.scratch(CHUNKS),
        flops=2 * local_crops * D * D,
        transcendentals=local_rows * D,
    )
    back_three = terms_over_dp(sums)
    other_grad, _ = lax.optimization_barrier((other_grad, back_three))
    peer_grad = swap_cores(other_grad)

    right = lax.all_gather(head_low, "dp", axis=0, tiled=True)

    def low_halves(width):
        return [((local_rows, width // 2), bf16)] * 2

    three_kept, three_sent, two_act_grad, sums, total_three = kernel_call(
        lambda *refs: expand_back_kernel(pixel_total, *refs),
        [*low_halves(D), mid_rows, ((copies, 2, MID + proj), f32), ((2, D), f32)],
        [
            core,
            own_grad,
            other_grad,
            Streamed(pre_three),
            norm_wide,
            Streamed(full_expand),
            Streamed(pre_two),
            norm_mid,
            bias_part,
            terms_three,
            back_three,
            terms_two,
        ],
        scratch=[pltpu.VMEM((local_rows, D), bf16)],
        flops=2 * local_rows * D * MID,
    )
    back_two = terms_over_dp(sums)
    before_two = []
    if by_steps:
        expand_sum = weight_grad(
            (act_two, swap_cores(act_two)),
            (three_kept, swap_cores(three_sent)),
            chip_slots,
            size,
            (
                (act_head, swap_cores(act_head)),
                (embed_low, swap_cores(embed_low)),
                core,
            ),
            after=[sums],
        )
        before_two = [expand_sum.kept]

    two_kept, two_sent, one_act_grad, sums, total_two = kernel_call(
        lambda *refs: spatial_back_kernel(pixel_total, *refs),
        [*low_halves(MID), mid_rows, mid_sums, ((2, MID + proj), f32)],
        [
            core,
            two_act_grad,
            Streamed(pre_two),
            norm_mid,
            Streamed(full_spatial),
            Streamed(pre_one),
            valid,
            terms_two,
            back_two,
            terms_one,
        ],
        scratch=[
            pltpu.VMEM((9, local_rows + 2 * EDGE, MID), f32),
            pltpu.VMEM((local_rows, MID), bf16),
        ],
        flops=2 * local_rows * 9 * MID * MID,
        after=before_two,
    )
    before_one = []
    if by_steps:
        spatial_sum = weight_grad(
            (image_patches, swap_cores(image_patches)),
            (two_kept, swap_cores(two_sent)),
            chip_slots,
            size,
        )
        spatial_sum.first(two_kept)
        sums, _ = lax.optimization_barrier((sums, spatial_sum.kept))

    back_one = terms_over_dp(sums)
    one_low, other_low, one_kept, one_sent, total_one = kernel_call(
        lambda *refs: reduce_back_kernel(pixel_total, *refs),
        [
            ((local_rows, MID), bf16),
            ((own_rows, MID), bf16),
            *low_halves(MID),
            ((2, MID), f32),
        ],
        [core, one_act_grad, Streamed(pre_one), norm_mid, terms_one, back_one],
        after=before_one,
    )
    if by_steps:
        expand_sum.first(back_one)
        spatial_sum.second([one_low])
        expand_sum.second([spatial_sum.kept])
        reduce_sum = weight_grad(
            (input_rows, swap_cores(input_rows)),
            (one_kept, swap_cores(one_sent)),
            chip_slots,
            size,
            after=[expand_sum.kept, right],
        )

    proto_other = swap_cores(proto_part)
    other_low = swap_cores(other_low)
    late = []
    if by_steps:
        reduce_sum.first(one_low)
        expand_sum.third([reduce_sum.kept])
        spatial_sum.third([expand_sum.kept])
        reduce_sum.second([spatial_sum.kept])
        late = [reduce_sum.kept]
    by_pixel = kernel_call(
        input_grad_kernel,
        [((MICRO, SIDE, SIDE, own_canvases, D), f32)],
        [core, own_grad, peer_grad, one_low, other_low, full_reduce],
        scratch=[pltpu.VMEM((own_rows, D), f32)],
        flops=2 * local_rows * D * MID,
        after=late,
    )[0]
    if by_steps:
        reduce_sum.third([by_pixel])
        late = [reduce_sum.kept]
    left, right, _ = lax.optimization_barrier((left, right, late))
    if gathered_codes:
        proto_grad = kernel_call(
            proto_grad_kernel,
            [(prototypes.shape, f32)],
            [Loaded(proto_part), Loaded(proto_other)],
            after=late,
        )[0]
    else:
        proto_grad = (proto_part + proto_other).T
    hidden_part = product_t(left, right)

    def own_half(part):
        half = chip_rows // 2
        mine = lax.dynamic_slice_in_dim(part, me_core * half, half, 0)
        other = lax.dynamic_slice_in_dim(part, (1 - me_core) * half, half, 0)
        return mine + swap_cores(other)

    grad_hidden = own_half(hidden_part)
    if by_steps:
        grad_spatial, grad_reduce = swap_columns(spatial_sum.finish(), reduce_sum.finish())
        total = expand_sum.finish()
        (grad_expand,) = swap_columns(total[:, : D // 2])
        grad_project = jnp.concatenate(
            [total[:, k : k + proj] for k in range(D // 2, total.shape[1], proj)], 0
        )
    else:

        def scatter(first, kept, sent):
            lows = jnp.concatenate(
                [jnp.where(me_core == 0, kept, sent), jnp.where(me_core == 0, sent, kept)], 1
            )
            return lax.psum_scatter(
                product_t(first, lows), BOTH, scatter_dimension=0, tiled=True
            )

        grad_reduce = scatter(input_rows, one_kept, one_sent)
        grad_spatial = scatter(image_patches, two_kept, two_sent)
        grad_expand = scatter(act_two, three_kept, three_sent)
        grad_project = lax.psum_scatter(
            product_t(act_head, embed_low), BOTH, scatter_dimension=0, tiled=True
        )

    totals = (total_one, total_two, total_three, total_head)
    (total_one, total_two, total_three, total_head), _ = lax.optimization_barrier((totals, late))
    narrow = jnp.concatenate(
        [
            jnp.stack([total_one[1], total_one[0], total_two[1, :MID], total_two[0, :MID]])
            .reshape(-1),
            jnp.stack([total_three[1], total_three[0], total_head[1], total_head[0]]).reshape(-1),
            total_two[0, MID:],
            jnp.broadcast_to(loss_part, (128,)),
        ]
    )
    narrow = narrow + swap_cores(narrow)
    mid_end, wide_end = norm_mid.size, norm_mid.size + norm_wide.size
    bias_end = wide_end + proj
    return (
        narrow[bias_end] * loss_factor_weight,
        by_pixel.transpose(0, 3, 1, 2, 4),
        grad_reduce,
        grad_spatial,
        grad_expand,
        grad_hidden,
        grad_project,
        narrow[:mid_end].reshape(norm_mid.shape),
        narrow[mid_end:wide_end].reshape(norm_wide.shape),
        narrow[wide_end:bias_end],
        proto_grad,
    )


def solution(mesh):
    return jax.shard_map(
        per_device,
        mesh=mesh,
        in_specs=(
            P(None, ("dp", "shard"), None, None, None),
            P(None, ("dp", "shard"), None),
            P(None, ("dp", "shard"), None),
            P(("dp", "shard"), None),
            P(("dp", "shard"), None),
            P(("dp", "shard"), None),
            P(("dp", "shard"), None),
            P(("dp", "shard"), None),
            P(("dp", "shard"), None),
            P(),
            P(),
            P(),
            P(),
        ),
        out_specs=(
            P(),
            P(None, ("dp", "shard"), None, None, None),
            P(("dp", "shard"), None),
            P(("dp", "shard"), None),
            P(("dp", "shard"), None),
            P(("dp", "shard"), None),
            P(("dp", "shard"), None),
            P(),
            P(),
            P(),
            P(),
        ),
        check_vma=False,
    )
```

```python
import dataclasses

import jax
import jax.numpy as jnp
import numpy as np
from jax import lax
from jax.experimental import pallas as pl
from jax.experimental.pallas import tpu as pltpu
from jax.sharding import PartitionSpec as P

D = 2048
MID = 512
PROTOS = 3000
SIDE = 6
CROPS = 4
SINK_ITERS = 3
MICRO = 2


EPS_NORM = 1e-05
EPS_UNIT = 1e-06
SOFTMAX_HEAT = 0.1
SINK_EPS = 0.05
HIGH = lax.Precision.HIGHEST
BOTH = ("dp", "shard")
GATHERED_CODES_BYTES = 32 * 2**20
MIB = 2**20
LANES = 512
CHUNKS = 4


def product(left, right):
    return jnp.dot(left, right, preferred_element_type=jnp.float32)


def product_t(left, right):
    return lax.dot_general(
        left, right, (((0,), (0,)), ((), ())), preferred_element_type=jnp.float32
    )


def product_bt(left, right):
    return lax.dot_general(
        left, right, (((1,), (1,)), ((), ())), preferred_element_type=jnp.float32
    )


def silu_slope(values):
    sigmoid_value = jax.nn.sigmoid(values)
    return sigmoid_value * (1.0 + values * (1.0 - sigmoid_value))


@dataclasses.dataclass
class Scalars:
    array: jax.Array


@dataclasses.dataclass
class Left:
    array: jax.Array


@dataclasses.dataclass
class Loaded:
    array: jax.Array


@dataclasses.dataclass
class Streamed:
    array: jax.Array


class Arriving:
    def __init__(self, ref, copy):
        self.ref, self.copy = ref, copy
        self.shape = ref.shape

    def __getitem__(self, index):
        if self.copy is not None:
            self.copy.wait()
            self.copy = None
        return self.ref[index]


FAR, PUT_FAR = "far", "put far"


def kernel_call(body, outs, args, scratch=(), flops=0, transcendentals=0, limit=17, after=()):
    spaces = {Scalars: pltpu.SMEM, Left: pltpu.HBM, Streamed: pltpu.HBM}
    in_spaces = [spaces.get(type(a), pltpu.VMEM) for a in args] + [pltpu.HBM] * len(after)
    after = [pltpu.with_memory_space_constraint(a, pltpu.HBM) for a in after]
    arrays = []
    for a in args:
        if isinstance(a, (Left, Loaded, Streamed)):
            a = pltpu.with_memory_space_constraint(a.array, pltpu.HBM)
        arrays.append(a.array if isinstance(a, Scalars) else a)
    used = len(arrays)
    out_spaces = [pltpu.HBM if FAR in out else pltpu.VMEM for out in outs]

    streamed = [i for i, a in enumerate(args) if isinstance(a, Streamed)]
    scratch = list(scratch)
    own_scratch = len(scratch)
    for i in streamed:
        scratch += [pltpu.VMEM(arrays[i].shape, arrays[i].dtype), pltpu.SemaphoreType.DMA]

    def kernel(*refs):
        inputs, refs = list(refs[:used]), refs[used + len(after) :]
        mine = len(outs) + own_scratch
        for k, i in enumerate(streamed):
            buffer, sem = refs[mine + 2 * k : mine + 2 * k + 2]
            copy = pltpu.make_async_copy(inputs[i], buffer, sem)
            copy.start()
            inputs[i] = Arriving(buffer, copy)
        body(*inputs, *refs[:mine])

    moved = sum(a.size * a.dtype.itemsize for a in arrays)
    return pl.pallas_call(
        kernel,
        out_shape=[
            jax.ShapeDtypeStruct(*out) if len(out) == 2 else pltpu.HBM(*out[:2]) for out in outs
        ],
        in_specs=[pl.BlockSpec(memory_space=space) for space in in_spaces],
        out_specs=[pl.BlockSpec(memory_space=space) for space in out_spaces],
        scratch_shapes=list(scratch),
        compiler_params=pltpu.CompilerParams(vmem_limit_bytes=limit * MIB),
        cost_estimate=pl.CostEstimate(
            flops=int(flops), bytes_accessed=int(moved), transcendentals=int(transcendentals)
        ),
    )(*arrays, *after)


def join_kernel(counts, *refs):
    outs = refs[sum(counts) :]
    start = 0
    for count, joined in zip(counts, outs):
        parts = refs[start : start + count]
        start += count
        length = parts[0].shape[0]

        def move(i, carry):
            for k, part in enumerate(parts):
                joined[i + k * length] = part[i]
            return carry

        lax.fori_loop(0, length, move, 0)


def join(groups, after=()):
    counts = [len(group) for group in groups]
    outs = [
        ((len(group) * group[0].shape[0],) + group[0].shape[1:], group[0].dtype)
        for group in groups
    ]
    return kernel_call(
        lambda *refs: join_kernel(counts, *refs),
        outs,
        [part for group in groups for part in group],
        after=after,
    )


def hold_kernel(source, target):
    target[...] = source[...]


def hold(values, after=()):
    return kernel_call(hold_kernel, [(values.shape, values.dtype)], [values], after=after)[0]


def add_parts_kernel(kept, received, *totals):
    length = totals[0].shape[0]

    def move(i, carry):
        for k, out_ref in enumerate(totals):
            place = i + k * length
            total = kept[place].astype(jnp.float32) + received[place].astype(jnp.float32)
            out_ref[i] = total.astype(out_ref.dtype)
        return carry

    lax.fori_loop(0, length, move, 0)


def add_parts(kept, received, count, after=()):
    shape = (kept.shape[0] // count,) + kept.shape[1:]
    kept, *sent = kernel_call(
        add_parts_kernel,
        [(shape, jnp.float32, PUT_FAR)] + [(shape, jnp.bfloat16, PUT_FAR)] * (count - 1),
        [Loaded(kept), received],
        after=after,
    )
    return kept, sent


def swap_cores(values):
    return lax.ppermute(values, "shard", [(0, 1), (1, 0)])


def flip_dp(values, bits, size):
    return lax.ppermute(values, "dp", [(i, i ^ bits) for i in range(size)])


def flip_both(values, dp_bits, size):
    pairs = [(2 * i + c, 2 * (i ^ dp_bits[c]) + c) for i in range(size) for c in range(2)]
    return lax.ppermute(values, BOTH, pairs)


def copies_of(size):
    return size if size <= STEPS_DP else 1


def terms_over_dp(copies):
    if copies.shape[0] > 1:
        return lax.all_to_all(copies, "dp", 0, 0)
    return lax.psum(copies, "dp")


Z_BITS = (8, 4, 12)
XY_BITS = ((2, 1), (1, 2))
STEPS_DP = 16


def relative_slots(size):
    me_dp, me_core = lax.axis_index("dp"), lax.axis_index("shard")
    device = jnp.arange(2 * size, dtype=jnp.int32)
    apart_dp, apart_core = (device // 2) ^ me_dp, (device % 2) ^ me_core
    holder = device % 2
    on = lambda bit: jnp.where((apart_dp & bit) != 0, 1, 0)
    low, high = (jnp.where(holder == 0, on(zero), on(one)) for zero, one in XY_BITS)
    slot = on(Z_BITS[0]) + 2 * on(Z_BITS[1]) + 4 * low + 8 * high + size * apart_core
    return slot.astype(jnp.int32)


class Gathering:
    def __init__(self, shard, size):
        self.size = size
        self.held = shard[None]
        self.step = 0

    def send(self):
        step, held = self.step, self.held
        self.step += 1
        if step == 0:
            return [held] + [flip_dp(held, bits, self.size) for bits in Z_BITS]
        return [held, flip_both(held, XY_BITS[step - 1], self.size)]

    def finish(self, slots):
        return Gathered(self.held, swap_cores(self.held), slots)


def gather_step(parts, after=()):
    joined = join([part.send() for part in parts], after)
    for part, held in zip(parts, joined):
        part.held = held


def other_core_dp(held, size):
    device = jnp.arange(2 * size, dtype=jnp.int32)
    other = (device % 2) != lax.axis_index("shard")
    slots = jnp.where(other, size, 0) + device // 2
    return Gathered(held, swap_cores(held), slots.astype(jnp.int32))


class Scattering:
    def __init__(self, kept, sent, size):
        self.size = size
        self.kept, self.sent = kept, sent

    def first(self, before):
        sent, _ = lax.optimization_barrier((self.sent, before))
        self.received = flip_both(sent, XY_BITS[1], self.size)

    def second(self, after=()):
        self.kept, sent = add_parts(self.kept, self.received, 2, after)
        self.received = flip_both(sent[0], XY_BITS[0], self.size)

    def third(self, after=()):
        self.kept, sent = add_parts(self.kept, self.received, 4, after)
        self.received = [flip_dp(part, bits, self.size) for part, bits in zip(sent, Z_BITS)]

    def finish(self):
        one, two, three = (part[0].astype(jnp.float32) for part in self.received)
        return (self.kept[0] + one) + (two + three)


@dataclasses.dataclass
class Gathered:
    held: jax.Array
    other: jax.Array | None = None
    slots: jax.Array | None = None

    @property
    def count(self):
        return 1 if self.other is None else 3

    @property
    def shape(self):
        if self.other is None:
            return self.held.shape
        half, rows, width = self.held.shape
        return (2 * half * rows, width)

    def inputs(self):
        if self.other is None:
            return [Left(self.held)]
        return [Scalars(self.slots), Left(self.held), Left(self.other)]

    def scratch(self, chunks=1):
        copies = chunks if self.other is None else 2 * self.held.shape[0]
        return [pltpu.VMEM(self.shape, jnp.bfloat16), pltpu.SemaphoreType.DMA((copies,))]


def fetch_weight(inputs, weight, sems, chunks=1):
    count = sems.shape[0]
    rows = weight.shape[0] // count
    each = count // chunks

    def copy(source, i):
        target = weight.at[pl.ds(pl.multiple_of(i * rows, rows), rows)]
        return pltpu.make_async_copy(source, target, sems.at[i])

    if len(inputs) == 1:
        copies = [copy(inputs[0].at[pl.ds(i * rows, rows)], i) for i in range(count)]
        for one in copies:
            one.start()

        def wait_ordered(chunk):
            for one in copies[chunk * each : (chunk + 1) * each]:
                one.wait()

        return wait_ordered

    table, held, other = inputs
    half = held.shape[0]

    def begin(i, carry):
        slot = table[i]

        @pl.when(slot < half)
        def _():
            copy(held.at[slot], i).start()

        @pl.when(slot >= half)
        def _():
            copy(other.at[slot - half], i).start()

        return carry

    lax.fori_loop(0, count, begin, 0)

    def wait(chunk):
        def finish(i, carry):
            copy(held.at[0], i).wait()
            return carry

        lax.fori_loop(chunk * each, (chunk + 1) * each, finish, 0)

    return wait


def weight_grad_kernel(beside, table, *refs):
    left, left_peer, right, right_peer = refs[:4]
    if beside:
        second, second_peer, second_right, second_right_peer, core = refs[4:9]
        kept_ref, sent_ref, total_ref, second_ref = refs[9:]
    else:
        kept_ref, sent_ref, total_ref = refs[4:]
    half, rows, _ = kept_ref.shape
    width = right.shape[1]
    for k in range(0, total_ref.shape[0], 512):
        total_ref[k : k + 512, :] = product_t(left[:, k : k + 512], right[...]) + product_t(
            left_peer[:, k : k + 512], right_peer[...]
        )
    if beside:
        second_ref[...] = product_t(second[...], second_right[...]) + product_t(
            second_peer[...], second_right_peer[...]
        )

    def place(out_ref, slot, i):
        found = total_ref[pl.ds(pl.multiple_of(i * rows, rows), rows), :]
        out_ref[slot, :, :width] = found.astype(out_ref.dtype)
        for part in range(beside):
            start = ((2 * i + core[0]) * beside + part) * rows
            across = second_ref.shape[1]
            columns = slice(width + part * across, width + (part + 1) * across)
            found = second_ref[pl.ds(pl.multiple_of(start, rows), rows), :]
            out_ref[slot, :, columns] = found.astype(out_ref.dtype)

    def move(i, carry):
        slot = table[i]

        @pl.when(slot < half)
        def _():
            place(kept_ref, slot, i)

        @pl.when(slot >= half)
        def _():
            place(sent_ref, slot - half, i)

        return carry

    lax.fori_loop(0, 2 * half, move, 0)


def weight_grad(left, right, slots, size, second=None, after=()):
    depth, width = left[0].shape[1], right[0].shape[1]
    rows = depth // size
    args = [Scalars(slots), *left, Loaded(right[0]), right[1]]
    scratch, beside, extra = [pltpu.VMEM((depth, width), jnp.float32)], 0, 0
    if second is not None:
        (second_left, second_right, core) = second
        args += [*second_left, *second_right, core]
        second_shape = (second_left[0].shape[1], second_right[0].shape[1])
        beside = second_shape[0] // (2 * depth)
        extra = beside * second_shape[1]
        scratch.append(pltpu.VMEM(second_shape, jnp.float32))
    shape = (size // 2, rows, width + extra)
    kept, sent = kernel_call(
        lambda *refs: weight_grad_kernel(beside, *refs),
        [(shape, jnp.float32, PUT_FAR), (shape, jnp.bfloat16, PUT_FAR)],
        args,
        scratch=scratch,
        flops=4 * left[0].shape[0] * depth * width,
        after=after,
    )
    return Scattering(kept, sent, size)


def swap_columns(*totals):
    me = lax.axis_index("shard")

    def half_of(core):
        halves = [total.shape[0] // 2 for total in totals]
        return jnp.concatenate(
            [
                lax.dynamic_slice_in_dim(total, core * half, half, 0)
                for total, half in zip(totals, halves)
            ]
        )

    mine, other = half_of(me), swap_cores(half_of(1 - me))
    first, second = jnp.where(me == 0, mine, other), jnp.where(me == 0, other, mine)
    both, found, start = jnp.concatenate([first, second], 1), [], 0
    for total in totals:
        found.append(both[start : start + total.shape[0] // 2])
        start += total.shape[0] // 2
    return found


def tiles(rows, width, high, wide):
    for r in range(0, rows, high):
        for k in range(0, width, wide):
            yield slice(r, r + high), slice(k, k + wide)


def norm_factors(terms, norm_ref, row, count):
    totals = jnp.sum(terms[...], 0)
    average = totals[0:1] / count
    inverse = lax.rsqrt(totals[1:2] / count - average * average + EPS_NORM)
    return average, inverse, norm_ref[row : row + 1, :], norm_ref[row + 1 : row + 2, :]


def normalize(values, factors, columns):
    average, inverse, gain, shift = (part[:, columns] for part in factors)
    unit = (values - average) * inverse
    return unit, gain * unit + shift


def silu(values):
    return values * jax.nn.sigmoid(values)


def norm_backward(grad, unit, factors, totals, count, columns):
    _, inverse, gain, _ = (part[:, columns] for part in factors)
    mean_grad = totals[0:1, columns] / count
    mean_product = totals[1:2, columns] / count
    return gain * inverse * (grad - mean_grad - unit * mean_product)


class Sums:
    def __init__(self, out_ref):
        self.out_ref = out_ref
        self.parts = {}

    def add(self, columns, first, second):
        key = (columns.start, columns.stop)
        fold = lambda v: jnp.sum(v.reshape(v.shape[0] // 8, 8, v.shape[1]), 0)
        first, second = fold(first), fold(second)
        if key in self.parts:
            first, second = self.parts[key][0] + first, self.parts[key][1] + second
        self.parts[key] = (first, second)

    def store(self):
        for (start, stop), (first, second) in self.parts.items():
            first = jnp.sum(first, 0, keepdims=True)
            second = jnp.sum(second, 0, keepdims=True)
            both = jnp.concatenate([first, second], 0).astype(self.out_ref.dtype)
            for copy in range(self.out_ref.shape[0]):
                self.out_ref[copy, :, start:stop] = both


def reduce_kernel(weights, x_ref, *refs):
    inputs, refs = refs[:weights], refs[weights:]
    pre_ref, sums_ref, weight_out, weight, sems, out_sem = refs
    fetch_weight(inputs, weight, sems)(0)
    copy_out = pltpu.make_async_copy(weight, weight_out, out_sem)
    copy_out.start()
    sums = Sums(sums_ref)
    for columns in (slice(k, k + 256) for k in range(0, MID, 256)):
        pre = product(x_ref[...], weight[:, columns])
        pre_ref[:, columns] = pre
        sums.add(columns, pre, pre * pre)
    sums.store()
    copy_out.wait()


def spatial_kernel(weights, count, pre_ref, norm_ref, valid_ref, *refs):
    term_refs, *refs = refs
    inputs, refs = refs[:weights], refs[weights:]
    out_ref, sums_ref, patches_out, weight_out, padded, patches, sem, weight, sems, out_sem = refs
    wait = fetch_weight(inputs, weight, sems)
    rows = pre_ref.shape[0]
    factors = norm_factors(term_refs, norm_ref, 0, count)
    edge = jnp.zeros((EDGE, MID), jnp.float32)
    padded[0:EDGE, :] = edge
    padded[EDGE + rows :, :] = edge
    for high, columns in tiles(rows, MID, 48, 512):
        _, shifted = normalize(pre_ref[high, columns], factors, columns)
        low = silu(shifted).astype(jnp.bfloat16)
        padded[EDGE + high.start : EDGE + high.stop, columns] = low.astype(jnp.float32)
    for place in range(9):
        offset = EDGE + neighbour(place, rows // (2 * SIDE * SIDE))
        for high, columns in tiles(rows, MID, 48, 512):
            values = padded[offset + high.start : offset + high.stop, columns]
            values = values * valid_ref[high, place : place + 1]
            patches[high, place * MID : (place + 1) * MID] = values.astype(jnp.bfloat16)
    copy = pltpu.make_async_copy(patches, patches_out, sem)
    copy.start()
    wait(0)
    copy_out = pltpu.make_async_copy(weight, weight_out, out_sem)
    copy_out.start()
    sums = Sums(sums_ref)
    for columns in (slice(k, k + 256) for k in range(0, MID, 256)):
        pre = product(patches[...], weight[:, columns])
        out_ref[:, columns] = pre
        sums.add(columns, pre, pre * pre)
    sums.store()
    copy.wait()
    copy_out.wait()


def expand_kernel(weights, count, pre_ref, norm_ref, *refs):
    term_refs, *refs = refs
    inputs, refs = refs[:weights], refs[weights:]
    act_ref, out_ref, sums_ref, weight_out, side_ref, weight, sems, out_sem = refs
    wait = fetch_weight(inputs, weight, sems)
    factors = norm_factors(term_refs, norm_ref, 2, count)
    for high, columns in tiles(pre_ref.shape[0], MID, 48, 512):
        _, shifted = normalize(pre_ref[high, columns], factors, columns)
        act_ref[high, columns] = silu(shifted).astype(jnp.bfloat16)
    wait(0)
    copy_out = pltpu.make_async_copy(weight, weight_out, out_sem)
    copy_out.start()
    if weight.shape[1] > D:
        side_ref[...] = weight[:, D:]
    else:
        side_ref[...] = jnp.zeros_like(side_ref)
    sums = Sums(sums_ref)
    for columns in (slice(k, k + 256) for k in range(0, D, 256)):
        pre = product(act_ref[...], weight[:, columns])
        out_ref[:, columns] = pre
        sums.add(columns, pre, pre * pre)
    sums.store()
    copy_out.wait()


def split(values):
    high = values.astype(jnp.bfloat16)
    return high, (values - high.astype(jnp.float32)).astype(jnp.bfloat16)


def pool_kernel(weights, count, pre_ref, x_ref, norm_ref, pool_ref, size_ref, *refs):
    term_refs, *refs = refs
    inputs, refs = refs[:weights], refs[weights:]
    pooled_ref, out_ref, sums_ref, project_ref, high_ref, rest_ref, weight, sems = refs
    wait = fetch_weight(inputs, weight, sems, CHUNKS)
    factors = norm_factors(term_refs, norm_ref, 0, count)
    rows = pre_ref.shape[0]
    for k in range(0, D, 256):
        for high, columns in tiles(rows, 256, 96, 256):
            across = slice(k + columns.start, k + columns.stop)
            _, shifted = normalize(pre_ref[high, across], factors, across)
            block = silu(shifted + x_ref[high, across].astype(jnp.float32))
            high_ref[high, columns], rest_ref[high, columns] = split(block)
        pooled = product(pool_ref[...], high_ref[...]) + product(pool_ref[...], rest_ref[...])
        pooled_ref[:, k : k + 256] = (pooled / size_ref[...]).astype(jnp.bfloat16)
    step = D // CHUNKS
    total = 0.0
    for chunk in range(CHUNKS):
        wait(chunk)
        part = slice(chunk * step, (chunk + 1) * step)
        total = total + product(pooled_ref[:, part], weight[part, :D])
    out_ref[...] = total
    project_ref[...] = weight[:, D:]
    sums = Sums(sums_ref)
    for columns in (slice(k, k + 512) for k in range(0, D, 512)):
        pre = out_ref[:, columns]
        sums.add(columns, pre, pre * pre)
    sums.store()


def embed_kernel(count, pre_ref, norm_ref, project_ref, bias_ref, pooled_ref, *refs):
    term_refs, *refs = refs
    act_ref, unit_ref, inverse_ref, low_ref = refs
    factors = norm_factors(term_refs, norm_ref, 2, count)
    for high, columns in tiles(pre_ref.shape[0], D, pre_ref.shape[0], 512):
        _, shifted = normalize(pre_ref[high, columns], factors, columns)
        act_ref[high, columns] = silu(shifted).astype(jnp.bfloat16)
    embed = product(act_ref[...], project_ref[...]) + bias_ref[...]
    inverse = lax.rsqrt(jnp.sum(embed * embed, 1, keepdims=True) + EPS_UNIT)
    unit = embed * inverse
    unit_ref[...] = unit
    inverse_ref[...] = jnp.broadcast_to(inverse, inverse_ref.shape)
    low = unit.astype(jnp.bfloat16)
    copies, rows, _ = low_ref.shape
    crops = low.shape[0]
    for copy in range(copies):
        low_ref[copy, :crops, :] = low
        if rows > crops:
            width = D // copies
            low_ref[copy, crops:, :] = pooled_ref[:, copy * width : (copy + 1) * width]


def embed_back_kernel(
    count, grad_ref, unit_ref, inverse_ref, project_ref, pre_ref, norm_ref, *refs
):
    term_refs, *refs = refs
    low_ref, out_ref, sums_ref, bias_ref = refs
    grad, unit = grad_ref[...], unit_ref[...]
    embed_grad = inverse_ref[...] * (grad - unit * jnp.sum(grad * unit, 1, keepdims=True))
    low_ref[...] = embed_grad.astype(jnp.bfloat16)
    bias_ref[...] = jnp.sum(embed_grad, 0, keepdims=True)
    factors = norm_factors(term_refs, norm_ref, 2, count)
    sums = Sums(sums_ref)
    for columns in (slice(k, k + 512) for k in range(0, D, 512)):
        back = product_bt(low_ref[...], project_ref[columns, :])
        head_unit, shifted = normalize(pre_ref[:, columns], factors, columns)
        back = back * silu_slope(shifted)
        out_ref[:, columns] = back
        sums.add(columns, back, back * head_unit)
    sums.store()


def pool_back_kernel(
    weights,
    crop_count,
    count,
    grad_ref,
    head_pre_ref,
    pre_ref,
    x_ref,
    norm_ref,
    spread_ref,
    size_ref,
    *refs,
):
    head_terms, head_back, pre_terms, *refs = refs
    inputs, refs = refs[:weights], refs[weights:]
    low_ref, own_ref, other_ref, sums_ref, total_ref, weight, sems = refs
    wait = fetch_weight(inputs, weight, sems, CHUNKS)
    step = D // CHUNKS
    head_factors = norm_factors(head_terms, norm_ref, 2, crop_count)
    totals = jnp.sum(head_back[...].astype(jnp.float32), 0)
    total_ref[...] = totals
    for columns in (slice(k, k + 512) for k in range(0, D, 512)):
        unit, _ = normalize(head_pre_ref[:, columns], head_factors, columns)
        grad = norm_backward(
            grad_ref[:, columns], unit, head_factors, totals, crop_count, columns
        )
        low_ref[:, columns] = grad.astype(jnp.bfloat16)
    factors = norm_factors(pre_terms, norm_ref, 0, count)
    sums = Sums(sums_ref)
    own_rows = own_ref.shape[0]
    for chunk in range(CHUNKS):
        wait(chunk)
        part = slice(chunk * step, (chunk + 1) * step)
        pooled = product_bt(low_ref[...], weight[part, :D]) / size_ref[...]
        high_part, rest_part = split(pooled)
        for rows, columns in tiles(2 * own_rows, part.stop - part.start, 48, 256):
            across = slice(part.start + columns.start, part.start + columns.stop)
            spread = spread_ref[rows, :]
            out_grad = product(spread, high_part[:, columns]) + product(
                spread, rest_part[:, columns]
            )
            unit, shifted = normalize(pre_ref[rows, across], factors, across)
            joined = shifted + x_ref[rows, across].astype(jnp.float32)
            joined_grad = out_grad * silu_slope(joined)
            if rows.start < own_rows:
                own_ref[rows, across] = joined_grad
            else:
                other_ref[rows.start - own_rows : rows.stop - own_rows, across] = joined_grad
            sums.add(across, joined_grad, joined_grad * unit)
    sums.store()


def column_halves(low_ref, core, kept_ref, sent_ref):
    half = kept_ref.shape[1]
    for out_ref, which in ((kept_ref, core[0]), (sent_ref, 1 - core[0])):
        out_ref[...] = low_ref[:, pl.ds(pl.multiple_of(which * half, half), half)]


def expand_back_kernel(
    count, core, own_ref, other_ref, pre_ref, wide_ref, weight_ref, before_ref, mid_ref, bias_ref, *refs
):
    pre_terms, back_terms, before_terms, *refs = refs
    kept_ref, sent_ref, out_ref, sums_ref, total_ref, low_ref = refs
    factors = norm_factors(pre_terms, wide_ref, 0, count)
    totals = jnp.sum(back_terms[...].astype(jnp.float32), 0)
    total_ref[...] = totals
    own_rows = own_ref.shape[0]
    for rows, columns in tiles(2 * own_rows, D, 48, 512):
        unit, _ = normalize(pre_ref[rows, columns], factors, columns)
        if rows.start < own_rows:
            grad = own_ref[rows, columns]
        else:
            grad = other_ref[rows.start - own_rows : rows.stop - own_rows, columns]
        grad = norm_backward(grad, unit, factors, totals, count, columns)
        low_ref[rows, columns] = grad.astype(jnp.bfloat16)
    column_halves(low_ref, core, kept_ref, sent_ref)
    factors = norm_factors(before_terms, mid_ref, 2, count)
    sums = Sums(sums_ref)
    for columns in (slice(k, k + 256) for k in range(0, MID, 256)):
        back = product_bt(low_ref[...], weight_ref[columns, :D])
        unit, shifted = normalize(before_ref[:, columns], factors, columns)
        back = back * silu_slope(shifted)
        out_ref[:, columns] = back
        sums.add(columns, back, back * unit)
    sums.store()
    bias = jnp.concatenate([bias_ref[...], jnp.zeros_like(bias_ref)], 0)
    for copy in range(sums_ref.shape[0]):
        sums_ref[copy, :, MID:] = bias


def spatial_back_kernel(
    count, core, grad_ref, pre_ref, norm_ref, weight_ref, before_ref, valid_ref, *refs
):
    pre_terms, back_terms, before_terms, *refs = refs
    kept_ref, sent_ref, out_ref, sums_ref, total_ref, slots, low_ref = refs
    rows = grad_ref.shape[0]
    factors = norm_factors(pre_terms, norm_ref, 2, count)
    totals = jnp.sum(back_terms[...].astype(jnp.float32), 0)
    total_ref[...] = totals
    for high, columns in tiles(rows, MID, 48, 512):
        unit, _ = normalize(pre_ref[high, columns], factors, columns)
        grad = norm_backward(grad_ref[high, columns], unit, factors, totals, count, columns)
        low_ref[high, columns] = grad.astype(jnp.bfloat16)
    column_halves(low_ref, core, kept_ref, sent_ref)
    edge = jnp.zeros((EDGE, MID), jnp.float32)
    for place in range(9):
        slots[place, 0:EDGE, :] = edge
        slots[place, EDGE + rows :, :] = edge
        for columns in (slice(k, k + 256) for k in range(0, MID, 256)):
            patch = product_bt(
                low_ref[...],
                weight_ref[place * MID + columns.start : place * MID + columns.stop, :],
            )
            slots[place, EDGE : EDGE + rows, columns] = patch * valid_ref[:, place : place + 1]
    factors = norm_factors(before_terms, norm_ref, 0, count)
    sums = Sums(sums_ref)
    for high, columns in tiles(rows, MID, 48, 256):
        back = 0.0
        for place in range(9):
            start = EDGE - neighbour(place, rows // (2 * SIDE * SIDE)) + high.start
            back = back + slots[place, start : start + high.stop - high.start, columns]
        unit, shifted = normalize(before_ref[high, columns], factors, columns)
        back = back * silu_slope(shifted)
        out_ref[high, columns] = back
        sums.add(columns, back, back * unit)
    sums.store()


def reduce_back_kernel(
    count,
    core,
    grad_ref,
    pre_ref,
    norm_ref,
    pre_terms,
    back_terms,
    low_ref,
    other_ref,
    kept_ref,
    sent_ref,
    total_ref,
):
    rows = grad_ref.shape[0]
    factors = norm_factors(pre_terms, norm_ref, 0, count)
    totals = jnp.sum(back_terms[...].astype(jnp.float32), 0)
    total_ref[...] = totals
    for high, columns in tiles(rows, MID, 48, 512):
        unit, _ = normalize(pre_ref[high, columns], factors, columns)
        grad = norm_backward(grad_ref[high, columns], unit, factors, totals, count, columns)
        low_ref[high, columns] = grad.astype(jnp.bfloat16)
    other_ref[...] = low_ref[rows // 2 :, :]
    column_halves(low_ref, core, kept_ref, sent_ref)


def arrange_kernel(core, canvases_ref, own_ref, other_ref, rows_ref):
    _, _, _, canvas_count, _ = canvases_ref.shape
    for which, out_ref in enumerate((own_ref, other_ref)):
        micro = core[0] if which == 0 else 1 - core[0]
        for pixel in range(SIDE * SIDE):
            rows = slice(pixel * canvas_count, (pixel + 1) * canvas_count)
            values = canvases_ref[micro, pixel // SIDE, pixel % SIDE]
            rows_ref[rows, :] = values.astype(jnp.float32)
        out_ref[...] = rows_ref[...].astype(jnp.bfloat16)


def input_grad_kernel(
    core, own_ref, other_ref, low_ref, other_low_ref, weight_ref, out_ref, rows_ref
):
    own_rows = own_ref.shape[0]
    canvas_count = out_ref.shape[3]
    for which in range(2):
        micro = core[0] if which == 0 else 1 - core[0]
        grad_ref = own_ref if which == 0 else other_ref
        low = low_ref[:own_rows, :] if which == 0 else other_low_ref[...]
        for columns in (slice(k, k + 512) for k in range(0, D, 512)):
            rows_ref[:, columns] = grad_ref[:, columns] + product_bt(low, weight_ref[columns, :])
        for pixel in range(SIDE * SIDE):
            rows = slice(pixel * canvas_count, (pixel + 1) * canvas_count)
            out_ref[micro, pixel // SIDE, pixel % SIDE] = rows_ref[rows, :]


def proto_grad_kernel(first_ref, second_ref, out_ref):
    rows = out_ref.shape[0]
    for k in range(0, rows, 128):
        stop = min(k + 128, rows)
        total = first_ref[:, k : k + 128] + second_ref[:, k : k + 128]
        out_ref[k:stop, :] = total.T[: stop - k, :]


def inside_canvas(own_canvases):
    valid = np.zeros((2, SIDE, SIDE, own_canvases, 16), np.float32)
    for place in range(9):
        down, right = place // 3 - 1, place % 3 - 1
        for y in range(SIDE):
            for x in range(SIDE):
                valid[:, y, x, :, place] = 0 <= y + down < SIDE and 0 <= x + right < SIDE
    return jnp.asarray(valid.reshape(-1, 16))


def neighbour(place, own_canvases):
    return ((place // 3 - 1) * SIDE + place % 3 - 1) * own_canvases


EDGE = 32


def add_columns(total_ref, columns, values):
    rows, width = values.shape
    total_ref[:, columns] += jnp.sum(values.reshape(rows // 8, 8, width), 0)


def codes_kernel(
    crops,
    device_crops,
    place,
    sent_ref,
    side_ref,
    prototypes_ref,
    loss_ref,
    proto_grad_ref,
    unit_grad_ref,
    units_ref,
    proto_ref,
    partner_ref,
    codes_ref,
    heat_ref,
    score_ref,
    total_ref,
    scale_ref,
    inverse_ref,
    *,
    factor,
):
    rows_all, width = codes_ref.shape
    own = unit_grad_ref.shape[0]
    chunks = [slice(k, k + LANES) for k in range(0, width, LANES)]
    real = lax.broadcasted_iota(jnp.int32, (1, width), 1) < PROTOS

    dim = units_ref.shape[1]
    for i in range(sent_ref.shape[0]):
        units_ref[i * own : (i + 1) * own, :] = sent_ref[i, :own, :]
    proto_ref[PROTOS // 16 * 16 :, :] = jnp.zeros((width - PROTOS // 16 * 16, dim), jnp.bfloat16)
    proto_ref[:PROTOS, :] = prototypes_ref[...]

    queue_rows = side_ref.shape[0]
    device_rows = queue_rows // (crops // device_crops)
    crop = lax.broadcasted_iota(jnp.int32, (crops, queue_rows), 0)
    holder = crop // device_crops ^ place[1]
    row = lax.broadcasted_iota(jnp.int32, (crops, queue_rows), 1)
    holds = (row == holder * device_rows).astype(jnp.bfloat16)
    found = product(holds, side_ref[:, dim:])
    crop = lax.broadcasted_iota(jnp.int32, found.shape, 0)
    lane = lax.broadcasted_iota(jnp.int32, found.shape, 1)
    here = lane == place[1] * device_crops + crop % device_crops
    partner = jnp.sum(jnp.where(here, found, 0.0), 1, keepdims=True)
    partner_ref[...] = partner.astype(jnp.int32)

    def scores(rows, columns, queue=False):
        left = side_ref[rows, :dim] if queue else units_ref[rows, :]
        return product_bt(left, proto_ref[columns, :])

    def keep(values, columns):
        if columns.stop <= PROTOS:
            return values
        lanes = columns.start + lax.broadcasted_iota(jnp.int32, values.shape, 1)
        return jnp.where(lanes < PROTOS, values, 0.0)

    def fold(values):
        return sum(values[:, k : k + 128] for k in range(0, values.shape[1], 128))

    total_ref[...] = jnp.zeros_like(total_ref)

    for queue, start, count in ((False, 0, crops), (True, crops, queue_rows)):

        def first(i, carry):
            rows = pl.ds(pl.multiple_of(i * 128, 128), 128)
            target = pl.ds(pl.multiple_of(start + i * 128, 128), 128)
            for columns in chunks:
                score = scores(rows, columns, queue)
                powers = keep(jnp.exp(score * (1.0 / SINK_EPS)), columns)
                codes_ref[target, columns] = powers
                add_columns(total_ref, columns, powers)
            return carry

        lax.fori_loop(0, count // 128, first, 0)

    def column_factors(turn):
        total = jnp.sum(total_ref[...], 0, keepdims=True)
        total = jnp.where(real, total, 1.0)
        if turn == 0:
            scale = jnp.where(total > 1e30, 2.0**-64, 1.0)
            scale_ref[...] = jnp.broadcast_to(scale, scale_ref.shape)
            total = total * scale
        inverse_ref[...] = jnp.broadcast_to(1.0 / total, inverse_ref.shape)

    def divided(turn, rows, columns):
        values = codes_ref[rows, columns]
        if turn == 0:
            values = values * scale_ref[0:1, columns]
        return values * inverse_ref[0:1, columns]

    def row_inverse(turn, rows):
        part = sum(fold(divided(turn, rows, columns)) for columns in chunks)
        return 1.0 / jnp.sum(part, 1, keepdims=True)

    for turn in range(SINK_ITERS - 1):
        column_factors(turn)
        total_ref[...] = jnp.zeros_like(total_ref)

        def both(i, carry):
            rows = pl.ds(pl.multiple_of(i * 64, 64), 64)
            inverse = row_inverse(turn, rows)
            for columns in chunks:
                values = divided(turn, rows, columns) * inverse
                codes_ref[rows, columns] = values
                add_columns(total_ref, columns, values)
            return carry

        lax.fori_loop(0, rows_all // 64, both, 0)

    column_factors(SINK_ITERS - 1)
    loss_ref[...] = jnp.zeros_like(loss_ref)
    block = 128

    def last(i, carry):
        rows = pl.ds(pl.multiple_of(i * block, block), block)
        inverse = row_inverse(SINK_ITERS - 1, rows)
        row = lax.broadcasted_iota(jnp.int32, (block, block), 0)
        column = lax.broadcasted_iota(jnp.int32, (block, block), 1)
        pick = (column == (row // CROPS) * CROPS + partner_ref[rows, :]).astype(jnp.bfloat16)
        pick = jnp.concatenate([pick, pick], 1)
        heat_part = jnp.zeros((block, 128), jnp.float32)
        target_part = jnp.zeros((block, 128), jnp.float32)
        loss_part = jnp.zeros((block, 128), jnp.float32)
        for columns in chunks:
            score = scores(rows, columns)
            heat = keep(jnp.exp(score * (1.0 / SOFTMAX_HEAT)), columns)
            heat_ref[:, columns] = heat
            heat_part += fold(heat)
            codes = divided(SINK_ITERS - 1, rows, columns) * inverse
            high = codes.astype(jnp.bfloat16)
            rest = (codes - high.astype(jnp.float32)).astype(jnp.bfloat16)
            target = product(pick, jnp.concatenate([high, rest], 0))
            codes_ref[rows, columns] = target
            target_part += fold(target)
            loss_part += fold(target * score)
        heat_sum = jnp.sum(heat_part, 1, keepdims=True)
        target_sum = jnp.sum(target_part, 1, keepdims=True)
        row_loss = (
            target_sum * jnp.log(heat_sum)
            - jnp.sum(loss_part, 1, keepdims=True) * (1.0 / SOFTMAX_HEAT)
        )
        loss_ref[...] += jnp.broadcast_to(jnp.sum(row_loss, 0, keepdims=True), loss_ref.shape)
        ratio = target_sum / heat_sum * factor
        for columns in chunks:
            grad = heat_ref[:, columns] * ratio - codes_ref[rows, columns] * factor
            score_ref[rows, columns] = grad.astype(jnp.bfloat16)
        return carry

    lax.fori_loop(0, crops // block, last, 0)
    for columns in chunks:
        proto_grad_ref[:, columns] = product_t(units_ref[...], score_ref[:, columns])
    mine = pl.ds(pl.multiple_of(place[0], own), own)
    unit_grad_ref[...] = product(score_ref[mine, :], proto_ref[...])


def gathered_loss(units, side, prototypes, place, own, device_crops, loss_factor_weight):
    crops, dim = units.shape[0] * own, units.shape[2]
    width = -(-PROTOS // LANES) * LANES
    rows_all = crops + side.shape[0]
    f32, bf16 = jnp.float32, jnp.bfloat16
    loss, proto_grad, unit_grad = kernel_call(
        lambda *refs: codes_kernel(
            crops, device_crops, *refs, factor=loss_factor_weight / SOFTMAX_HEAT
        ),
        [((8, 128), f32), ((dim, width), f32, PUT_FAR), ((own, dim), f32)],
        [Scalars(place), units, Loaded(side), Loaded(prototypes)],
        scratch=[
            pltpu.VMEM((crops, dim), bf16),
            pltpu.VMEM((width, dim), bf16),
            pltpu.VMEM((crops, 1), jnp.int32),
            pltpu.VMEM((rows_all, width), f32),
            pltpu.VMEM((128, width), f32),
            pltpu.VMEM((crops, width), bf16),
            pltpu.VMEM((8, width), f32),
            pltpu.VMEM((8, width), f32),
            pltpu.VMEM((8, width), f32),
        ],
        flops=2 * width * (rows_all * dim + 6 * crops * dim),
        transcendentals=width * (rows_all + crops),
        limit=24,
    )
    return loss[0, 0], proto_grad, unit_grad


def sinkhorn(batch_codes, stored_codes, total):
    for turn in range(SINK_ITERS):
        column_totals = total(jnp.sum(batch_codes, 0) + jnp.sum(stored_codes, 0))
        batch_codes = batch_codes / column_totals
        stored_codes = stored_codes / column_totals
        batch_codes = batch_codes / jnp.sum(batch_codes, 1, keepdims=True)
        stored_codes = stored_codes / jnp.sum(stored_codes, 1, keepdims=True)
    return batch_codes


def swapped_loss(scores, codes, pick, loss_factor_weight):
    rows = scores.shape[0]
    target = jnp.einsum(
        "cab,cbk->cak", pick, codes.reshape(rows // CROPS, CROPS, PROTOS), precision=HIGH
    ).reshape(rows, PROTOS)
    log_likelihoods = jax.nn.log_softmax(scores / SOFTMAX_HEAT, axis=1)
    score_grad = (jnp.exp(log_likelihoods) * jnp.sum(target, 1, keepdims=True) - target) * (
        loss_factor_weight / SOFTMAX_HEAT
    )
    return -jnp.sum(target * log_likelihoods), score_grad.astype(jnp.bfloat16)


def per_device(
    canvases,
    crop_map,
    partner,
    queue,
    w_reduce,
    w_spatial,
    w_expand,
    w_hidden,
    w_project,
    norm_mid,
    norm_wide,
    bias_out,
    prototypes,
):
    f32, bf16 = jnp.float32, jnp.bfloat16
    size = lax.axis_size("dp")
    me_dp, me_core = lax.axis_index("dp"), lax.axis_index("shard")
    core = Scalars(me_core.astype(jnp.int32).reshape(1))
    own_canvases = canvases.shape[1]
    canvas_count = 2 * own_canvases
    pixels = SIDE * SIDE
    own_rows = own_canvases * pixels
    local_rows = canvas_count * pixels
    local_crops = canvas_count * CROPS
    pixel_total = float(local_rows * size)
    crop_count = local_crops * size
    crop_total = float(crop_count)
    loss_factor_weight = 1.0 / (MICRO * crop_total)
    crop_ids = jnp.arange(CROPS, dtype=jnp.int32)
    valid = inside_canvas(own_canvases)
    proj = bias_out.shape[0]
    partner_size = partner.size
    copies = copies_of(size)
    by_steps = size == STEPS_DP
    if by_steps:
        slots = relative_slots(size)
        chip_slots = lax.dynamic_slice_in_dim(slots.reshape(size, 2), me_core, 1, 1)[:, 0]

    def both_cores(values):
        mine = lax.dynamic_index_in_dim(values, me_core, 0, keepdims=False)
        other = lax.dynamic_index_in_dim(values, 1 - me_core, 0, keepdims=False)
        return jnp.concatenate([mine, swap_cores(other)], 0)

    def gather_whole(shard):
        return Gathered(lax.all_gather(shard, BOTH, axis=0, tiled=True))

    head_shard = jnp.concatenate([w_hidden, w_project], 1)
    beside = queue.shape[1]
    gathered_codes = (
        crop_count * PROTOS * 4 <= GATHERED_CODES_BYTES
        and queue.shape[0] == w_expand.shape[0]
        and partner_size <= beside
    )
    if gathered_codes:
        partners = jnp.pad(
            partner.astype(bf16).reshape(1, -1),
            ((0, 0), (0, beside - partner_size)),
        )
        partners = jnp.broadcast_to(partners, (queue.shape[0], beside))
        w_expand = jnp.concatenate([w_expand, queue, partners], 1)

    labels = both_cores(jnp.concatenate([crop_map, partner], 2))
    crop_map, partner = labels[:, :pixels], labels[:, pixels:]
    crop_of = jnp.arange(local_crops, dtype=jnp.int32)
    pixel_crop = crop_map + CROPS * jnp.arange(canvas_count, dtype=jnp.int32)[:, None]
    pixel_crop = pixel_crop.reshape(2, own_canvases, pixels).swapaxes(1, 2).reshape(local_rows)
    pool = (crop_of[:, None] == pixel_crop[None, :]).astype(bf16)
    spread = (pixel_crop[:, None] == crop_of[None, :]).astype(bf16)
    crop_sizes = jnp.sum(pool.astype(f32), 1, keepdims=True)

    half_rows = ((own_rows, D), bf16)
    own_x, other_x = kernel_call(
        arrange_kernel,
        [half_rows, half_rows],
        [core, canvases.transpose(0, 2, 3, 1, 4)],
        scratch=[pltpu.VMEM((own_rows, D), f32)],
    )
    input_rows = join([(own_x[None], swap_cores(other_x)[None])])[0].reshape(local_rows, D)

    if by_steps:
        reduce_part = Gathering(w_reduce, size)
        gather_step([reduce_part])
        spatial_part = Gathering(hold(w_spatial, [reduce_part.held]), size)
        gather_step([reduce_part], [pool, spread, crop_sizes, input_rows])
        head_held = lax.all_gather(hold(head_shard, [reduce_part.held]), "dp", axis=0)
        gather_step([reduce_part, spatial_part])
        expand_part = Gathering(hold(w_expand, [spatial_part.held]), size)
        reduce_all = reduce_part.finish(slots)
    else:
        reduce_all = gather_whole(w_reduce)

    mid_rows, wide_rows = ((local_rows, MID), f32), ((local_rows, D), f32)
    mid_sums, wide_sums = ((copies, 2, MID), f32), ((copies, 2, D), f32, PUT_FAR)

    back_sums = ((copies, 2, D), bf16 if copies > 1 else f32, PUT_FAR)

    def weight_out(weight):
        return (weight.shape, bf16, FAR)

    pre_one, sums, full_reduce = kernel_call(
        lambda *refs: reduce_kernel(reduce_all.count, *refs),
        [mid_rows, mid_sums, weight_out(reduce_all)],
        [input_rows] + reduce_all.inputs(),
        scratch=reduce_all.scratch() + [pltpu.SemaphoreType.DMA],
        flops=2 * local_rows * D * MID,
    )
    terms_one = terms_over_dp(sums)
    if by_steps:
        gather_step([spatial_part, expand_part], [sums])
        gather_step([spatial_part], [terms_one])
        spatial_all = spatial_part.finish(slots)
    else:
        spatial_all, expand_all = gather_whole(w_spatial), gather_whole(w_expand)

    pre_two, sums, image_patches, full_spatial = kernel_call(
        lambda *refs: spatial_kernel(spatial_all.count, pixel_total, *refs),
        [
            mid_rows,
            mid_sums,
            ((local_rows, 9 * MID), bf16, FAR),
            weight_out(spatial_all),
        ],
        [pre_one, norm_mid, valid, terms_one] + spatial_all.inputs(),
        scratch=[
            pltpu.VMEM((local_rows + 2 * EDGE, MID), f32),
            pltpu.VMEM((local_rows, 9 * MID), bf16),
            pltpu.SemaphoreType.DMA,
        ]
        + spatial_all.scratch()
        + [pltpu.SemaphoreType.DMA],
        flops=2 * local_rows * 9 * MID * MID,
    )
    terms_two = terms_over_dp(sums)
    if by_steps:
        gather_step([expand_part], [sums])
        gather_step([expand_part], [terms_two])
        expand_all = expand_part.finish(slots)

    side = ((expand_all.shape[0], max(expand_all.shape[1] - D, 128)), bf16, PUT_FAR)
    act_two, pre_three, sums, full_expand, side = kernel_call(
        lambda *refs: expand_kernel(expand_all.count, pixel_total, *refs),
        [
            ((local_rows, MID), bf16, PUT_FAR),
            wide_rows,
            wide_sums,
            weight_out(expand_all),
            side,
        ],
        [pre_two, norm_mid, terms_two] + expand_all.inputs(),
        scratch=expand_all.scratch() + [pltpu.SemaphoreType.DMA],
        flops=2 * local_rows * D * MID,
    )
    terms_three = terms_over_dp(sums)
    if by_steps:
        head_held, _ = lax.optimization_barrier((head_held, sums))
        head = other_core_dp(head_held, size)
    else:
        head = gather_whole(head_shard)

    crop_rows = ((local_crops, D), f32, PUT_FAR)
    pooled_low, pre_head, sums, full_project = kernel_call(
        lambda *refs: pool_kernel(head.count, pixel_total, *refs),
        [
            ((local_crops, D), bf16, PUT_FAR),
            crop_rows,
            wide_sums,
            ((D, proj), bf16, PUT_FAR),
        ],
        [
            pre_three,
            input_rows,
            Loaded(norm_wide),
            Loaded(pool),
            Loaded(crop_sizes),
            terms_three,
        ]
        + head.inputs(),
        scratch=[pltpu.VMEM((local_rows, 256), bf16), pltpu.VMEM((local_rows, 256), bf16)]
        + head.scratch(CHUNKS),
        flops=2 * local_crops * D * D,
        transcendentals=local_rows * D,
    )
    terms_head = terms_over_dp(sums)

    embed_rows = ((local_crops, proj), f32)
    send_pooled = gathered_codes and copies * proj == D
    act_head, unit_embed, inv_length, unit_low = kernel_call(
        lambda *refs: embed_kernel(crop_total, *refs),
        [
            ((local_crops, D), bf16),
            embed_rows,
            embed_rows,
            ((copies, local_crops * (2 if send_pooled else 1), proj), bf16, PUT_FAR),
        ],
        [
            Loaded(pre_head),
            Loaded(norm_wide),
            Streamed(full_project),
            Loaded(bias_out.reshape(1, proj)),
            Streamed(pooled_low),
            terms_head,
        ],
        flops=2 * local_crops * D * proj,
    )

    if gathered_codes:
        all_units = lax.all_to_all(unit_low, "dp", 0, 0)
        loss_part, proto_part, unit_grad = gathered_loss(
            all_units,
            side,
            prototypes,
            jnp.stack([me_dp * local_crops, me_core]).astype(jnp.int32),
            local_crops,
            own_canvases * CROPS,
            loss_factor_weight,
        )
    else:
        chip_queue = jnp.concatenate([queue, swap_cores(queue)], 0)
        queue_codes = jnp.exp(product_bt(chip_queue, prototypes) / SINK_EPS)
        pick = (partner[:, :, None] == crop_ids[None, None, :]).astype(f32)
        all_units = unit_low
        scores = product_bt(unit_low[0], prototypes)
        codes = sinkhorn(
            jnp.exp(scores / SINK_EPS), queue_codes, lambda sums: lax.psum(sums, "dp")
        )
        loss_part, score_low = swapped_loss(scores, codes, pick, loss_factor_weight)
        proto_part, loss_part = lax.psum((product_t(unit_low[0], score_low), loss_part), "dp")
        unit_grad = product(score_low, prototypes)

    embed_low, head_act_grad, sums, bias_part = kernel_call(
        lambda *refs: embed_back_kernel(crop_total, *refs),
        [((local_crops, proj), bf16), crop_rows, back_sums, ((1, proj), f32)],
        [
            unit_grad,
            unit_embed,
            inv_length,
            Streamed(full_project),
            Streamed(pre_head),
            Loaded(norm_wide),
            terms_head,
        ],
        flops=2 * local_crops * D * proj,
    )
    back_head = terms_over_dp(sums)

    chip_rows = 2 * w_hidden.shape[0]
    if send_pooled:
        left = all_units[:, local_crops:].reshape(crop_count, chip_rows)
    else:
        left = lax.all_gather(pooled_low, "dp", axis=0, tiled=True)
        left = lax.dynamic_slice_in_dim(left, me_dp * chip_rows, chip_rows, 1)

    own_part = ((own_rows, D), f32)
    head_low, own_grad, other_grad, sums, total_head = kernel_call(
        lambda *refs: pool_back_kernel(head.count, crop_total, pixel_total, *refs),
        [
            ((local_crops, D), bf16),
            own_part,
            own_part + (PUT_FAR,),
            back_sums,
            ((2, D), f32, PUT_FAR),
        ],
        [
            Loaded(head_act_grad),
            Loaded(pre_head),
            Streamed(pre_three),
            Streamed(input_rows),
            Loaded(norm_wide),
            Loaded(spread),
            Loaded(crop_sizes),
            terms_head,
            back_head,
            terms_three,
        ]
        + head.inputs(),
        scratch=head.scratch(CHUNKS),
        flops=2 * local_crops * D * D,
        transcendentals=local_rows * D,
    )
    back_three = terms_over_dp(sums)
    other_grad, _ = lax.optimization_barrier((other_grad, back_three))
    peer_grad = swap_cores(other_grad)

    right = lax.all_gather(head_low, "dp", axis=0, tiled=True)

    def low_halves(width):
        return [((local_rows, width // 2), bf16, PUT_FAR)] * 2

    three_kept, three_sent, two_act_grad, sums, total_three = kernel_call(
        lambda *refs: expand_back_kernel(pixel_total, *refs),
        [
            *low_halves(D),
            mid_rows,
            ((copies, 2, MID + proj), f32, PUT_FAR),
            ((2, D), f32, PUT_FAR),
        ],
        [
            core,
            own_grad,
            Loaded(other_grad),
            Streamed(pre_three),
            Loaded(norm_wide),
            Streamed(full_expand),
            Streamed(pre_two),
            norm_mid,
            bias_part,
            terms_three,
            back_three,
            terms_two,
        ],
        scratch=[pltpu.VMEM((local_rows, D), bf16)],
        flops=2 * local_rows * D * MID,
    )
    back_two = terms_over_dp(sums)
    before_two = []
    if by_steps:
        expand_sum = weight_grad(
            (act_two, swap_cores(act_two)),
            (three_kept, swap_cores(three_sent)),
            chip_slots,
            size,
            (
                (act_head, swap_cores(act_head)),
                (embed_low, swap_cores(embed_low)),
                core,
            ),
            after=[sums],
        )
        before_two = [expand_sum.kept]

    two_kept, two_sent, one_act_grad, sums, total_two = kernel_call(
        lambda *refs: spatial_back_kernel(pixel_total, *refs),
        [*low_halves(MID), mid_rows, mid_sums, ((2, MID + proj), f32)],
        [
            core,
            two_act_grad,
            Streamed(pre_two),
            norm_mid,
            Streamed(full_spatial),
            Streamed(pre_one),
            valid,
            terms_two,
            back_two,
            terms_one,
        ],
        scratch=[
            pltpu.VMEM((9, local_rows + 2 * EDGE, MID), f32),
            pltpu.VMEM((local_rows, MID), bf16),
        ],
        flops=2 * local_rows * 9 * MID * MID,
        after=before_two,
    )
    before_one = []
    if by_steps:
        spatial_sum = weight_grad(
            (image_patches, swap_cores(image_patches)),
            (two_kept, swap_cores(two_sent)),
            chip_slots,
            size,
        )
        spatial_sum.first(two_kept)
        sums, _ = lax.optimization_barrier((sums, spatial_sum.kept))

    back_one = terms_over_dp(sums)
    one_low, other_low, one_kept, one_sent, total_one = kernel_call(
        lambda *refs: reduce_back_kernel(pixel_total, *refs),
        [
            ((local_rows, MID), bf16, PUT_FAR),
            ((own_rows, MID), bf16, PUT_FAR),
            *low_halves(MID),
            ((2, MID), f32, PUT_FAR),
        ],
        [core, one_act_grad, Streamed(pre_one), norm_mid, terms_one, back_one],
        after=before_one,
    )
    if by_steps:
        expand_sum.first(back_one)
        spatial_sum.second([one_low])
        expand_sum.second([spatial_sum.kept])
        reduce_sum = weight_grad(
            (input_rows, swap_cores(input_rows)),
            (one_kept, swap_cores(one_sent)),
            chip_slots,
            size,
            after=[expand_sum.kept, right],
        )

    proto_other = swap_cores(proto_part)
    other_low = swap_cores(other_low)
    late = []
    if by_steps:
        reduce_sum.first(one_low)
        expand_sum.third([reduce_sum.kept])
        spatial_sum.third([expand_sum.kept])
        reduce_sum.second([spatial_sum.kept])
        late = [reduce_sum.kept]
    by_pixel = kernel_call(
        input_grad_kernel,
        [((MICRO, SIDE, SIDE, own_canvases, D), f32)],
        [core, own_grad, peer_grad, one_low, other_low, full_reduce],
        scratch=[pltpu.VMEM((own_rows, D), f32)],
        flops=2 * local_rows * D * MID,
        after=late,
    )[0]
    if by_steps:
        reduce_sum.third([by_pixel])
        late = [reduce_sum.kept]
    left, right, _ = lax.optimization_barrier((left, right, late))
    if gathered_codes:
        proto_grad = kernel_call(
            proto_grad_kernel,
            [(prototypes.shape, f32)],
            [Loaded(proto_part), proto_other],
            after=late,
        )[0]
    else:
        proto_grad = (proto_part + proto_other).T
    hidden_part = product_t(left, right)

    def own_half(part):
        half = chip_rows // 2
        mine = lax.dynamic_slice_in_dim(part, me_core * half, half, 0)
        other = lax.dynamic_slice_in_dim(part, (1 - me_core) * half, half, 0)
        return mine + swap_cores(other)

    grad_hidden = own_half(hidden_part)
    if by_steps:
        grad_spatial, grad_reduce = swap_columns(spatial_sum.finish(), reduce_sum.finish())
        total = expand_sum.finish()
        (grad_expand,) = swap_columns(total[:, : D // 2])
        grad_project = jnp.concatenate(
            [total[:, k : k + proj] for k in range(D // 2, total.shape[1], proj)], 0
        )
    else:

        def scatter(first, kept, sent):
            lows = jnp.concatenate(
                [jnp.where(me_core == 0, kept, sent), jnp.where(me_core == 0, sent, kept)], 1
            )
            return lax.psum_scatter(
                product_t(first, lows), BOTH, scatter_dimension=0, tiled=True
            )

        grad_reduce = scatter(input_rows, one_kept, one_sent)
        grad_spatial = scatter(image_patches, two_kept, two_sent)
        grad_expand = scatter(act_two, three_kept, three_sent)
        grad_project = lax.psum_scatter(
            product_t(act_head, embed_low), BOTH, scatter_dimension=0, tiled=True
        )

    totals = (total_one, total_two, total_three, total_head)
    (total_one, total_two, total_three, total_head), _ = lax.optimization_barrier((totals, late))
    narrow = jnp.concatenate(
        [
            jnp.stack([total_one[1], total_one[0], total_two[1, :MID], total_two[0, :MID]])
            .reshape(-1),
            jnp.stack([total_three[1], total_three[0], total_head[1], total_head[0]]).reshape(-1),
            total_two[0, MID:],
            jnp.broadcast_to(loss_part, (128,)),
        ]
    )
    narrow = narrow + swap_cores(narrow)
    mid_end, wide_end = norm_mid.size, norm_mid.size + norm_wide.size
    bias_end = wide_end + proj
    return (
        narrow[bias_end] * loss_factor_weight,
        by_pixel.transpose(0, 3, 1, 2, 4),
        grad_reduce,
        grad_spatial,
        grad_expand,
        grad_hidden,
        grad_project,
        narrow[:mid_end].reshape(norm_mid.shape),
        narrow[mid_end:wide_end].reshape(norm_wide.shape),
        narrow[wide_end:bias_end],
        proto_grad,
    )


def solution(mesh):
    return jax.shard_map(
        per_device,
        mesh=mesh,
        in_specs=(
            P(None, ("dp", "shard"), None, None, None),
            P(None, ("dp", "shard"), None),
            P(None, ("dp", "shard"), None),
            P(("dp", "shard"), None),
            P(("dp", "shard"), None),
            P(("dp", "shard"), None),
            P(("dp", "shard"), None),
            P(("dp", "shard"), None),
            P(("dp", "shard"), None),
            P(),
            P(),
            P(),
            P(),
        ),
        out_specs=(
            P(),
            P(None, ("dp", "shard"), None, None, None),
            P(("dp", "shard"), None),
            P(("dp", "shard"), None),
            P(("dp", "shard"), None),
            P(("dp", "shard"), None),
            P(("dp", "shard"), None),
            P(),
            P(),
            P(),
            P(),
        ),
        check_vma=False,
    )
```

```python
import dataclasses

import jax
import jax.numpy as jnp
import numpy as np
from jax import lax
from jax.experimental import pallas as pl
from jax.experimental.pallas import tpu as pltpu
from jax.sharding import PartitionSpec as P

D = 2048
MID = 512
PROTOS = 3000
SIDE = 6
CROPS = 4
SINK_ITERS = 3
MICRO = 2


EPS_NORM = 1e-05
EPS_UNIT = 1e-06
SOFTMAX_HEAT = 0.1
SINK_EPS = 0.05
HIGH = lax.Precision.HIGHEST
BOTH = ("dp", "shard")
GATHERED_CODES_BYTES = 32 * 2**20
MIB = 2**20
LANES = 768
CHUNKS = 4


def product(left, right):
    return jnp.dot(left, right, preferred_element_type=jnp.float32)


def product_t(left, right):
    return lax.dot_general(
        left, right, (((0,), (0,)), ((), ())), preferred_element_type=jnp.float32
    )


def product_bt(left, right):
    return lax.dot_general(
        left, right, (((1,), (1,)), ((), ())), preferred_element_type=jnp.float32
    )


def silu_slope(values):
    sigmoid_value = jax.nn.sigmoid(values)
    return sigmoid_value * (1.0 + values * (1.0 - sigmoid_value))


@dataclasses.dataclass
class Scalars:
    array: jax.Array


@dataclasses.dataclass
class Left:
    array: jax.Array


@dataclasses.dataclass
class Loaded:
    array: jax.Array


@dataclasses.dataclass
class Streamed:
    array: jax.Array


class Arriving:
    def __init__(self, ref, copy):
        self.ref, self.copy = ref, copy
        self.shape = ref.shape

    def __getitem__(self, index):
        if self.copy is not None:
            self.copy.wait()
            self.copy = None
        return self.ref[index]


FAR, PUT_FAR = "far", "put far"


def kernel_call(body, outs, args, scratch=(), flops=0, transcendentals=0, limit=17, after=()):
    spaces = {Scalars: pltpu.SMEM, Left: pltpu.HBM, Streamed: pltpu.HBM}
    in_spaces = [spaces.get(type(a), pltpu.VMEM) for a in args] + [pltpu.HBM] * len(after)
    after = [pltpu.with_memory_space_constraint(a, pltpu.HBM) for a in after]
    arrays = []
    for a in args:
        if isinstance(a, (Left, Loaded, Streamed)):
            a = pltpu.with_memory_space_constraint(a.array, pltpu.HBM)
        arrays.append(a.array if isinstance(a, Scalars) else a)
    used = len(arrays)
    out_spaces = [pltpu.HBM if FAR in out else pltpu.VMEM for out in outs]

    streamed = [i for i, a in enumerate(args) if isinstance(a, Streamed)]
    scratch = list(scratch)
    own_scratch = len(scratch)
    for i in streamed:
        scratch += [pltpu.VMEM(arrays[i].shape, arrays[i].dtype), pltpu.SemaphoreType.DMA]

    def kernel(*refs):
        inputs, refs = list(refs[:used]), refs[used + len(after) :]
        mine = len(outs) + own_scratch
        for k, i in enumerate(streamed):
            buffer, sem = refs[mine + 2 * k : mine + 2 * k + 2]
            copy = pltpu.make_async_copy(inputs[i], buffer, sem)
            copy.start()
            inputs[i] = Arriving(buffer, copy)
        body(*inputs, *refs[:mine])

    moved = sum(a.size * a.dtype.itemsize for a in arrays)
    return pl.pallas_call(
        kernel,
        out_shape=[
            jax.ShapeDtypeStruct(*out) if len(out) == 2 else pltpu.HBM(*out[:2]) for out in outs
        ],
        in_specs=[pl.BlockSpec(memory_space=space) for space in in_spaces],
        out_specs=[pl.BlockSpec(memory_space=space) for space in out_spaces],
        scratch_shapes=list(scratch),
        compiler_params=pltpu.CompilerParams(vmem_limit_bytes=limit * MIB),
        cost_estimate=pl.CostEstimate(
            flops=int(flops), bytes_accessed=int(moved), transcendentals=int(transcendentals)
        ),
    )(*arrays, *after)


def join_kernel(counts, *refs):
    outs = refs[sum(counts) :]
    start = 0
    for count, joined in zip(counts, outs):
        parts = refs[start : start + count]
        start += count
        length = parts[0].shape[0]

        def move(i, carry):
            for k, part in enumerate(parts):
                joined[i + k * length] = part[i]
            return carry

        lax.fori_loop(0, length, move, 0)


def join(groups, after=()):
    counts = [len(group) for group in groups]
    outs = [
        ((len(group) * group[0].shape[0],) + group[0].shape[1:], group[0].dtype)
        for group in groups
    ]
    return kernel_call(
        lambda *refs: join_kernel(counts, *refs),
        outs,
        [part for group in groups for part in group],
        after=after,
    )


def hold_kernel(source, target):
    target[...] = source[...]


def hold(values, after=()):
    return kernel_call(hold_kernel, [(values.shape, values.dtype)], [values], after=after)[0]


def add_parts_kernel(kept, received, *totals):
    length = totals[0].shape[0]

    def move(i, carry):
        for k, out_ref in enumerate(totals):
            place = i + k * length
            total = kept[place].astype(jnp.float32) + received[place].astype(jnp.float32)
            out_ref[i] = total.astype(out_ref.dtype)
        return carry

    lax.fori_loop(0, length, move, 0)


def add_parts(kept, received, count, after=()):
    shape = (kept.shape[0] // count,) + kept.shape[1:]
    kept, *sent = kernel_call(
        add_parts_kernel,
        [(shape, jnp.float32, PUT_FAR)] + [(shape, jnp.bfloat16, PUT_FAR)] * (count - 1),
        [Loaded(kept), received],
        after=after,
    )
    return kept, sent


def swap_cores(values):
    return lax.ppermute(values, "shard", [(0, 1), (1, 0)])


def flip_dp(values, bits, size):
    return lax.ppermute(values, "dp", [(i, i ^ bits) for i in range(size)])


def flip_both(values, dp_bits, size):
    pairs = [(2 * i + c, 2 * (i ^ dp_bits[c]) + c) for i in range(size) for c in range(2)]
    return lax.ppermute(values, BOTH, pairs)


def copies_of(size):
    return size if size <= STEPS_DP else 1


def terms_over_dp(copies):
    if copies.shape[0] > 1:
        return lax.all_to_all(copies, "dp", 0, 0)
    return lax.psum(copies, "dp")


Z_BITS = (8, 4, 12)
XY_BITS = ((2, 1), (1, 2))
STEPS_DP = 16


def relative_slots(size):
    me_dp, me_core = lax.axis_index("dp"), lax.axis_index("shard")
    device = jnp.arange(2 * size, dtype=jnp.int32)
    apart_dp, apart_core = (device // 2) ^ me_dp, (device % 2) ^ me_core
    holder = device % 2
    on = lambda bit: jnp.where((apart_dp & bit) != 0, 1, 0)
    low, high = (jnp.where(holder == 0, on(zero), on(one)) for zero, one in XY_BITS)
    slot = on(Z_BITS[0]) + 2 * on(Z_BITS[1]) + 4 * low + 8 * high + size * apart_core
    return slot.astype(jnp.int32)


class Gathering:
    def __init__(self, shard, size):
        self.size = size
        self.held = shard[None]
        self.step = 0

    def send(self):
        step, held = self.step, self.held
        self.step += 1
        if step == 0:
            return [held] + [flip_dp(held, bits, self.size) for bits in Z_BITS]
        return [held, flip_both(held, XY_BITS[step - 1], self.size)]

    def finish(self, slots):
        return Gathered(self.held, swap_cores(self.held), slots)


def gather_step(parts, after=()):
    joined = join([part.send() for part in parts], after)
    for part, held in zip(parts, joined):
        part.held = held


def other_core_dp(held, size):
    device = jnp.arange(2 * size, dtype=jnp.int32)
    other = (device % 2) != lax.axis_index("shard")
    slots = jnp.where(other, size, 0) + device // 2
    return Gathered(held, swap_cores(held), slots.astype(jnp.int32))


class Scattering:
    def __init__(self, kept, sent, size):
        self.size = size
        self.kept, self.sent = kept, sent

    def first(self, before):
        sent, _ = lax.optimization_barrier((self.sent, before))
        self.received = flip_both(sent, XY_BITS[1], self.size)

    def second(self, after=()):
        self.kept, sent = add_parts(self.kept, self.received, 2, after)
        self.received = flip_both(sent[0], XY_BITS[0], self.size)

    def third(self, after=()):
        self.kept, sent = add_parts(self.kept, self.received, 4, after)
        self.received = [flip_dp(part, bits, self.size) for part, bits in zip(sent, Z_BITS)]

    def finish(self):
        one, two, three = (part[0].astype(jnp.float32) for part in self.received)
        return (self.kept[0] + one) + (two + three)


@dataclasses.dataclass
class Gathered:
    held: jax.Array
    other: jax.Array | None = None
    slots: jax.Array | None = None

    @property
    def count(self):
        return 1 if self.other is None else 3

    @property
    def shape(self):
        if self.other is None:
            return self.held.shape
        half, rows, width = self.held.shape
        return (2 * half * rows, width)

    def inputs(self):
        if self.other is None:
            return [Left(self.held)]
        return [Scalars(self.slots), Left(self.held), Left(self.other)]

    def scratch(self, chunks=1):
        copies = chunks if self.other is None else 2 * self.held.shape[0]
        return [pltpu.VMEM(self.shape, jnp.bfloat16), pltpu.SemaphoreType.DMA((copies,))]


def fetch_weight(inputs, weight, sems, chunks=1):
    count = sems.shape[0]
    rows = weight.shape[0] // count
    each = count // chunks

    def copy(source, i):
        target = weight.at[pl.ds(pl.multiple_of(i * rows, rows), rows)]
        return pltpu.make_async_copy(source, target, sems.at[i])

    if len(inputs) == 1:
        copies = [copy(inputs[0].at[pl.ds(i * rows, rows)], i) for i in range(count)]
        for one in copies:
            one.start()

        def wait_ordered(chunk):
            for one in copies[chunk * each : (chunk + 1) * each]:
                one.wait()

        return wait_ordered

    table, held, other = inputs
    half = held.shape[0]

    def begin(i, carry):
        slot = table[i]

        @pl.when(slot < half)
        def _():
            copy(held.at[slot], i).start()

        @pl.when(slot >= half)
        def _():
            copy(other.at[slot - half], i).start()

        return carry

    lax.fori_loop(0, count, begin, 0)

    def wait(chunk):
        def finish(i, carry):
            copy(held.at[0], i).wait()
            return carry

        lax.fori_loop(chunk * each, (chunk + 1) * each, finish, 0)

    return wait


def weight_grad_kernel(beside, table, *refs):
    left, left_peer, right, right_peer = refs[:4]
    if beside:
        second, second_peer, second_right, second_right_peer, core = refs[4:9]
        kept_ref, sent_ref, total_ref, second_ref = refs[9:]
    else:
        kept_ref, sent_ref, total_ref = refs[4:]
    half, rows, _ = kept_ref.shape
    width = right.shape[1]
    for k in range(0, total_ref.shape[0], 512):
        total_ref[k : k + 512, :] = product_t(left[:, k : k + 512], right[...]) + product_t(
            left_peer[:, k : k + 512], right_peer[...]
        )
    if beside:
        second_ref[...] = product_t(second[...], second_right[...]) + product_t(
            second_peer[...], second_right_peer[...]
        )

    def place(out_ref, slot, i):
        found = total_ref[pl.ds(pl.multiple_of(i * rows, rows), rows), :]
        out_ref[slot, :, :width] = found.astype(out_ref.dtype)
        for part in range(beside):
            start = ((2 * i + core[0]) * beside + part) * rows
            across = second_ref.shape[1]
            columns = slice(width + part * across, width + (part + 1) * across)
            found = second_ref[pl.ds(pl.multiple_of(start, rows), rows), :]
            out_ref[slot, :, columns] = found.astype(out_ref.dtype)

    def move(i, carry):
        slot = table[i]

        @pl.when(slot < half)
        def _():
            place(kept_ref, slot, i)

        @pl.when(slot >= half)
        def _():
            place(sent_ref, slot - half, i)

        return carry

    lax.fori_loop(0, 2 * half, move, 0)


def weight_grad(left, right, slots, size, second=None, after=()):
    depth, width = left[0].shape[1], right[0].shape[1]
    rows = depth // size
    args = [Scalars(slots), *left, Loaded(right[0]), right[1]]
    scratch, beside, extra = [pltpu.VMEM((depth, width), jnp.float32)], 0, 0
    if second is not None:
        (second_left, second_right, core) = second
        args += [*second_left, *second_right, core]
        second_shape = (second_left[0].shape[1], second_right[0].shape[1])
        beside = second_shape[0] // (2 * depth)
        extra = beside * second_shape[1]
        scratch.append(pltpu.VMEM(second_shape, jnp.float32))
    shape = (size // 2, rows, width + extra)
    kept, sent = kernel_call(
        lambda *refs: weight_grad_kernel(beside, *refs),
        [(shape, jnp.float32, PUT_FAR), (shape, jnp.bfloat16, PUT_FAR)],
        args,
        scratch=scratch,
        flops=4 * left[0].shape[0] * depth * width,
        after=after,
    )
    return Scattering(kept, sent, size)


def swap_columns(*totals):
    me = lax.axis_index("shard")

    def half_of(core):
        halves = [total.shape[0] // 2 for total in totals]
        return jnp.concatenate(
            [
                lax.dynamic_slice_in_dim(total, core * half, half, 0)
                for total, half in zip(totals, halves)
            ]
        )

    mine, other = half_of(me), swap_cores(half_of(1 - me))
    first, second = jnp.where(me == 0, mine, other), jnp.where(me == 0, other, mine)
    both, found, start = jnp.concatenate([first, second], 1), [], 0
    for total in totals:
        found.append(both[start : start + total.shape[0] // 2])
        start += total.shape[0] // 2
    return found


def tiles(rows, width, high, wide):
    for r in range(0, rows, high):
        for k in range(0, width, wide):
            yield slice(r, r + high), slice(k, k + wide)


def norm_factors(terms, norm_ref, row, count):
    totals = jnp.sum(terms[...], 0)
    average = totals[0:1] / count
    inverse = lax.rsqrt(totals[1:2] / count - average * average + EPS_NORM)
    return average, inverse, norm_ref[row : row + 1, :], norm_ref[row + 1 : row + 2, :]


def normalize(values, factors, columns):
    average, inverse, gain, shift = (part[:, columns] for part in factors)
    unit = (values - average) * inverse
    return unit, gain * unit + shift


def silu(values):
    return values * jax.nn.sigmoid(values)


def norm_backward(grad, unit, factors, totals, count, columns):
    _, inverse, gain, _ = (part[:, columns] for part in factors)
    mean_grad = totals[0:1, columns] / count
    mean_product = totals[1:2, columns] / count
    return gain * inverse * (grad - mean_grad - unit * mean_product)


class Sums:
    def __init__(self, out_ref):
        self.out_ref = out_ref
        self.parts = {}

    def add(self, columns, first, second):
        key = (columns.start, columns.stop)
        fold = lambda v: jnp.sum(v.reshape(v.shape[0] // 8, 8, v.shape[1]), 0)
        first, second = fold(first), fold(second)
        if key in self.parts:
            first, second = self.parts[key][0] + first, self.parts[key][1] + second
        self.parts[key] = (first, second)

    def store(self):
        for (start, stop), (first, second) in self.parts.items():
            first = jnp.sum(first, 0, keepdims=True)
            second = jnp.sum(second, 0, keepdims=True)
            both = jnp.concatenate([first, second], 0).astype(self.out_ref.dtype)
            for copy in range(self.out_ref.shape[0]):
                self.out_ref[copy, :, start:stop] = both


def reduce_kernel(weights, x_ref, *refs):
    inputs, refs = refs[:weights], refs[weights:]
    pre_ref, sums_ref, weight_out, weight, sems, out_sem = refs
    fetch_weight(inputs, weight, sems)(0)
    copy_out = pltpu.make_async_copy(weight, weight_out, out_sem)
    copy_out.start()
    sums = Sums(sums_ref)
    for columns in (slice(k, k + 256) for k in range(0, MID, 256)):
        pre = product(x_ref[...], weight[:, columns])
        pre_ref[:, columns] = pre
        sums.add(columns, pre, pre * pre)
    sums.store()
    copy_out.wait()


def spatial_kernel(weights, count, pre_ref, norm_ref, valid_ref, *refs):
    term_refs, *refs = refs
    inputs, refs = refs[:weights], refs[weights:]
    out_ref, sums_ref, patches_out, weight_out, padded, patches, sem, weight, sems, out_sem = refs
    wait = fetch_weight(inputs, weight, sems)
    rows = pre_ref.shape[0]
    factors = norm_factors(term_refs, norm_ref, 0, count)
    edge = jnp.zeros((EDGE, MID), jnp.float32)
    padded[0:EDGE, :] = edge
    padded[EDGE + rows :, :] = edge
    for high, columns in tiles(rows, MID, 48, 512):
        _, shifted = normalize(pre_ref[high, columns], factors, columns)
        low = silu(shifted).astype(jnp.bfloat16)
        padded[EDGE + high.start : EDGE + high.stop, columns] = low.astype(jnp.float32)
    for place in range(9):
        offset = EDGE + neighbour(place, rows // (2 * SIDE * SIDE))
        for high, columns in tiles(rows, MID, 48, 512):
            values = padded[offset + high.start : offset + high.stop, columns]
            values = values * valid_ref[high, place : place + 1]
            patches[high, place * MID : (place + 1) * MID] = values.astype(jnp.bfloat16)
    copy = pltpu.make_async_copy(patches, patches_out, sem)
    copy.start()
    wait(0)
    copy_out = pltpu.make_async_copy(weight, weight_out, out_sem)
    copy_out.start()
    sums = Sums(sums_ref)
    for columns in (slice(k, k + 256) for k in range(0, MID, 256)):
        pre = product(patches[...], weight[:, columns])
        out_ref[:, columns] = pre
        sums.add(columns, pre, pre * pre)
    sums.store()
    copy.wait()
    copy_out.wait()


def expand_kernel(weights, count, pre_ref, norm_ref, *refs):
    term_refs, *refs = refs
    inputs, refs = refs[:weights], refs[weights:]
    act_ref, out_ref, sums_ref, weight_out, side_ref, weight, sems, out_sem = refs
    wait = fetch_weight(inputs, weight, sems)
    factors = norm_factors(term_refs, norm_ref, 2, count)
    for high, columns in tiles(pre_ref.shape[0], MID, 48, 512):
        _, shifted = normalize(pre_ref[high, columns], factors, columns)
        act_ref[high, columns] = silu(shifted).astype(jnp.bfloat16)
    wait(0)
    copy_out = pltpu.make_async_copy(weight, weight_out, out_sem)
    copy_out.start()
    if weight.shape[1] > D:
        side_ref[...] = weight[:, D:]
    else:
        side_ref[...] = jnp.zeros_like(side_ref)
    sums = Sums(sums_ref)
    for columns in (slice(k, k + 256) for k in range(0, D, 256)):
        pre = product(act_ref[...], weight[:, columns])
        out_ref[:, columns] = pre
        sums.add(columns, pre, pre * pre)
    sums.store()
    copy_out.wait()


def split(values):
    high = values.astype(jnp.bfloat16)
    return high, (values - high.astype(jnp.float32)).astype(jnp.bfloat16)


def pool_kernel(weights, count, pre_ref, x_ref, norm_ref, pool_ref, size_ref, *refs):
    term_refs, *refs = refs
    inputs, refs = refs[:weights], refs[weights:]
    pooled_ref, out_ref, sums_ref, project_ref, high_ref, rest_ref, weight, sems = refs
    wait = fetch_weight(inputs, weight, sems, CHUNKS)
    factors = norm_factors(term_refs, norm_ref, 0, count)
    rows = pre_ref.shape[0]
    for k in range(0, D, 256):
        for high, columns in tiles(rows, 256, 96, 256):
            across = slice(k + columns.start, k + columns.stop)
            _, shifted = normalize(pre_ref[high, across], factors, across)
            block = silu(shifted + x_ref[high, across].astype(jnp.float32))
            high_ref[high, columns], rest_ref[high, columns] = split(block)
        pooled = product(pool_ref[...], high_ref[...]) + product(pool_ref[...], rest_ref[...])
        pooled_ref[:, k : k + 256] = (pooled / size_ref[...]).astype(jnp.bfloat16)
    step = D // CHUNKS
    total = 0.0
    for chunk in range(CHUNKS):
        wait(chunk)
        part = slice(chunk * step, (chunk + 1) * step)
        total = total + product(pooled_ref[:, part], weight[part, :D])
    out_ref[...] = total
    project_ref[...] = weight[:, D:]
    sums = Sums(sums_ref)
    for columns in (slice(k, k + 512) for k in range(0, D, 512)):
        pre = out_ref[:, columns]
        sums.add(columns, pre, pre * pre)
    sums.store()


def embed_kernel(count, pre_ref, norm_ref, project_ref, bias_ref, pooled_ref, *refs):
    term_refs, *refs = refs
    act_ref, unit_ref, inverse_ref, low_ref = refs
    factors = norm_factors(term_refs, norm_ref, 2, count)
    for high, columns in tiles(pre_ref.shape[0], D, pre_ref.shape[0], 512):
        _, shifted = normalize(pre_ref[high, columns], factors, columns)
        act_ref[high, columns] = silu(shifted).astype(jnp.bfloat16)
    embed = product(act_ref[...], project_ref[...]) + bias_ref[...]
    inverse = lax.rsqrt(jnp.sum(embed * embed, 1, keepdims=True) + EPS_UNIT)
    unit = embed * inverse
    unit_ref[...] = unit
    inverse_ref[...] = jnp.broadcast_to(inverse, inverse_ref.shape)
    low = unit.astype(jnp.bfloat16)
    copies, rows, _ = low_ref.shape
    crops = low.shape[0]
    for copy in range(copies):
        low_ref[copy, :crops, :] = low
        if rows > crops:
            width = D // copies
            low_ref[copy, crops:, :] = pooled_ref[:, copy * width : (copy + 1) * width]


def embed_back_kernel(
    count, grad_ref, unit_ref, inverse_ref, project_ref, pre_ref, norm_ref, *refs
):
    term_refs, *refs = refs
    low_ref, out_ref, sums_ref, bias_ref = refs
    grad, unit = grad_ref[...], unit_ref[...]
    embed_grad = inverse_ref[...] * (grad - unit * jnp.sum(grad * unit, 1, keepdims=True))
    low_ref[...] = embed_grad.astype(jnp.bfloat16)
    bias_ref[...] = jnp.sum(embed_grad, 0, keepdims=True)
    factors = norm_factors(term_refs, norm_ref, 2, count)
    sums = Sums(sums_ref)
    for columns in (slice(k, k + 512) for k in range(0, D, 512)):
        back = product_bt(low_ref[...], project_ref[columns, :])
        head_unit, shifted = normalize(pre_ref[:, columns], factors, columns)
        back = back * silu_slope(shifted)
        out_ref[:, columns] = back
        sums.add(columns, back, back * head_unit)
    sums.store()


def pool_back_kernel(
    weights,
    crop_count,
    count,
    grad_ref,
    head_pre_ref,
    pre_ref,
    x_ref,
    norm_ref,
    spread_ref,
    size_ref,
    *refs,
):
    head_terms, head_back, pre_terms, *refs = refs
    inputs, refs = refs[:weights], refs[weights:]
    low_ref, own_ref, other_ref, sums_ref, total_ref, weight, sems = refs
    wait = fetch_weight(inputs, weight, sems, CHUNKS)
    step = D // CHUNKS
    head_factors = norm_factors(head_terms, norm_ref, 2, crop_count)
    totals = jnp.sum(head_back[...].astype(jnp.float32), 0)
    total_ref[...] = totals
    for columns in (slice(k, k + 512) for k in range(0, D, 512)):
        unit, _ = normalize(head_pre_ref[:, columns], head_factors, columns)
        grad = norm_backward(
            grad_ref[:, columns], unit, head_factors, totals, crop_count, columns
        )
        low_ref[:, columns] = grad.astype(jnp.bfloat16)
    factors = norm_factors(pre_terms, norm_ref, 0, count)
    sums = Sums(sums_ref)
    own_rows = own_ref.shape[0]
    for chunk in range(CHUNKS):
        wait(chunk)
        part = slice(chunk * step, (chunk + 1) * step)
        pooled = product_bt(low_ref[...], weight[part, :D]) / size_ref[...]
        high_part, rest_part = split(pooled)
        for rows, columns in tiles(2 * own_rows, part.stop - part.start, 48, 256):
            across = slice(part.start + columns.start, part.start + columns.stop)
            spread = spread_ref[rows, :]
            out_grad = product(spread, high_part[:, columns]) + product(
                spread, rest_part[:, columns]
            )
            unit, shifted = normalize(pre_ref[rows, across], factors, across)
            joined = shifted + x_ref[rows, across].astype(jnp.float32)
            joined_grad = out_grad * silu_slope(joined)
            if rows.start < own_rows:
                own_ref[rows, across] = joined_grad
            else:
                other_ref[rows.start - own_rows : rows.stop - own_rows, across] = joined_grad
            sums.add(across, joined_grad, joined_grad * unit)
    sums.store()


def column_halves(low_ref, core, kept_ref, sent_ref):
    half = kept_ref.shape[1]
    for out_ref, which in ((kept_ref, core[0]), (sent_ref, 1 - core[0])):
        out_ref[...] = low_ref[:, pl.ds(pl.multiple_of(which * half, half), half)]


def expand_back_kernel(
    count, core, own_ref, other_ref, pre_ref, wide_ref, weight_ref, before_ref, mid_ref, bias_ref, *refs
):
    pre_terms, back_terms, before_terms, *refs = refs
    kept_ref, sent_ref, out_ref, sums_ref, total_ref, low_ref = refs
    factors = norm_factors(pre_terms, wide_ref, 0, count)
    totals = jnp.sum(back_terms[...].astype(jnp.float32), 0)
    total_ref[...] = totals
    own_rows = own_ref.shape[0]
    for rows, columns in tiles(2 * own_rows, D, 48, 512):
        unit, _ = normalize(pre_ref[rows, columns], factors, columns)
        if rows.start < own_rows:
            grad = own_ref[rows, columns]
        else:
            grad = other_ref[rows.start - own_rows : rows.stop - own_rows, columns]
        grad = norm_backward(grad, unit, factors, totals, count, columns)
        low_ref[rows, columns] = grad.astype(jnp.bfloat16)
    column_halves(low_ref, core, kept_ref, sent_ref)
    factors = norm_factors(before_terms, mid_ref, 2, count)
    sums = Sums(sums_ref)
    for columns in (slice(k, k + 256) for k in range(0, MID, 256)):
        back = product_bt(low_ref[...], weight_ref[columns, :D])
        unit, shifted = normalize(before_ref[:, columns], factors, columns)
        back = back * silu_slope(shifted)
        out_ref[:, columns] = back
        sums.add(columns, back, back * unit)
    sums.store()
    bias = jnp.concatenate([bias_ref[...], jnp.zeros_like(bias_ref)], 0)
    for copy in range(sums_ref.shape[0]):
        sums_ref[copy, :, MID:] = bias.astype(sums_ref.dtype)


def spatial_back_kernel(
    count, core, grad_ref, pre_ref, norm_ref, weight_ref, before_ref, valid_ref, *refs
):
    pre_terms, back_terms, before_terms, *refs = refs
    kept_ref, sent_ref, out_ref, sums_ref, total_ref, slots, low_ref = refs
    rows = grad_ref.shape[0]
    factors = norm_factors(pre_terms, norm_ref, 2, count)
    totals = jnp.sum(back_terms[...].astype(jnp.float32), 0)
    total_ref[...] = totals
    for high, columns in tiles(rows, MID, 48, 512):
        unit, _ = normalize(pre_ref[high, columns], factors, columns)
        grad = norm_backward(grad_ref[high, columns], unit, factors, totals, count, columns)
        low_ref[high, columns] = grad.astype(jnp.bfloat16)
    column_halves(low_ref, core, kept_ref, sent_ref)
    edge = jnp.zeros((EDGE, MID), jnp.float32)
    for place in range(9):
        slots[place, 0:EDGE, :] = edge
        slots[place, EDGE + rows :, :] = edge
        for columns in (slice(k, k + 256) for k in range(0, MID, 256)):
            patch = product_bt(
                low_ref[...],
                weight_ref[place * MID + columns.start : place * MID + columns.stop, :],
            )
            slots[place, EDGE : EDGE + rows, columns] = patch * valid_ref[:, place : place + 1]
    factors = norm_factors(before_terms, norm_ref, 0, count)
    sums = Sums(sums_ref)
    for high, columns in tiles(rows, MID, 48, 256):
        back = 0.0
        for place in range(9):
            start = EDGE - neighbour(place, rows // (2 * SIDE * SIDE)) + high.start
            back = back + slots[place, start : start + high.stop - high.start, columns]
        unit, shifted = normalize(before_ref[high, columns], factors, columns)
        back = back * silu_slope(shifted)
        out_ref[high, columns] = back
        sums.add(columns, back, back * unit)
    sums.store()


def reduce_back_kernel(
    count,
    core,
    grad_ref,
    pre_ref,
    norm_ref,
    pre_terms,
    back_terms,
    low_ref,
    other_ref,
    kept_ref,
    sent_ref,
    total_ref,
):
    rows = grad_ref.shape[0]
    factors = norm_factors(pre_terms, norm_ref, 0, count)
    totals = jnp.sum(back_terms[...].astype(jnp.float32), 0)
    total_ref[...] = totals
    for high, columns in tiles(rows, MID, 48, 512):
        unit, _ = normalize(pre_ref[high, columns], factors, columns)
        grad = norm_backward(grad_ref[high, columns], unit, factors, totals, count, columns)
        low_ref[high, columns] = grad.astype(jnp.bfloat16)
    other_ref[...] = low_ref[rows // 2 :, :]
    column_halves(low_ref, core, kept_ref, sent_ref)


def arrange_kernel(core, canvases_ref, own_ref, other_ref, rows_ref):
    _, _, _, canvas_count, _ = canvases_ref.shape
    for which, out_ref in enumerate((own_ref, other_ref)):
        micro = core[0] if which == 0 else 1 - core[0]
        for pixel in range(SIDE * SIDE):
            rows = slice(pixel * canvas_count, (pixel + 1) * canvas_count)
            values = canvases_ref[micro, pixel // SIDE, pixel % SIDE]
            rows_ref[rows, :] = values.astype(jnp.float32)
        out_ref[...] = rows_ref[...].astype(jnp.bfloat16)


def input_grad_kernel(
    core, own_ref, other_ref, low_ref, other_low_ref, weight_ref, out_ref, rows_ref
):
    own_rows = own_ref.shape[0]
    canvas_count = out_ref.shape[3]
    for which in range(2):
        micro = core[0] if which == 0 else 1 - core[0]
        grad_ref = own_ref if which == 0 else other_ref
        low = low_ref[:own_rows, :] if which == 0 else other_low_ref[...]
        for columns in (slice(k, k + 512) for k in range(0, D, 512)):
            rows_ref[:, columns] = grad_ref[:, columns] + product_bt(low, weight_ref[columns, :])
        for pixel in range(SIDE * SIDE):
            rows = slice(pixel * canvas_count, (pixel + 1) * canvas_count)
            out_ref[micro, pixel // SIDE, pixel % SIDE] = rows_ref[rows, :]


def proto_grad_kernel(first_ref, second_ref, out_ref):
    rows = out_ref.shape[0]
    for k in range(0, rows, 128):
        stop = min(k + 128, rows)
        total = first_ref[:, k : k + 128] + second_ref[:, k : k + 128]
        out_ref[k:stop, :] = total.T[: stop - k, :]


def inside_canvas(own_canvases):
    valid = np.zeros((2, SIDE, SIDE, own_canvases, 16), np.float32)
    for place in range(9):
        down, right = place // 3 - 1, place % 3 - 1
        for y in range(SIDE):
            for x in range(SIDE):
                valid[:, y, x, :, place] = 0 <= y + down < SIDE and 0 <= x + right < SIDE
    return jnp.asarray(valid.reshape(-1, 16))


def neighbour(place, own_canvases):
    return ((place // 3 - 1) * SIDE + place % 3 - 1) * own_canvases


EDGE = 32


def add_columns(total_ref, columns, values):
    rows, width = values.shape
    total_ref[:, columns] += jnp.sum(values.reshape(rows // 8, 8, width), 0)


def codes_kernel(
    crops,
    device_crops,
    place,
    sent_ref,
    side_ref,
    prototypes_ref,
    loss_ref,
    proto_grad_ref,
    unit_grad_ref,
    units_ref,
    proto_ref,
    partner_ref,
    codes_ref,
    heat_ref,
    score_ref,
    total_ref,
    scale_ref,
    inverse_ref,
    *,
    factor,
):
    rows_all, width = codes_ref.shape
    own = unit_grad_ref.shape[0]
    chunks = [slice(k, k + LANES) for k in range(0, width, LANES)]
    real = lax.broadcasted_iota(jnp.int32, (1, width), 1) < PROTOS

    dim = units_ref.shape[1]
    for i in range(sent_ref.shape[0]):
        units_ref[i * own : (i + 1) * own, :] = sent_ref[i, :own, :]
    proto_ref[PROTOS // 16 * 16 :, :] = jnp.zeros((width - PROTOS // 16 * 16, dim), jnp.bfloat16)
    proto_ref[:PROTOS, :] = prototypes_ref[...]

    queue_rows = side_ref.shape[0]
    device_rows = queue_rows // (crops // device_crops)
    crop = lax.broadcasted_iota(jnp.int32, (crops, queue_rows), 0)
    holder = crop // device_crops ^ place[1]
    row = lax.broadcasted_iota(jnp.int32, (crops, queue_rows), 1)
    holds = (row == holder * device_rows).astype(jnp.bfloat16)
    found = product(holds, side_ref[:, dim:])
    crop = lax.broadcasted_iota(jnp.int32, found.shape, 0)
    lane = lax.broadcasted_iota(jnp.int32, found.shape, 1)
    here = lane == place[1] * device_crops + crop % device_crops
    partner = jnp.sum(jnp.where(here, found, 0.0), 1, keepdims=True)
    partner_ref[...] = partner.astype(jnp.int32)

    def scores(rows, columns, queue=False):
        left = side_ref[rows, :dim] if queue else units_ref[rows, :]
        return product_bt(left, proto_ref[columns, :])

    def keep(values, columns):
        if columns.stop <= PROTOS:
            return values
        lanes = columns.start + lax.broadcasted_iota(jnp.int32, values.shape, 1)
        return jnp.where(lanes < PROTOS, values, 0.0)

    def fold(values):
        return sum(values[:, k : k + 128] for k in range(0, values.shape[1], 128))

    total_ref[...] = jnp.zeros_like(total_ref)

    for queue, start, count in ((False, 0, crops), (True, crops, queue_rows)):

        def first(i, carry):
            rows = pl.ds(pl.multiple_of(i * 128, 128), 128)
            target = pl.ds(pl.multiple_of(start + i * 128, 128), 128)
            for columns in chunks:
                score = scores(rows, columns, queue)
                powers = keep(jnp.exp(score * (1.0 / SINK_EPS)), columns)
                codes_ref[target, columns] = powers
                add_columns(total_ref, columns, powers)
            return carry

        lax.fori_loop(0, count // 128, first, 0)

    def column_factors(turn):
        total = jnp.sum(total_ref[...], 0, keepdims=True)
        total = jnp.where(real, total, 1.0)
        if turn == 0:
            scale = jnp.where(total > 1e30, 2.0**-64, 1.0)
            scale_ref[...] = jnp.broadcast_to(scale, scale_ref.shape)
            total = total * scale
        inverse_ref[...] = jnp.broadcast_to(1.0 / total, inverse_ref.shape)

    def divided(turn, rows, columns):
        values = codes_ref[rows, columns]
        if turn == 0:
            values = values * scale_ref[0:1, columns]
        return values * inverse_ref[0:1, columns]

    def row_inverse(turn, rows):
        part = sum(fold(divided(turn, rows, columns)) for columns in chunks)
        return 1.0 / jnp.sum(part, 1, keepdims=True)

    for turn in range(SINK_ITERS - 1):
        column_factors(turn)
        total_ref[...] = jnp.zeros_like(total_ref)

        def both(i, carry):
            rows = pl.ds(pl.multiple_of(i * 64, 64), 64)
            inverse = row_inverse(turn, rows)
            for columns in chunks:
                values = divided(turn, rows, columns) * inverse
                codes_ref[rows, columns] = values
                add_columns(total_ref, columns, values)
            return carry

        lax.fori_loop(0, rows_all // 64, both, 0)

    column_factors(SINK_ITERS - 1)
    loss_ref[...] = jnp.zeros_like(loss_ref)
    block = 128

    def last(i, carry):
        rows = pl.ds(pl.multiple_of(i * block, block), block)
        inverse = row_inverse(SINK_ITERS - 1, rows)
        row = lax.broadcasted_iota(jnp.int32, (block, block), 0)
        column = lax.broadcasted_iota(jnp.int32, (block, block), 1)
        pick = (column == (row // CROPS) * CROPS + partner_ref[rows, :]).astype(jnp.bfloat16)
        pick = jnp.concatenate([pick, pick], 1)
        heat_part = jnp.zeros((block, 128), jnp.float32)
        target_part = jnp.zeros((block, 128), jnp.float32)
        loss_part = jnp.zeros((block, 128), jnp.float32)
        for columns in chunks:
            score = scores(rows, columns)
            heat = keep(jnp.exp(score * (1.0 / SOFTMAX_HEAT)), columns)
            heat_ref[:, columns] = heat
            heat_part += fold(heat)
            codes = divided(SINK_ITERS - 1, rows, columns) * inverse
            high = codes.astype(jnp.bfloat16)
            rest = (codes - high.astype(jnp.float32)).astype(jnp.bfloat16)
            target = product(pick, jnp.concatenate([high, rest], 0))
            codes_ref[rows, columns] = target
            target_part += fold(target)
            loss_part += fold(target * score)
        heat_sum = jnp.sum(heat_part, 1, keepdims=True)
        target_sum = jnp.sum(target_part, 1, keepdims=True)
        row_loss = (
            target_sum * jnp.log(heat_sum)
            - jnp.sum(loss_part, 1, keepdims=True) * (1.0 / SOFTMAX_HEAT)
        )
        loss_ref[...] += jnp.broadcast_to(jnp.sum(row_loss, 0, keepdims=True), loss_ref.shape)
        ratio = target_sum / heat_sum * factor
        for columns in chunks:
            grad = heat_ref[:, columns] * ratio - codes_ref[rows, columns] * factor
            score_ref[rows, columns] = grad.astype(jnp.bfloat16)
        return carry

    lax.fori_loop(0, crops // block, last, 0)
    for columns in chunks:
        proto_grad_ref[:, columns] = product_t(units_ref[...], score_ref[:, columns])
    mine = pl.ds(pl.multiple_of(place[0], own), own)
    unit_grad_ref[...] = product(score_ref[mine, :], proto_ref[...])


def gathered_loss(units, side, prototypes, place, own, device_crops, loss_factor_weight):
    crops, dim = units.shape[0] * own, units.shape[2]
    width = -(-PROTOS // LANES) * LANES
    rows_all = crops + side.shape[0]
    f32, bf16 = jnp.float32, jnp.bfloat16
    loss, proto_grad, unit_grad = kernel_call(
        lambda *refs: codes_kernel(
            crops, device_crops, *refs, factor=loss_factor_weight / SOFTMAX_HEAT
        ),
        [((8, 128), f32), ((dim, width), f32, PUT_FAR), ((own, dim), f32)],
        [Scalars(place), units, Loaded(side), Loaded(prototypes)],
        scratch=[
            pltpu.VMEM((crops, dim), bf16),
            pltpu.VMEM((width, dim), bf16),
            pltpu.VMEM((crops, 1), jnp.int32),
            pltpu.VMEM((rows_all, width), f32),
            pltpu.VMEM((128, width), f32),
            pltpu.VMEM((crops, width), bf16),
            pltpu.VMEM((8, width), f32),
            pltpu.VMEM((8, width), f32),
            pltpu.VMEM((8, width), f32),
        ],
        flops=2 * width * (rows_all * dim + 6 * crops * dim),
        transcendentals=width * (rows_all + crops),
        limit=24,
    )
    return loss[0, 0], proto_grad, unit_grad


def sinkhorn(batch_codes, stored_codes, total):
    for turn in range(SINK_ITERS):
        column_totals = total(jnp.sum(batch_codes, 0) + jnp.sum(stored_codes, 0))
        batch_codes = batch_codes / column_totals
        stored_codes = stored_codes / column_totals
        batch_codes = batch_codes / jnp.sum(batch_codes, 1, keepdims=True)
        stored_codes = stored_codes / jnp.sum(stored_codes, 1, keepdims=True)
    return batch_codes


def swapped_loss(scores, codes, pick, loss_factor_weight):
    rows = scores.shape[0]
    target = jnp.einsum(
        "cab,cbk->cak", pick, codes.reshape(rows // CROPS, CROPS, PROTOS), precision=HIGH
    ).reshape(rows, PROTOS)
    log_likelihoods = jax.nn.log_softmax(scores / SOFTMAX_HEAT, axis=1)
    score_grad = (jnp.exp(log_likelihoods) * jnp.sum(target, 1, keepdims=True) - target) * (
        loss_factor_weight / SOFTMAX_HEAT
    )
    return -jnp.sum(target * log_likelihoods), score_grad.astype(jnp.bfloat16)


def per_device(
    canvases,
    crop_map,
    partner,
    queue,
    w_reduce,
    w_spatial,
    w_expand,
    w_hidden,
    w_project,
    norm_mid,
    norm_wide,
    bias_out,
    prototypes,
):
    f32, bf16 = jnp.float32, jnp.bfloat16
    size = lax.axis_size("dp")
    me_dp, me_core = lax.axis_index("dp"), lax.axis_index("shard")
    core = Scalars(me_core.astype(jnp.int32).reshape(1))
    own_canvases = canvases.shape[1]
    canvas_count = 2 * own_canvases
    pixels = SIDE * SIDE
    own_rows = own_canvases * pixels
    local_rows = canvas_count * pixels
    local_crops = canvas_count * CROPS
    pixel_total = float(local_rows * size)
    crop_count = local_crops * size
    crop_total = float(crop_count)
    loss_factor_weight = 1.0 / (MICRO * crop_total)
    crop_ids = jnp.arange(CROPS, dtype=jnp.int32)
    valid = inside_canvas(own_canvases)
    proj = bias_out.shape[0]
    partner_size = partner.size
    copies = copies_of(size)
    by_steps = size == STEPS_DP
    if by_steps:
        slots = relative_slots(size)
        chip_slots = lax.dynamic_slice_in_dim(slots.reshape(size, 2), me_core, 1, 1)[:, 0]

    def both_cores(values):
        mine = lax.dynamic_index_in_dim(values, me_core, 0, keepdims=False)
        other = lax.dynamic_index_in_dim(values, 1 - me_core, 0, keepdims=False)
        return jnp.concatenate([mine, swap_cores(other)], 0)

    def gather_whole(shard):
        return Gathered(lax.all_gather(shard, BOTH, axis=0, tiled=True))

    head_shard = jnp.concatenate([w_hidden, w_project], 1)
    beside = queue.shape[1]
    gathered_codes = (
        crop_count * PROTOS * 4 <= GATHERED_CODES_BYTES
        and queue.shape[0] == w_expand.shape[0]
        and partner_size <= beside
    )
    if gathered_codes:
        partners = jnp.pad(
            partner.astype(bf16).reshape(1, -1),
            ((0, 0), (0, beside - partner_size)),
        )
        partners = jnp.broadcast_to(partners, (queue.shape[0], beside))
        w_expand = jnp.concatenate([w_expand, queue, partners], 1)

    labels = both_cores(jnp.concatenate([crop_map, partner], 2))
    crop_map, partner = labels[:, :pixels], labels[:, pixels:]
    crop_of = jnp.arange(local_crops, dtype=jnp.int32)
    pixel_crop = crop_map + CROPS * jnp.arange(canvas_count, dtype=jnp.int32)[:, None]
    pixel_crop = pixel_crop.reshape(2, own_canvases, pixels).swapaxes(1, 2).reshape(local_rows)
    pool = (crop_of[:, None] == pixel_crop[None, :]).astype(bf16)
    spread = (pixel_crop[:, None] == crop_of[None, :]).astype(bf16)
    crop_sizes = jnp.sum(pool.astype(f32), 1, keepdims=True)

    half_rows = ((own_rows, D), bf16)
    own_x, other_x = kernel_call(
        arrange_kernel,
        [half_rows, half_rows],
        [core, canvases.transpose(0, 2, 3, 1, 4)],
        scratch=[pltpu.VMEM((own_rows, D), f32)],
    )
    input_rows = join([(own_x[None], swap_cores(other_x)[None])])[0].reshape(local_rows, D)

    if by_steps:
        reduce_part = Gathering(w_reduce, size)
        gather_step([reduce_part])
        spatial_part = Gathering(hold(w_spatial, [reduce_part.held]), size)
        gather_step([reduce_part], [pool, spread, crop_sizes, input_rows])
        head_held = lax.all_gather(hold(head_shard, [reduce_part.held]), "dp", axis=0)
        gather_step([reduce_part, spatial_part])
        expand_part = Gathering(hold(w_expand, [spatial_part.held]), size)
        reduce_all = reduce_part.finish(slots)
    else:
        reduce_all = gather_whole(w_reduce)

    mid_rows, wide_rows = ((local_rows, MID), f32), ((local_rows, D), f32)
    mid_sums, wide_sums = ((copies, 2, MID), f32), ((copies, 2, D), f32, PUT_FAR)

    back_type = bf16 if copies > 1 else f32
    back_sums = ((copies, 2, D), back_type, PUT_FAR)

    def weight_out(weight):
        return (weight.shape, bf16, FAR)

    pre_one, sums, full_reduce = kernel_call(
        lambda *refs: reduce_kernel(reduce_all.count, *refs),
        [mid_rows, mid_sums, weight_out(reduce_all)],
        [input_rows] + reduce_all.inputs(),
        scratch=reduce_all.scratch() + [pltpu.SemaphoreType.DMA],
        flops=2 * local_rows * D * MID,
    )
    terms_one = terms_over_dp(sums)
    if by_steps:
        gather_step([spatial_part, expand_part], [sums])
        gather_step([spatial_part], [terms_one])
        spatial_all = spatial_part.finish(slots)
    else:
        spatial_all, expand_all = gather_whole(w_spatial), gather_whole(w_expand)

    pre_two, sums, image_patches, full_spatial = kernel_call(
        lambda *refs: spatial_kernel(spatial_all.count, pixel_total, *refs),
        [
            mid_rows,
            mid_sums,
            ((local_rows, 9 * MID), bf16, FAR),
            weight_out(spatial_all),
        ],
        [pre_one, norm_mid, valid, terms_one] + spatial_all.inputs(),
        scratch=[
            pltpu.VMEM((local_rows + 2 * EDGE, MID), f32),
            pltpu.VMEM((local_rows, 9 * MID), bf16),
            pltpu.SemaphoreType.DMA,
        ]
        + spatial_all.scratch()
        + [pltpu.SemaphoreType.DMA],
        flops=2 * local_rows * 9 * MID * MID,
    )
    terms_two = terms_over_dp(sums)
    if by_steps:
        gather_step([expand_part], [sums])
        gather_step([expand_part], [terms_two])
        expand_all = expand_part.finish(slots)

    side = ((expand_all.shape[0], max(expand_all.shape[1] - D, 128)), bf16, PUT_FAR)
    act_two, pre_three, sums, full_expand, side = kernel_call(
        lambda *refs: expand_kernel(expand_all.count, pixel_total, *refs),
        [
            ((local_rows, MID), bf16, PUT_FAR),
            wide_rows,
            wide_sums,
            weight_out(expand_all),
            side,
        ],
        [pre_two, norm_mid, terms_two] + expand_all.inputs(),
        scratch=expand_all.scratch() + [pltpu.SemaphoreType.DMA],
        flops=2 * local_rows * D * MID,
    )
    terms_three = terms_over_dp(sums)
    if by_steps:
        head_held, _ = lax.optimization_barrier((head_held, sums))
        head = other_core_dp(head_held, size)
    else:
        head = gather_whole(head_shard)

    crop_rows = ((local_crops, D), f32, PUT_FAR)
    pooled_low, pre_head, sums, full_project = kernel_call(
        lambda *refs: pool_kernel(head.count, pixel_total, *refs),
        [
            ((local_crops, D), bf16, PUT_FAR),
            crop_rows,
            wide_sums,
            ((D, proj), bf16, PUT_FAR),
        ],
        [
            pre_three,
            input_rows,
            Loaded(norm_wide),
            Loaded(pool),
            Loaded(crop_sizes),
            terms_three,
        ]
        + head.inputs(),
        scratch=[pltpu.VMEM((local_rows, 256), bf16), pltpu.VMEM((local_rows, 256), bf16)]
        + head.scratch(CHUNKS),
        flops=2 * local_crops * D * D,
        transcendentals=local_rows * D,
    )
    terms_head = terms_over_dp(sums)

    embed_rows = ((local_crops, proj), f32)
    send_pooled = gathered_codes and copies * proj == D
    act_head, unit_embed, inv_length, unit_low = kernel_call(
        lambda *refs: embed_kernel(crop_total, *refs),
        [
            ((local_crops, D), bf16),
            embed_rows,
            embed_rows,
            ((copies, local_crops * (2 if send_pooled else 1), proj), bf16, PUT_FAR),
        ],
        [
            Loaded(pre_head),
            Loaded(norm_wide),
            Streamed(full_project),
            Loaded(bias_out.reshape(1, proj)),
            Streamed(pooled_low),
            terms_head,
        ],
        flops=2 * local_crops * D * proj,
    )

    if gathered_codes:
        all_units = lax.all_to_all(unit_low, "dp", 0, 0)
        loss_part, proto_part, unit_grad = gathered_loss(
            all_units,
            side,
            prototypes,
            jnp.stack([me_dp * local_crops, me_core]).astype(jnp.int32),
            local_crops,
            own_canvases * CROPS,
            loss_factor_weight,
        )
    else:
        chip_queue = jnp.concatenate([queue, swap_cores(queue)], 0)
        queue_codes = jnp.exp(product_bt(chip_queue, prototypes) / SINK_EPS)
        pick = (partner[:, :, None] == crop_ids[None, None, :]).astype(f32)
        all_units = unit_low
        scores = product_bt(unit_low[0], prototypes)
        codes = sinkhorn(
            jnp.exp(scores / SINK_EPS), queue_codes, lambda sums: lax.psum(sums, "dp")
        )
        loss_part, score_low = swapped_loss(scores, codes, pick, loss_factor_weight)
        proto_part, loss_part = lax.psum((product_t(unit_low[0], score_low), loss_part), "dp")
        unit_grad = product(score_low, prototypes)

    embed_low, head_act_grad, sums, bias_part = kernel_call(
        lambda *refs: embed_back_kernel(crop_total, *refs),
        [((local_crops, proj), bf16), crop_rows, back_sums, ((1, proj), f32)],
        [
            unit_grad,
            unit_embed,
            inv_length,
            Streamed(full_project),
            Streamed(pre_head),
            Loaded(norm_wide),
            terms_head,
        ],
        flops=2 * local_crops * D * proj,
    )
    back_head = terms_over_dp(sums)

    chip_rows = 2 * w_hidden.shape[0]
    if send_pooled:
        left = all_units[:, local_crops:].reshape(crop_count, chip_rows)
    else:
        left = lax.all_gather(pooled_low, "dp", axis=0, tiled=True)
        left = lax.dynamic_slice_in_dim(left, me_dp * chip_rows, chip_rows, 1)

    own_part = ((own_rows, D), f32)
    head_low, own_grad, other_grad, sums, total_head = kernel_call(
        lambda *refs: pool_back_kernel(head.count, crop_total, pixel_total, *refs),
        [
            ((local_crops, D), bf16),
            own_part,
            own_part + (PUT_FAR,),
            back_sums,
            ((2, D), f32, PUT_FAR),
        ],
        [
            Loaded(head_act_grad),
            Loaded(pre_head),
            Streamed(pre_three),
            Streamed(input_rows),
            Loaded(norm_wide),
            Loaded(spread),
            Loaded(crop_sizes),
            terms_head,
            back_head,
            terms_three,
        ]
        + head.inputs(),
        scratch=head.scratch(CHUNKS),
        flops=2 * local_crops * D * D,
        transcendentals=local_rows * D,
    )
    back_three = terms_over_dp(sums)
    other_grad, _ = lax.optimization_barrier((other_grad, back_three))
    peer_grad = swap_cores(other_grad)

    right = lax.all_gather(head_low, "dp", axis=0, tiled=True)

    def low_halves(width):
        return [((local_rows, width // 2), bf16, PUT_FAR)] * 2

    three_kept, three_sent, two_act_grad, sums, total_three = kernel_call(
        lambda *refs: expand_back_kernel(pixel_total, *refs),
        [
            *low_halves(D),
            mid_rows,
            ((copies, 2, MID + proj), back_type, PUT_FAR),
            ((2, D), f32, PUT_FAR),
        ],
        [
            core,
            own_grad,
            Loaded(other_grad),
            Streamed(pre_three),
            Loaded(norm_wide),
            Streamed(full_expand),
            Streamed(pre_two),
            norm_mid,
            bias_part,
            terms_three,
            back_three,
            terms_two,
        ],
        scratch=[pltpu.VMEM((local_rows, D), bf16)],
        flops=2 * local_rows * D * MID,
    )
    back_two = terms_over_dp(sums)
    before_two = []
    if by_steps:
        expand_sum = weight_grad(
            (act_two, swap_cores(act_two)),
            (three_kept, swap_cores(three_sent)),
            chip_slots,
            size,
            (
                (act_head, swap_cores(act_head)),
                (embed_low, swap_cores(embed_low)),
                core,
            ),
            after=[sums],
        )
        before_two = [expand_sum.kept]

    two_kept, two_sent, one_act_grad, sums, total_two = kernel_call(
        lambda *refs: spatial_back_kernel(pixel_total, *refs),
        [
            *low_halves(MID),
            mid_rows,
            ((copies, 2, MID), back_type),
            ((2, MID + proj), f32),
        ],
        [
            core,
            two_act_grad,
            Streamed(pre_two),
            norm_mid,
            Streamed(full_spatial),
            Streamed(pre_one),
            valid,
            terms_two,
            back_two,
            terms_one,
        ],
        scratch=[
            pltpu.VMEM((9, local_rows + 2 * EDGE, MID), f32),
            pltpu.VMEM((local_rows, MID), bf16),
        ],
        flops=2 * local_rows * 9 * MID * MID,
        after=before_two,
    )
    before_one = []
    if by_steps:
        spatial_sum = weight_grad(
            (image_patches, swap_cores(image_patches)),
            (two_kept, swap_cores(two_sent)),
            chip_slots,
            size,
        )
        spatial_sum.first(two_kept)
        sums, _ = lax.optimization_barrier((sums, spatial_sum.kept))

    back_one = terms_over_dp(sums)
    one_low, other_low, one_kept, one_sent, total_one = kernel_call(
        lambda *refs: reduce_back_kernel(pixel_total, *refs),
        [
            ((local_rows, MID), bf16, PUT_FAR),
            ((own_rows, MID), bf16, PUT_FAR),
            *low_halves(MID),
            ((2, MID), f32, PUT_FAR),
        ],
        [core, one_act_grad, Streamed(pre_one), norm_mid, terms_one, back_one],
        after=before_one,
    )
    if by_steps:
        expand_sum.first(back_one)
        spatial_sum.second([one_low])
        expand_sum.second([spatial_sum.kept])
        reduce_sum = weight_grad(
            (input_rows, swap_cores(input_rows)),
            (one_kept, swap_cores(one_sent)),
            chip_slots,
            size,
            after=[expand_sum.kept, right],
        )

    proto_other = swap_cores(proto_part)
    other_low = swap_cores(other_low)
    late = []
    if by_steps:
        reduce_sum.first(one_low)
        expand_sum.third([reduce_sum.kept])
        spatial_sum.third([expand_sum.kept])
        reduce_sum.second([spatial_sum.kept])
        late = [reduce_sum.kept]
    by_pixel = kernel_call(
        input_grad_kernel,
        [((MICRO, SIDE, SIDE, own_canvases, D), f32)],
        [core, own_grad, peer_grad, one_low, other_low, full_reduce],
        scratch=[pltpu.VMEM((own_rows, D), f32)],
        flops=2 * local_rows * D * MID,
        after=late,
    )[0]
    if by_steps:
        reduce_sum.third([by_pixel])
        late = [reduce_sum.kept]
    left, right, _ = lax.optimization_barrier((left, right, late))
    if gathered_codes:
        proto_grad = kernel_call(
            proto_grad_kernel,
            [(prototypes.shape, f32)],
            [Loaded(proto_part), proto_other],
            after=late,
        )[0]
    else:
        proto_grad = (proto_part + proto_other).T
    hidden_part = product_t(left, right)

    def own_half(part):
        half = chip_rows // 2
        mine = lax.dynamic_slice_in_dim(part, me_core * half, half, 0)
        other = lax.dynamic_slice_in_dim(part, (1 - me_core) * half, half, 0)
        return mine + swap_cores(other)

    grad_hidden = own_half(hidden_part)
    if by_steps:
        grad_spatial, grad_reduce = swap_columns(spatial_sum.finish(), reduce_sum.finish())
        total = expand_sum.finish()
        (grad_expand,) = swap_columns(total[:, : D // 2])
        grad_project = jnp.concatenate(
            [total[:, k : k + proj] for k in range(D // 2, total.shape[1], proj)], 0
        )
    else:

        def scatter(first, kept, sent):
            lows = jnp.concatenate(
                [jnp.where(me_core == 0, kept, sent), jnp.where(me_core == 0, sent, kept)], 1
            )
            return lax.psum_scatter(
                product_t(first, lows), BOTH, scatter_dimension=0, tiled=True
            )

        grad_reduce = scatter(input_rows, one_kept, one_sent)
        grad_spatial = scatter(image_patches, two_kept, two_sent)
        grad_expand = scatter(act_two, three_kept, three_sent)
        grad_project = lax.psum_scatter(
            product_t(act_head, embed_low), BOTH, scatter_dimension=0, tiled=True
        )

    totals = (total_one, total_two, total_three, total_head)
    (total_one, total_two, total_three, total_head), _ = lax.optimization_barrier((totals, late))
    narrow = jnp.concatenate(
        [
            jnp.stack([total_one[1], total_one[0], total_two[1, :MID], total_two[0, :MID]])
            .reshape(-1),
            jnp.stack([total_three[1], total_three[0], total_head[1], total_head[0]]).reshape(-1),
            total_two[0, MID:],
            jnp.broadcast_to(loss_part, (128,)),
        ]
    )
    narrow = narrow + swap_cores(narrow)
    mid_end, wide_end = norm_mid.size, norm_mid.size + norm_wide.size
    bias_end = wide_end + proj
    return (
        narrow[bias_end] * loss_factor_weight,
        by_pixel.transpose(0, 3, 1, 2, 4),
        grad_reduce,
        grad_spatial,
        grad_expand,
        grad_hidden,
        grad_project,
        narrow[:mid_end].reshape(norm_mid.shape),
        narrow[mid_end:wide_end].reshape(norm_wide.shape),
        narrow[wide_end:bias_end],
        proto_grad,
    )


def solution(mesh):
    return jax.shard_map(
        per_device,
        mesh=mesh,
        in_specs=(
            P(None, ("dp", "shard"), None, None, None),
            P(None, ("dp", "shard"), None),
            P(None, ("dp", "shard"), None),
            P(("dp", "shard"), None),
            P(("dp", "shard"), None),
            P(("dp", "shard"), None),
            P(("dp", "shard"), None),
            P(("dp", "shard"), None),
            P(("dp", "shard"), None),
            P(),
            P(),
            P(),
            P(),
        ),
        out_specs=(
            P(),
            P(None, ("dp", "shard"), None, None, None),
            P(("dp", "shard"), None),
            P(("dp", "shard"), None),
            P(("dp", "shard"), None),
            P(("dp", "shard"), None),
            P(("dp", "shard"), None),
            P(),
            P(),
            P(),
            P(),
        ),
        check_vma=False,
    )
```
